32 devices in a mesh: dp: 16 (over z, y, x), mp: 2 (over core).
Axes of the slice: x: 2, y: 2, z: 4, core: 2. Of those that a mesh axis runs over, the one named last changes fastest.
Arguments:
- piece_ids: int32 [512, 8], replicated, may hold values from 0 to 31999
- piece_lengths: int32 [512], P(('dp', 'mp')), may hold values from 1 to 8
- group_ids: int32 [16, 1024], P('dp', 'mp'), may hold values from 0 to 511
- piece_table: bfloat16 [32000, 512], P(('dp', 'mp')), may hold values from -6 to 6
- ln_gains: bfloat16 [2, 512], P(None, ('dp', 'mp')), may hold values from 0.5 to 1.5
- hyp_biases: bfloat16 [3, 512], P(None, ('dp', 'mp')), may hold values from -3 to 3
- attn_weights: bfloat16 [4, 512, 512], P(None, ('dp', 'mp')), may hold values from -0.25 to 0.25
- ffn_in_weight: bfloat16 [512, 2048], P(('dp', 'mp')), may hold values from -0.25 to 0.25
- ffn_in_bias: bfloat16 [2048], P(('dp', 'mp')), may hold values from -3 to 3
- ffn_out_weight: bfloat16 [2048, 512], P(('dp', 'mp')), may hold values from -0.125 to 0.125
- proj_weight: bfloat16 [512, 2048], P(('dp', 'mp')), may hold values from -0.25 to 0.25
- proj_bias: bfloat16 [2048], P(('dp', 'mp')), may hold values from -3 to 3
- lm_gains: bfloat16 [2, 2048], replicated, may hold values from 0.5 to 1.5
- query_weight: bfloat16 [2048, 2048], P(None, 'mp'), may hold values from -0.125 to 0.125
- kv_weights: bfloat16 [2, 2048, 256], replicated, may hold values from -0.125 to 0.125
- output_weight: bfloat16 [2048, 2048], P('mp'), may hold values from -0.75 to 0.75
- gate_up_weight: bfloat16 [2, 2048, 5632], P(None, None, 'mp'), may hold values from -0.125 to 0.125
- down_weight: bfloat16 [5632, 2048], P('mp'), may hold values from -0.078125 to 0.078125
- out_grad: bfloat16 [16, 1024, 2048], P('dp', 'mp'), may hold values from -6 to 6
Outputs:
- lm_out: bfloat16 [16, 1024, 2048], P('dp', 'mp')
- row_grad: float32 [512, 2048], P(('dp', 'mp'))
- table_grad: float32 [32000, 512], P(('dp', 'mp'))
- ln_gains_grad: float32 [2, 512], P(None, ('dp', 'mp'))
- hyp_biases_grad: float32 [3, 512], P(None, ('dp', 'mp'))
- attn_weights_grad: float32 [4, 512, 512], P(None, ('dp', 'mp'))
- ffn_in_weight_grad: float32 [512, 2048], P(('dp', 'mp'))
- ffn_in_bias_grad: float32 [2048], P(('dp', 'mp'))
- ffn_out_weight_grad: float32 [2048, 512], P(('dp', 'mp'))
- proj_weight_grad: float32 [512, 2048], P(('dp', 'mp'))
- proj_bias_grad: float32 [2048], P(('dp', 'mp'))
The draws below stay inside these ranges and needn't reach their ends.
Inputs may be any that keep to these rules, and one draw needn't show every extreme that they name: `piece_ids`: slots at or past an entry's length hold arbitrary ids; those slots are masked out of the attention.
All inputs are finite; a program needn't handle non-finite values.
Results may differ from the reference program's by a relative error of at most 0.025.
Values may be sent and summed in bfloat16 or wider, within the bound.
A program may use at most 256 MiB of HBM per device.

```python
import jax
import jax.numpy as jnp
from jax import lax

D = 2048
HEADS = 32
KV_HEADS = 4
HEAD_DIM = 64
FF = 5632
HYP = 512
HYP_HEADS = 8
HYP_FF = 2048
SLOTS = 8
PIECES = 32000
ENTRIES = 512
SEQ = 1024
TEXT_ROWS = 16
N_MP = 2


def touch_ends(values, stream_key, low, top_value):
    dims = values.shape
    spot = [jax.random.randint(jax.random.fold_in(stream_key, axis), (), 0, dims[axis]) for axis in range(len(dims))]
    values = values.at[tuple(spot)].set(low)
    longest = dims.index(max(dims))
    spot[longest] = (spot[longest] + 1) % dims[longest]
    return values.at[tuple(spot)].set(top_value)


def steps_of(rng, shape, cuts, smallest, top_value):
    def one(dim, parts):
        heights = jax.random.uniform(jax.random.fold_in(jax.random.fold_in(rng, 6), dim), (parts,), jnp.float32, smallest / len(cuts), top_value / len(cuts))
        return jnp.repeat(jnp.exp(heights), shape[dim] // parts).reshape((-1,) + (1,) * (len(shape) - dim - 1))

    loudness = one(*cuts[0])
    for cut in cuts[1:]:
        loudness = loudness * one(*cut)
    return loudness


def gaussian(stream_key, dims, scale, limit, split=(), held_as=jnp.bfloat16):
    result = scale * jax.random.normal(stream_key, dims, jnp.float32)
    if split:
        result = result * steps_of(stream_key, dims, split, -0.22, 0.18)
    return jnp.clip(result, -limit, limit).astype(held_as)


def setup_inputs(seed: int = 0) -> dict:
    keys = jax.random.split(jax.random.key(seed), 20)
    return {
        "piece_ids": touch_ends(jax.random.randint(keys[0], (ENTRIES, SLOTS), 0, PIECES), jax.random.fold_in(keys[0], 1), 0, PIECES - 1).astype(jnp.int32),
        "piece_lengths": touch_ends(jax.random.randint(keys[1], (ENTRIES,), 1, SLOTS + 1), jax.random.fold_in(keys[1], 1), 1, SLOTS).astype(jnp.int32),
        "group_ids": touch_ends(jax.random.randint(keys[2], (TEXT_ROWS, SEQ), 0, ENTRIES), jax.random.fold_in(keys[2], 1), 0, ENTRIES - 1).astype(jnp.int32),
        "piece_table": gaussian(keys[3], (PIECES, HYP), 1.0, 6.0, ((0, 32),)),
        "ln_gains": jnp.clip(1.0 + 0.1 * jax.random.normal(keys[4], (2, HYP), jnp.float32), 0.5, 1.5).astype(jnp.bfloat16),
        "hyp_biases": gaussian(keys[5], (3, HYP), 0.5, 3.0, ((1, 32),)),
        "attn_weights": gaussian(keys[6], (4, HYP, HYP), HYP ** -0.5, 0.25, ((1, 32),)),
        "ffn_in_weight": gaussian(keys[7], (HYP, HYP_FF), HYP ** -0.5, 0.25, ((0, 32),)),
        "ffn_in_bias": gaussian(keys[8], (HYP_FF,), 0.5, 3.0, ((0, 32),)),
        "ffn_out_weight": gaussian(keys[9], (HYP_FF, HYP), HYP_FF ** -0.5, 0.125, ((0, 32),)),
        "proj_weight": gaussian(keys[10], (HYP, D), HYP ** -0.5, 0.25, ((0, 32),)),
        "proj_bias": gaussian(keys[11], (D,), 0.5, 3.0, ((0, 32),)),
        "lm_gains": jnp.clip(1.0 + 0.1 * jax.random.normal(keys[12], (2, D), jnp.float32), 0.5, 1.5).astype(jnp.bfloat16),
        "query_weight": gaussian(keys[13], (D, HEADS * HEAD_DIM), D ** -0.5, 0.125, ((1, 2),)),
        "kv_weights": gaussian(keys[14], (2, D, KV_HEADS * HEAD_DIM), D ** -0.5, 0.125),
        "output_weight": gaussian(keys[15], (HEADS * HEAD_DIM, D), HEAD_DIM ** -0.5, 0.75, ((0, 2),)),
        "gate_up_weight": gaussian(keys[16], (2, D, FF), D ** -0.5, 0.125, ((2, 2),)),
        "down_weight": gaussian(keys[17], (FF, D), FF ** -0.5, 0.078125, ((0, 2),)),
        "out_grad": gaussian(keys[18], (TEXT_ROWS, SEQ, D), 1.0, 6.0, ((0, 16), (1, 2))),
    }


EPSILON = 1e-05
ROPE_BASE = 10000.0
MASKED = -1e+30

@jax.custom_vjp
def low(v):
    return lax.optimization_barrier(v.astype(jnp.bfloat16)).astype(jnp.float32)

@jax.custom_vjp
def low_back(v):
    return v

def low_keep(v):
    return (low(v), None)

def low_pass(kept, grad):
    return (grad,)

def back_keep(v):
    return (v, None)

def back_low(kept, grad):
    return (low(grad),)
low.defvjp(low_keep, low_pass)
low_back.defvjp(back_keep, back_low)

def product(left, right):
    return jnp.dot(left, right, precision=lax.Precision.HIGHEST, preferred_element_type=jnp.float32)

def layer_norm(values, gain_row, shift_row):
    center = values - lax.optimization_barrier(jnp.mean(values, -1, keepdims=True))
    spread = lax.optimization_barrier(jnp.mean(center * center, -1, keepdims=True))
    return center * lax.rsqrt(spread + EPSILON) * gain_row + shift_row

def rms_norm(values, gain_row):
    return values * lax.rsqrt(lax.optimization_barrier(jnp.mean(values * values, -1, keepdims=True)) + EPSILON) * gain_row

def rope_tables(length, head_width):
    half_width = head_width // 2
    frequency = ROPE_BASE ** (-2.0 * jnp.arange(half_width, dtype=jnp.float32) / head_width)
    angles = jnp.arange(length, dtype=jnp.float32)[:, None] * frequency[None, :]
    angles = jnp.concatenate([angles, angles], -1)
    return (jnp.cos(angles), jnp.sin(angles))

def rotate(values, cosine_table, sine_table):
    half_width = values.shape[-1] // 2
    turned = jnp.concatenate([-values[..., half_width:], values[..., :half_width]], -1)
    return values * cosine_table[:, None, :] + turned * sine_table[:, None, :]

def hyper_forward(table, ln_gains, hyp_biases, attn_weights, ffn_in_weight, ffn_in_bias, ffn_out_weight, proj_weight, proj_bias, piece_ids, piece_lengths):
    entries = piece_ids.shape[0]
    head_width = HYP // HYP_HEADS
    slot_rows = low_back(table[piece_ids])
    normed = low(layer_norm(slot_rows, ln_gains[0], hyp_biases[0]))
    queries = low(low_back(product(normed[:, 0], attn_weights[0]))).reshape(entries, HYP_HEADS, head_width)
    key_rows = low(low_back(jnp.einsum('esw,wv->esv', normed, attn_weights[1], precision=lax.Precision.HIGHEST)))
    value_rows = low(low_back(jnp.einsum('esw,wv->esv', normed, attn_weights[2], precision=lax.Precision.HIGHEST)))
    key_rows = key_rows.reshape(entries, SLOTS, HYP_HEADS, head_width)
    value_rows = value_rows.reshape(entries, SLOTS, HYP_HEADS, head_width)
    scores = low_back(jnp.einsum('ehd,eshd->ehs', queries, key_rows, precision=lax.Precision.HIGHEST)) * head_width ** (-0.5)
    valid = jnp.arange(SLOTS)[None, :] < piece_lengths[:, None]
    scores = jnp.where(valid[:, None, :], scores, MASKED)
    attn_probs = low(jax.nn.softmax(scores, axis=-1))
    heads_out = low(low_back(jnp.einsum('ehs,eshd->ehd', attn_probs, value_rows, precision=lax.Precision.HIGHEST)))
    heads_out = heads_out.reshape(entries, HYP)
    residual = slot_rows[:, 0] + low_back(product(heads_out, attn_weights[3]))
    normed_two = low(layer_norm(residual, ln_gains[1], hyp_biases[1]))
    pre_act = low_back(product(normed_two, ffn_in_weight) + ffn_in_bias)
    act_low = low(jax.nn.gelu(pre_act))
    residual_two = residual + low_back(product(act_low, ffn_out_weight) + hyp_biases[2])
    pooled = low(residual_two)
    return low(low_back(product(pooled, proj_weight) + proj_bias))

def lm_sequence(row_table, token_ids, lm_gains, query_weight, kv_weights, output_weight, gate_up_weight, down_weight):
    inputs = low_back(row_table[token_ids])
    first_low = low(rms_norm(inputs, lm_gains[0]))
    cosine_table, sine_table = rope_tables(SEQ, HEAD_DIM)
    q_heads = HEADS // N_MP
    kv_here = max(KV_HEADS // N_MP, 1)
    group_size = HEADS // KV_HEADS
    per_group = q_heads // kv_here
    positions = jnp.arange(SEQ)
    allowed = positions[None, :] <= positions[:, None]
    attn_scale = HEAD_DIM ** (-0.5)
    attended = jnp.zeros((SEQ, D), jnp.float32)
    for group_index in range(N_MP):
        q_first = group_index * q_heads
        kv_first = q_first // group_size
        q_cols = slice(q_first * HEAD_DIM, (q_first + q_heads) * HEAD_DIM)
        kv_cols = slice(kv_first * HEAD_DIM, (kv_first + kv_here) * HEAD_DIM)
        q_raw = low_back(product(first_low, query_weight[:, q_cols])).reshape(SEQ, q_heads, HEAD_DIM)
        queries = low(rotate(q_raw, cosine_table, sine_table)).reshape(SEQ, kv_here, per_group, HEAD_DIM)
        k_raw = low_back(product(first_low, kv_weights[0][:, kv_cols])).reshape(SEQ, kv_here, HEAD_DIM)
        key_rows = low(rotate(k_raw, cosine_table, sine_table))
        value_rows = low(low_back(product(first_low, kv_weights[1][:, kv_cols]))).reshape(SEQ, kv_here, HEAD_DIM)
        scores = low_back(jnp.einsum('qkgd,skd->kgqs', queries, key_rows, precision=lax.Precision.HIGHEST)) * attn_scale
        scores = jnp.where(allowed, scores, MASKED)
        attn_probs = low(jax.nn.softmax(scores, axis=-1))
        heads_out = low(low_back(jnp.einsum('kgqs,skd->qkgd', attn_probs, value_rows, precision=lax.Precision.HIGHEST)))
        heads_out = heads_out.reshape(SEQ, q_heads * HEAD_DIM)
        attended = attended + product(heads_out, output_weight[q_cols])
    hidden = inputs + low_back(attended)
    second_low = low(rms_norm(hidden, lm_gains[1]))
    gate_rows = low_back(product(second_low, gate_up_weight[0]))
    up_rows = low_back(product(second_low, gate_up_weight[1]))
    ffn_act = low(jax.nn.silu(gate_rows) * up_rows)
    return hidden + low_back(product(ffn_act, down_weight))

def to_float(array):
    return array.astype(jnp.float32)

def reference(piece_ids, piece_lengths, group_ids, piece_table, ln_gains, hyp_biases, attn_weights, ffn_in_weight, ffn_in_bias, ffn_out_weight, proj_weight, proj_bias, lm_gains, query_weight, kv_weights, output_weight, gate_up_weight, down_weight, out_grad):
    hyper_params = (to_float(piece_table), to_float(ln_gains), to_float(hyp_biases), to_float(attn_weights), to_float(ffn_in_weight), to_float(ffn_in_bias), to_float(ffn_out_weight), to_float(proj_weight), to_float(proj_bias))

    def hyper_apply(*params):
        return hyper_forward(*params, piece_ids, piece_lengths)
    new_rows, hyper_back = jax.vjp(hyper_apply, *hyper_params)
    lm_weights = (to_float(lm_gains), to_float(query_weight), to_float(kv_weights), to_float(output_weight), to_float(gate_up_weight), to_float(down_weight))

    def lm_all(row_table):

        def per_sequence(token_ids):
            return lm_sequence(row_table, token_ids, *lm_weights)
        return lax.map(jax.checkpoint(per_sequence), group_ids)
    lm_out, lm_back = jax.vjp(lm_all, new_rows)
    row_grad, = lm_back(to_float(out_grad))
    hyper_grads = hyper_back(row_grad)
    return (lm_out.astype(jnp.bfloat16), row_grad, hyper_grads[0], hyper_grads[1], hyper_grads[2], hyper_grads[3], hyper_grads[4], hyper_grads[5], hyper_grads[6], hyper_grads[7], hyper_grads[8])
```

```python
import functools

import jax
import jax.numpy as jnp
from jax import lax
from jax.experimental import pallas as pl
from jax.experimental.pallas import tpu as pltpu
from jax.sharding import PartitionSpec as P

HEADS = 32
KV_HEADS = 4
HEAD_DIM = 64
HYP_HEADS = 8

EPSILON = 1e-05
ROPE_BASE = 10000.0
MASKED = -1e30
BOTH = ("dp", "mp")
LOW = jnp.bfloat16
WIDE = jnp.float32
QUERY_BLOCK = 256
MIB = 1 << 20
PLANES = 4
DENSE_ROWS, REST_ROWS = 192, 80
UNIT_BLOCK = 256
VMEM_LIMIT = 62 * MIB
FIRST_ORDER = (
    1, 0, 2, 2, 2, 2, 2, 0, 1, 0, 0, 2, 2, 0, 3, 1, 0, 2, 2, 1, 0, 2, 1, 0, 2, 3, 3, 0, 1, 2, 2, 0, 3, 2, 1, 2, 0,
    0, 1, 2, 1, 1, 2, 0, 2, 3, 3, 0, 1, 0, 0, 0, 0, 0, 1, 1, 1, 3, 1, 1, 0, 0, 2, 0, 3, 2, 2, 2, 1, 1, 0, 3, 2, 0,
    1, 1, 1, 1, 2, 1, 0, 0, 0, 2, 2, 0, 1, 3, 1, 0, 1, 0, 2, 1, 1, 2, 3, 0, 2, 2, 2, 0, 1, 0, 0, 0, 2, 2, 1, 2, 2,
    0, 2, 0, 2, 2,
)
LAST_ORDER = (
    5, 4, 1, 4, 4, 4, 2, 4, 4, 4, 0, 4, 4, 4, 4, 4, 4, 0, 4, 4, 4, 4, 2, 4, 1, 3, 0, 4, 4, 3, 0, 4, 4, 2, 2, 4, 3,
    4, 1, 3, 4, 4, 4, 2, 4, 1, 3, 3, 4, 4, 1, 2, 1, 0, 0,
)
GATHER_STEPS = 22
ROW_ORDER = (
    0, 0, 0, 0, 0, 0, 0, 0, 0, 0, 0, 0, 0, 0, 0, 0, 0, 0, 0, 0, 0, 0, 0, 0, 0, 0, 0, 0, 0, 0, 0, 1, 0,
)
HEADS_A_STEP = 4
QUERY_SCALE = HEAD_DIM ** (-0.5) * 1.4426950408889634


def rms_norm(values, gain_row):
    return values * lax.rsqrt(jnp.mean(values * values, -1, keepdims=True) + EPSILON) * gain_row


def dot(left, right, dims):
    return lax.dot_general(left, right, ((dims[:1], dims[1:]), ((), ())), preferred_element_type=WIDE)


def rope_tables(length):
    half = HEAD_DIM // 2
    frequency = ROPE_BASE ** (-2.0 * jnp.arange(half, dtype=WIDE) / HEAD_DIM)
    angles = frequency[:, None] * jnp.arange(length, dtype=WIDE)[None, :]
    return jnp.cos(angles), jnp.sin(angles)


def turn(columns, cosine, sine):
    half = HEAD_DIM // 2
    first, second = columns[:half], columns[half:]
    return jnp.concatenate([first * cosine - second * sine, second * cosine + first * sine], 0)


def turn_back(columns, cosine, sine):
    half = HEAD_DIM // 2
    first, second = columns[:half], columns[half:]
    return jnp.concatenate([first * cosine + second * sine, second * cosine - first * sine], 0)


def keep_causal(block, fill):
    key = lax.broadcasted_iota(jnp.int32, block.shape, 0)
    query = lax.broadcasted_iota(jnp.int32, block.shape, 1)
    return jnp.where(key <= query, block, fill)


def own_half(me_ref, left, right):
    first = me_ref[0] == 0
    return jnp.where(first, left, right), jnp.where(first, right, left)


def attend_kernel(per_group, me_ref, q_ref, k_ref, v_ref, cos_ref, sin_ref, *refs):
    *out_refs, log_ref, key_rows, out_all = refs
    seq_len = q_ref.shape[1]
    width = min(QUERY_BLOCK, seq_len)
    cosine, sine = cos_ref[...], sin_ref[...]
    count = q_ref.shape[0] // HEAD_DIM

    @pl.when(lax.rem(pl.program_id(0) * count, per_group) == 0)
    def _():
        key_rows[...] = turn(k_ref[...].astype(WIDE), cosine, sine).T.astype(LOW)

    queries = [
        (turn(q_ref[head * HEAD_DIM : (head + 1) * HEAD_DIM].astype(WIDE), cosine, sine) * QUERY_SCALE).astype(LOW)
        for head in range(count)
    ]

    def scores(start, head):
        q_block = queries[head][:, start : start + width]
        edge = dot(key_rows[start : start + width], q_block, (1, 0))
        return edge, dot(key_rows[:start], q_block, (1, 0)) if start else None

    def finish(start, head, edge, past):
        here = slice(start, start + width)
        lanes = slice(head * HEAD_DIM, (head + 1) * HEAD_DIM)
        edge = keep_causal(edge, MASKED)
        top = jnp.max(edge, 0, keepdims=True)
        if start:
            top = jnp.maximum(top, jnp.max(past, 0, keepdims=True))
        edge = jnp.exp2(edge - top)
        total = jnp.sum(edge, 0, keepdims=True)
        out = dot(v_ref[:, here], edge.astype(LOW), (1, 0))
        if start:
            past = jnp.exp2(past - top)
            total = total + jnp.sum(past, 0, keepdims=True)
            out = out + dot(v_ref[:, :start], past.astype(LOW), (1, 0))
        out_all[lanes, here] = (out / total).astype(LOW)
        log_ref[head, :, here] = top + jnp.log2(total)

    items = [(start, head) for start in range(0, seq_len, width) for head in range(count)]
    ready = scores(*items[0])
    for number, item in enumerate(items):
        following = scores(*items[number + 1]) if number + 1 < len(items) else None
        finish(*item, *ready)
        ready = following
    if len(out_refs) == 2:
        half = seq_len // 2
        out_refs[0][...], out_refs[1][...] = own_half(me_ref, out_all[:, :half], out_all[:, half:])
    else:
        out_refs[0][...] = out_all[...]


def attend(me, qkv, cosine, sine, q_heads, kv_heads, parts):
    per_group = q_heads // kv_heads
    seq_len = qkv.shape[1]
    column = (HEAD_DIM, seq_len)
    count = HEADS_A_STEP
    several = (count * HEAD_DIM, seq_len)
    whole = pl.BlockSpec(cosine.shape, lambda h: (0, 0))
    return pl.pallas_call(
        functools.partial(attend_kernel, per_group),
        grid=(q_heads // count,),
        in_specs=[
            pl.BlockSpec(memory_space=pltpu.SMEM),
            pl.BlockSpec(several, lambda h: (h, 0)),
            pl.BlockSpec(column, lambda h: (q_heads + h * count // per_group, 0)),
            pl.BlockSpec(column, lambda h: (q_heads + kv_heads + h * count // per_group, 0)),
            whole,
            whole,
        ],
        out_specs=[pl.BlockSpec((count * HEAD_DIM, seq_len // parts), lambda h: (h, 0))] * parts
        + [pl.BlockSpec((count, 1, seq_len), lambda h: (h, 0, 0))],
        out_shape=[jax.ShapeDtypeStruct((q_heads * HEAD_DIM, seq_len // parts), LOW)] * parts
        + [jax.ShapeDtypeStruct((q_heads, 1, seq_len), WIDE)],
        scratch_shapes=[pltpu.VMEM((seq_len, HEAD_DIM), LOW), pltpu.VMEM(several, LOW)],
        compiler_params=pltpu.CompilerParams(vmem_limit_bytes=VMEM_LIMIT),
        cost_estimate=pl.CostEstimate(
            flops=2 * q_heads * seq_len * seq_len * HEAD_DIM,
            bytes_accessed=4 * qkv.size,
            transcendentals=q_heads * seq_len * seq_len // 2,
        ),
        name="attend",
    )(me, qkv, qkv, qkv, cosine, sine)


def attend_back_kernel(per_group, parts, terms, me_ref, q_ref, k_ref, v_ref, log_ref, cos_ref, sin_ref, *refs):
    out_refs, grad_refs, refs = refs[:parts], refs[parts : 2 * parts], refs[2 * parts :]
    term_refs, refs = refs[:terms], refs[terms:]
    if terms:
        sum_ref, refs = refs[3], refs[:3] + refs[4:]
        sum_ref[...] = sum(ref[...].astype(WIDE) for ref in term_refs).astype(LOW)
    dq_ref, dk_ref, dv_ref, key_cols, key_rows, value_rows, key_sum, value_sum = refs
    seq_len = q_ref.shape[1]
    width = min(QUERY_BLOCK, seq_len)
    cosine, sine = cos_ref[...], sin_ref[...]
    count = q_ref.shape[0] // HEAD_DIM
    heads = range(count)
    member = lax.rem(pl.program_id(0) * count, per_group)

    def in_order(pieces, lanes):
        if len(pieces) == 1:
            return pieces[0][lanes]
        return jnp.concatenate(own_half(me_ref, pieces[0][lanes], pieces[1][lanes]), 1)

    @pl.when(member == 0)
    def _():
        turned = turn(k_ref[...].astype(WIDE), cosine, sine)
        key_cols[...] = turned.astype(LOW)
        key_rows[...] = turned.T.astype(LOW)
        value_rows[...] = v_ref[...].astype(WIDE).T.astype(LOW)
        key_sum[...] = jnp.zeros_like(key_sum)
        value_sum[...] = jnp.zeros_like(value_sum)

    queries, query_rows, grads, grad_rows, deltas = [], [], [], [], []
    for head in heads:
        lanes = slice(head * HEAD_DIM, (head + 1) * HEAD_DIM)
        turned = turn(q_ref[lanes].astype(WIDE), cosine, sine) * QUERY_SCALE
        queries.append(turned.astype(LOW))
        query_rows.append(turned.T.astype(LOW))
        grad = in_order(grad_refs, lanes)
        grads.append(grad)
        grad_wide = grad.astype(WIDE)
        grad_rows.append(grad_wide.T.astype(LOW))
        deltas.append(jnp.sum(grad_wide * in_order(out_refs, lanes).astype(WIDE), 0, keepdims=True))

    def pieces_of(start):
        return [slice(start, start + width)] + ([slice(0, start)] if start else [])

    def products(start):
        here = slice(start, start + width)
        return [
            [
                (dot(key_rows[keys], queries[head][:, here], (1, 0)), dot(value_rows[keys], grads[head][:, here], (1, 0)))
                for head in heads
            ]
            for keys in pieces_of(start)
        ]

    def finish(start, found):
        here = slice(start, start + width)
        dq = [0.0] * count
        for number, keys in enumerate(pieces_of(start)):
            probs, scores = [], []
            for head in heads:
                raw, grad_probs = found[number][head]
                prob = jnp.exp2(raw - log_ref[head, :, here])
                if number == 0:
                    prob = keep_causal(prob, 0.0)
                probs.append(prob.astype(LOW))
                scores.append((prob * (grad_probs - deltas[head][:, here])).astype(LOW))
                dq[head] += dot(key_cols[:, keys], scores[head], (1, 0))
            grad_part = jnp.concatenate([rows[here] for rows in grad_rows], 0)
            query_part = jnp.concatenate([rows[here] for rows in query_rows], 0)
            value_sum[keys] += dot(jnp.concatenate(probs, 1), grad_part, (1, 0))
            key_sum[keys] += dot(jnp.concatenate(scores, 1), query_part, (1, 0))
        for head in heads:
            back = turn_back(dq[head] * HEAD_DIM ** (-0.5), cosine[:, here], sine[:, here])
            dq_ref[head * HEAD_DIM : (head + 1) * HEAD_DIM, here] = back.astype(LOW)

    starts = list(range(0, seq_len, width))
    ready = products(0)
    for number, start in enumerate(starts):
        following = products(starts[number + 1]) if number + 1 < len(starts) else None
        finish(start, ready)
        ready = following

    @pl.when(member == per_group - count)
    def _():
        dk_ref[...] = turn_back(key_sum[...].T * (HEAD_DIM ** (-0.5) / QUERY_SCALE), cosine, sine).astype(LOW)
        dv_ref[...] = value_sum[...].T.astype(LOW)


def attend_back(me, qkv, outs, log_total, grads, cosine, sine, q_heads, kv_heads, terms=()):
    per_group = q_heads // kv_heads
    seq_len = qkv.shape[1]
    parts = len(outs)
    count = HEADS_A_STEP
    column = (HEAD_DIM, seq_len)
    whole = pl.BlockSpec(cosine.shape, lambda h: (0, 0))
    by_head = pl.BlockSpec((count * HEAD_DIM, seq_len), lambda h: (h, 0))
    by_group = pl.BlockSpec(column, lambda h: (h * count // per_group, 0))
    in_parts = pl.BlockSpec((count * HEAD_DIM, seq_len // parts), lambda h: (h, 0))
    steps = q_heads // count
    term_rows = [pl.BlockSpec((term.shape[0] // steps, term.shape[1]), lambda h: (h, 0)) for term in terms]
    return pl.pallas_call(
        functools.partial(attend_back_kernel, per_group, parts, len(terms)),
        grid=(q_heads // count,),
        in_specs=[
            pl.BlockSpec(memory_space=pltpu.SMEM),
            by_head,
            pl.BlockSpec(column, lambda h: (q_heads + h * count // per_group, 0)),
            pl.BlockSpec(column, lambda h: (q_heads + kv_heads + h * count // per_group, 0)),
            pl.BlockSpec((count, 1, seq_len), lambda h: (h, 0, 0)),
            whole,
            whole,
        ]
        + [in_parts] * (2 * parts)
        + term_rows,
        out_specs=[by_head, by_group, by_group] + term_rows[:1],
        out_shape=[
            jax.ShapeDtypeStruct((q_heads * HEAD_DIM, seq_len), LOW),
            jax.ShapeDtypeStruct((kv_heads * HEAD_DIM, seq_len), LOW),
            jax.ShapeDtypeStruct((kv_heads * HEAD_DIM, seq_len), LOW),
        ]
        + [jax.ShapeDtypeStruct(term.shape, LOW) for term in terms[:1]],
        scratch_shapes=[
            pltpu.VMEM((HEAD_DIM, seq_len), LOW),
            pltpu.VMEM((seq_len, HEAD_DIM), LOW),
            pltpu.VMEM((seq_len, HEAD_DIM), LOW),
            pltpu.VMEM((seq_len, HEAD_DIM), WIDE),
            pltpu.VMEM((seq_len, HEAD_DIM), WIDE),
        ],
        compiler_params=pltpu.CompilerParams(vmem_limit_bytes=VMEM_LIMIT),
        cost_estimate=pl.CostEstimate(
            flops=5 * q_heads * seq_len * seq_len * HEAD_DIM,
            bytes_accessed=8 * qkv.size,
            transcendentals=q_heads * seq_len * seq_len // 2,
        ),
        name="attend_back",
    )(me, qkv, qkv, qkv, log_total, cosine, sine, *outs, *grads, *terms)


def feed_kernel(last_block, x_ref, d_act_ref, gate_up_ref, down_ref, out_ref, back_ref, out_sum, back_sum):
    step, last = pl.program_id(0), pl.num_programs(0) - 1

    @pl.when(step == 0)
    def _():
        out_sum[...] = jnp.zeros_like(out_sum)
        back_sum[...] = jnp.zeros_like(back_sum)

    def units(size):
        x, down = x_ref[...], down_ref[:size]
        gate_weight, up_weight = gate_up_ref[0, :, :size], gate_up_ref[1, :, :size]
        gate = dot(x, gate_weight, (1, 0))
        up = dot(x, up_weight, (1, 0))
        d_act = d_act_ref[:, :size].astype(WIDE)
        sigmoid = jax.nn.sigmoid(gate)
        silu = gate * sigmoid
        act = (silu * up).astype(LOW)
        d_up = (d_act * silu).astype(LOW)
        d_gate = (d_act * up * (sigmoid + silu * (1.0 - sigmoid))).astype(LOW)
        out_sum[...] += dot(act, down, (1, 0))
        back_sum[...] += dot(d_gate, gate_weight, (1, 1))
        back_sum[...] += dot(d_up, up_weight, (1, 1))

    block = down_ref.shape[0]
    if last_block == block:
        units(block)
    else:
        pl.when(step < last)(lambda: units(block))
        pl.when(step == last)(lambda: units(last_block))

    @pl.when(step == last)
    def _():
        out_ref[...] = out_sum[...].astype(LOW)
        back_ref[...] = back_sum[...].astype(LOW)


def feed_forward(x, d_act, which, gate_up, down):
    tokens, width = x.shape
    units = down.shape[0]
    block = 2 * UNIT_BLOCK if units % UNIT_BLOCK == 0 else units
    steps = pl.cdiv(units, block)
    whole = pl.BlockSpec((tokens, width), lambda f: (0, 0))
    result = jax.ShapeDtypeStruct((tokens, width), LOW)
    return pl.pallas_call(
        functools.partial(feed_kernel, units - (steps - 1) * block),
        grid=(steps,),
        in_specs=[
            whole,
            pl.BlockSpec((tokens, block), lambda f: (which, f)),
            pl.BlockSpec((2, width, block), lambda f: (0, 0, f)),
            pl.BlockSpec((block, width), lambda f: (f, 0)),
        ],
        out_specs=[whole, whole],
        out_shape=[result, result],
        scratch_shapes=[pltpu.VMEM((tokens, width), WIDE), pltpu.VMEM((tokens, width), WIDE)],
        compiler_params=pltpu.CompilerParams(vmem_limit_bytes=VMEM_LIMIT),
        cost_estimate=pl.CostEstimate(
            flops=10 * tokens * width * units,
            bytes_accessed=6 * width * units + 8 * tokens * width,
            transcendentals=tokens * units,
        ),
        name="feed_forward",
    )(x, d_act, gate_up, down)


def second_back_kernel(hidden_ref, dy_ref, gain_ref, *refs):
    *part_refs, out_ref, grad_ref = refs
    outs, backs = part_refs[: len(part_refs) // 2], part_refs[len(part_refs) // 2 :]
    hidden = hidden_ref[...]
    out_ref[...] = (hidden + sum(ref[...].astype(WIDE) for ref in outs)).astype(LOW)
    scale = lax.rsqrt(jnp.mean(hidden * hidden, -1, keepdims=True) + EPSILON)
    inner = sum(ref[...].astype(WIDE) for ref in backs) * gain_ref[1:2].astype(WIDE)
    mean = jnp.mean(hidden * inner, -1, keepdims=True)
    back = scale * inner - hidden * (scale * scale * scale * mean)
    grad_ref[...] = (dy_ref[...].astype(WIDE) + back).astype(LOW)


def second_back(hidden, dy, gains, outs, backs):
    tokens, width = hidden.shape
    block = min(64, tokens)
    rows = pl.BlockSpec((block, width), lambda i: (i, 0))
    result = jax.ShapeDtypeStruct(hidden.shape, LOW)
    return pl.pallas_call(
        second_back_kernel,
        grid=(tokens // block,),
        in_specs=[rows, rows, pl.BlockSpec((2, width), lambda i: (0, 0))] + [rows] * (len(outs) + len(backs)),
        out_specs=[rows, rows],
        out_shape=[result, result],
        compiler_params=pltpu.CompilerParams(vmem_limit_bytes=VMEM_LIMIT),
        cost_estimate=pl.CostEstimate(flops=12 * hidden.size, bytes_accessed=18 * hidden.size, transcendentals=0),
        name="second_back",
    )(hidden, dy, gains, *outs, *backs)


class Place:
    def __init__(self):
        chip, self.core = lax.axis_index("dp"), lax.axis_index("mp")
        self.z = lax.div(chip, 4)
        self.y, self.x = lax.rem(lax.div(chip, 2), 2), lax.rem(chip, 2)
        self.below, self.above = self.z > 0, self.z < PLANES - 1
        z, y, x, core = self.z, self.y, self.x, self.core
        self.others = (z + 1 - 2 * lax.rem(z, 2), lax.rem(z + 2, PLANES), PLANES - 1 - z)
        self.targets = {
            "x": self.device(z, y, 1 - x, core),
            "y": self.device(z, 1 - y, x, core),
            "diagonal": self.device(z, 1 - y, 1 - x, core),
            "core": self.device(z, y, x, 1 - core),
            "up": self.device(z + 1, y, x, core),
            "down": self.device(z - 1, y, x, core),
        }
        for turn, plane in enumerate(self.others):
            self.targets[turn] = self.device(plane, y, x, core)

    def device(self, plane, y, x, core):
        return {"dp": (plane * 2 + y) * 2 + x, "mp": core}

    def chip(self, kind):
        y = 1 - self.y if kind in (2, 3) else self.y
        x = 1 - self.x if kind in (1, 3) else self.x
        return y * 2 + x

    def slot(self, kind, plane, core):
        return (plane * 4 + self.chip(kind)) * 2 + core

    def levels(self, distance):
        if distance == 0:
            return [(0, self.z, None)]
        return [
            (1, self.z + distance, self.z + distance < PLANES),
            (-1, self.z - distance, self.z >= distance),
        ]

    def at(self, distance, step):
        for sign, plane, valid in self.levels(distance):
            if valid is None:
                step(sign, plane)
            else:
                pl.when(valid)(functools.partial(step, sign, plane))

    def steps_at(self, distance, step):
        for sign, plane, valid in self.levels(distance):
            if valid is None:
                step(sign, plane)
            else:
                pl.when(valid)(functools.partial(step, sign, plane))
            yield

    def greet(self):
        barrier = pltpu.get_barrier_semaphore()
        names = ("x", "y", "diagonal", "core", 0, 1, 2)
        for name in names:
            pl.semaphore_signal(barrier, inc=1, device_id=self.targets[name], device_id_type=pl.DeviceIdType.MESH)
        pl.semaphore_wait(barrier, len(names))


def halves(shape):
    rows, columns = shape[-2:]
    if rows >= 32:
        cut = rows // 32 * 16
        return (slice(0, cut), slice(None)), (slice(cut, rows), slice(None))
    cut = columns // 2
    return (slice(None), slice(0, cut)), (slice(None), slice(cut, columns))


def send(source, target, send_sem, recv_sem, device):
    pltpu.make_async_remote_copy(
        src_ref=source,
        dst_ref=target,
        send_sem=send_sem,
        recv_sem=recv_sem,
        device_id=device,
        device_id_type=pl.DeviceIdType.MESH,
    ).start()


def sent(view, sem):
    pltpu.make_async_copy(view, view, sem).wait()


def dma_grid(*shape):
    return pltpu.SemaphoreType.DMA(shape)


def gather_sems():
    return [pltpu.SemaphoreType.DMA, dma_grid(6, PLANES), dma_grid(5, PLANES), dma_grid(5, PLANES), dma_grid(5, PLANES)]


def gather_steps(place, share, whole, sems):
    own_sem, link_send, link_recv, core_send, core_recv = sems
    near, far = halves(share.shape)
    z, core = place.z, place.core

    def view(kind, plane, whose=None):
        whose = core if whose is None else whose
        if kind >= 3:
            return whole.at[(place.slot(3, plane, whose), *(near if kind == 3 else far))]
        return whole.at[place.slot(kind, plane, whose)]

    def forward(name, source, target, number, kind, plane):
        send(source, target, link_send.at[number, plane], link_recv.at[kind, plane], place.targets[name])

    def to_core(source, kind, plane):
        send(source, view(kind, plane), core_send.at[kind, plane], core_recv.at[kind, plane], place.targets["core"])

    def column(sign, plane):
        target = view(0, plane)
        source = target if sign else share
        if sign:
            sent(target, link_recv.at[0, plane])
        if sign <= 0:
            pl.when(place.above)(lambda: forward("up", source, target, 4, 0, plane))
        if sign >= 0:
            pl.when(place.below)(lambda: forward("down", source, target, 5, 0, plane))
        forward("x", source, target, 0, 1, plane)
        forward("y", source, target, 1, 2, plane)
        to_core(source, 0, plane)

    def side_x(sign, plane):
        sent(view(1, plane), link_recv.at[1, plane])
        part = whole.at[(place.slot(1, plane, core), *far)]
        forward("y", part, part, 3, 4, plane)
        to_core(view(1, plane), 1, plane)

    def side_y(sign, plane):
        sent(view(2, plane), link_recv.at[2, plane])
        part = whole.at[(place.slot(2, plane, core), *near)]
        forward("x", part, part, 2, 3, plane)
        to_core(view(2, plane), 2, plane)

    def diagonal(kind, sign, plane):
        sent(view(kind, plane), link_recv.at[kind, plane])
        to_core(view(kind, plane), kind, plane)

    diagonal_x, diagonal_y = functools.partial(diagonal, 3), functools.partial(diagonal, 4)
    keep = pltpu.make_async_copy(share, view(0, z), own_sem)
    keep.start()
    for step in range(PLANES + 2):
        for stage, lag in ((column, 0), (side_x, 1), (side_y, 1), (diagonal_x, 2), (diagonal_y, 2)):
            if 0 <= step - lag < PLANES:
                yield from place.steps_at(step - lag, stage)
    keep.wait()
    for plane in range(PLANES):
        for kind in range(5):
            sent(view(kind, plane, 1 - core), core_recv.at[kind, plane])
    yield
    for plane in range(PLANES):
        for kind in range(5):
            sent(view(kind, plane), core_send.at[kind, plane])
        for number, part in enumerate((share, share, share.at[near], share.at[far])):
            sent(part, link_send.at[number, plane])
        pl.when((plane <= z) & place.above)(lambda: sent(share, link_send.at[4, plane]))
        pl.when((plane >= z) & place.below)(lambda: sent(share, link_send.at[5, plane]))
    yield


def late_gather_sems():
    return [
        pltpu.SemaphoreType.DMA,
        dma_grid(4),
        dma_grid(4),
        dma_grid(2, 4, PLANES),
        dma_grid(4, PLANES),
        dma_grid(4, PLANES),
        dma_grid(4, PLANES),
    ]


def late_gather_steps(place, share, whole, sems):
    own_sem, plane_send, plane_recv, line_send, line_recv, core_send, core_recv = sems
    near, far = halves(share.shape)
    z, core = place.z, place.core

    def view(kind, plane, whose=None):
        return whole.at[place.slot(kind, plane, core if whose is None else whose)]

    def part(kind, half):
        return whole.at[(place.slot(kind, z, core), *half)]

    def forward(name, source, target, number):
        send(source, target, plane_send.at[number], plane_recv.at[number], place.targets[name])

    def on_line(name, source, kind, plane):
        which = 0 if name == "up" else 1
        send(
            source, view(kind, plane), line_send.at[which, kind, plane], line_recv.at[kind, plane], place.targets[name]
        )

    def own_plane(source, kind):
        pl.when(place.above)(lambda: on_line("up", source, kind, z))
        pl.when(place.below)(lambda: on_line("down", source, kind, z))
        send(source, view(kind, z), core_send.at[kind, z], core_recv.at[kind, z], place.targets["core"])

    def line(kind, sign, plane):
        target = view(kind, plane)
        sent(target, line_recv.at[kind, plane])
        if sign < 0:
            pl.when(place.above)(lambda: on_line("up", target, kind, plane))
        else:
            pl.when(place.below)(lambda: on_line("down", target, kind, plane))
        send(target, target, core_send.at[kind, plane], core_recv.at[kind, plane], place.targets["core"])

    keep = pltpu.make_async_copy(share, view(0, z), own_sem)
    keep.start()
    forward("x", share, view(0, z), 0)
    forward("y", share, view(0, z), 1)
    own_plane(share, 0)
    yield
    sent(view(1, z), plane_recv.at[0])
    forward("y", part(1, far), part(1, far), 3)
    own_plane(view(1, z), 1)
    yield
    sent(view(2, z), plane_recv.at[1])
    forward("x", part(2, near), part(2, near), 2)
    own_plane(view(2, z), 2)
    yield
    for distance in range(1, PLANES):
        for kind in range(4):
            if distance == 1 and kind == 3:
                sent(part(3, near), plane_recv.at[2])
                sent(part(3, far), plane_recv.at[3])
                own_plane(view(3, z), 3)
                yield
            yield from place.steps_at(distance, functools.partial(line, kind))
    keep.wait()
    for plane in range(PLANES):
        for kind in range(4):
            sent(view(kind, plane, 1 - core), core_recv.at[kind, plane])
    yield
    for number, sent_part in enumerate((share, share, share.at[near], share.at[far])):
        sent(sent_part, plane_send.at[number])
    for plane in range(PLANES):
        for kind in range(4):
            sent(share, core_send.at[kind, plane])
            up, down = line_send.at[0, kind, plane], line_send.at[1, kind, plane]
            pl.when((plane <= z) & place.above)(functools.partial(sent, share, up))
            pl.when((plane >= z) & place.below)(functools.partial(sent, share, down))
    yield


def half_shapes(one):
    return [tuple(len(range(*cut.indices(size))) for cut, size in zip(half, one)) for half in halves(one)]


def scatter_scratch(one):
    near, far = half_shapes(one)
    line = pltpu.VMEM((PLANES, *one), LOW)
    buffers = [
        pltpu.VMEM((4, PLANES, *one), LOW),
        line,
        line,
        pltpu.VMEM((PLANES, *near), LOW),
        pltpu.VMEM((PLANES, *far), LOW),
        line,
        line,
        pltpu.VMEM(one, WIDE),
    ]
    return buffers + [dma_grid(6, PLANES), dma_grid(6, PLANES), dma_grid(4, PLANES), dma_grid(4, PLANES)]


def from_other_core(place, parts, mine, core_send, core_recv, between=None):
    def start(plane):
        for kind in (3, 1, 2, 0):
            send(
                parts.at[place.slot(kind, plane, 1 - place.core)],
                mine.at[kind, plane],
                core_send.at[kind, plane],
                core_recv.at[kind, plane],
                place.targets["core"],
            )

    if between is None:
        for step in range(PLANES):
            place.at(PLANES - 1 - step, lambda sign, plane: start(plane))
    else:
        start(place.others[2])
        start(place.others[1])
        between()
        start(place.others[0])
        start(place.z)


def scatter_steps(place, parts, total, scratch, between=None):
    mine, by_x, by_y, diagonal_x, diagonal_y, line_up, line_down, wide, *sems = scratch
    link_send, link_recv, core_send, core_recv = sems
    near, far = halves(parts.shape)
    z, core, last = place.z, place.core, PLANES - 1

    def own(kind, plane):
        return parts[place.slot(kind, plane, core)]

    def forward(name, source, target, number, plane):
        send(source, target, link_send.at[number, plane], link_recv.at[number, plane], place.targets[name])

    def arrived(view, number, plane):
        sent(view, link_recv.at[number, plane])

    def from_core(kind, plane):
        sent(mine.at[kind, plane], core_recv.at[kind, plane])

    def diagonal(sign, plane):
        from_core(3, plane)
        mine[3, plane] += own(3, plane)
        forward("x", mine.at[(3, plane, *near)], diagonal_x.at[plane], 0, plane)
        forward("y", mine.at[(3, plane, *far)], diagonal_y.at[plane], 1, plane)

    def side_x(sign, plane):
        from_core(1, plane)
        mine[1, plane] += own(1, plane)
        arrived(diagonal_y.at[plane], 1, plane)
        mine[(1, plane, *far)] += diagonal_y[plane]
        forward("x", mine.at[1, plane], by_x.at[plane], 2, plane)

    def side_y(sign, plane):
        from_core(2, plane)
        mine[2, plane] += own(2, plane)
        arrived(diagonal_x.at[plane], 0, plane)
        mine[(2, plane, *near)] += diagonal_x[plane]
        forward("y", mine.at[2, plane], by_y.at[plane], 3, plane)

    def column(sign, plane):
        from_core(0, plane)
        arrived(by_x.at[plane], 2, plane)
        arrived(by_y.at[plane], 3, plane)
        wide[...] = (own(0, plane).astype(WIDE) + mine[0, plane].astype(WIDE)) + (
            by_x[plane].astype(WIDE) + by_y[plane].astype(WIDE)
        )

        def add(line, number):
            arrived(line.at[plane], number, plane)
            wide[...] += line[plane].astype(WIDE)

        if sign >= 0:
            pl.when(place.below)(lambda: add(line_up, 4))
        if sign <= 0:
            pl.when(place.above)(lambda: add(line_down, 5))
        if sign == 0:
            total[...] = wide[...]
        else:
            mine[0, plane] = wide[...].astype(LOW)
        if sign > 0:
            forward("up", mine.at[0, plane], line_up.at[plane], 4, plane)
        if sign < 0:
            forward("down", mine.at[0, plane], line_down.at[plane], 5, plane)

    from_other_core(place, parts, mine, core_send, core_recv, between)
    yield
    for step in range(PLANES + 2):
        for stage, lag in ((diagonal, 0), (side_x, 1), (side_y, 1), (column, 2)):
            if 0 <= step - lag < PLANES:
                yield from place.steps_at(last - (step - lag), stage)
    for plane in range(PLANES):
        for kind in range(4):
            sent(mine.at[kind, plane], core_send.at[kind, plane])
        views = (diagonal_x.at[plane], diagonal_y.at[plane], by_x.at[plane], by_y.at[plane])
        for number, part in enumerate(views):
            sent(part, link_send.at[number, plane])
        pl.when(plane > z)(lambda: sent(mine.at[0, plane], link_send.at[4, plane]))
        pl.when(plane < z)(lambda: sent(mine.at[0, plane], link_send.at[5, plane]))
    yield


def line_share_sems():
    return [dma_grid(3), dma_grid(3)]


def line_share_steps(place, buffer, sems):
    line_send, line_recv = sems
    own = buffer.at[place.z]
    for turn in range(3):
        send(own, own, line_send.at[turn], line_recv.at[turn], place.targets[turn])
    yield
    for turn, plane in enumerate(place.others):
        sent(buffer.at[plane], line_recv.at[turn])
    for turn in range(3):
        sent(own, line_send.at[turn])
    yield


def small_gather_sems():
    return [dma_grid(3), dma_grid(3), dma_grid(3), dma_grid(3), pltpu.SemaphoreType.DMA, pltpu.SemaphoreType.DMA]


def small_gather(place, share, whole, sems):
    line_send, line_recv, plane_send, plane_recv, core_send, core_recv = sems
    here, core = place.chip(0), place.core
    whole[place.z, here, core] = share
    own = whole.at[place.z, here, core]
    for turn in range(3):
        send(own, own, line_send.at[turn], line_recv.at[turn], place.targets[turn])
    for turn, plane in enumerate(place.others):
        sent(whole.at[plane, here, core], line_recv.at[turn])
    column = whole.at[:, here, core]
    names = ("x", "y", "diagonal")
    for turn, name in enumerate(names):
        send(column, column, plane_send.at[turn], plane_recv.at[turn], place.targets[name])
    for turn in range(3):
        sent(whole.at[:, place.chip(turn + 1), core], plane_recv.at[turn])
    mine = whole.at[:, :, core]
    send(mine, mine, core_send, core_recv, place.targets["core"])
    sent(whole.at[:, :, 1 - core], core_recv)
    for turn in range(3):
        sent(own, line_send.at[turn])
        sent(column, plane_send.at[turn])
    sent(mine, core_send)


def plane_gather_sems():
    return [dma_grid(4, PLANES), dma_grid(4, PLANES), dma_grid(5, PLANES), dma_grid(5, PLANES)]


def plane_gather_steps(place, whole, sems):
    plane_send, plane_recv, core_send, core_recv = sems
    near, far = halves(whole.shape)
    core = place.core

    def view(kind, part, whose=None):
        whose = core if whose is None else whose
        if kind >= 3:
            return whole.at[(place.slot(3, part, whose), *(near if kind == 3 else far))]
        return whole.at[place.slot(kind, part, whose)]

    def forward(name, view, number, part):
        send(view, view, plane_send.at[number, part], plane_recv.at[number, part], place.targets[name])

    def to_core(kind, part):
        here = view(kind, part)
        send(here, here, core_send.at[kind, part], core_recv.at[kind, part], place.targets["core"])

    def start(part):
        forward("x", view(0, part), 0, part)
        forward("y", view(0, part), 1, part)
        to_core(0, part)

    def side(kind, part):
        sent(view(kind, part), plane_recv.at[kind - 1, part])
        half = whole.at[(place.slot(kind, part, core), *(far if kind == 1 else near))]
        forward("y" if kind == 1 else "x", half, 3 if kind == 1 else 2, part)
        to_core(kind, part)

    def diagonal(kind, part):
        sent(view(kind, part), plane_recv.at[kind - 1, part])
        to_core(kind, part)

    for part in range(PLANES):
        start(part)
        yield
    for step in range(PLANES + 1):
        for stage, kind, lag in ((side, 1, 0), (side, 2, 0), (diagonal, 3, 1), (diagonal, 4, 1)):
            if 0 <= step - lag < PLANES:
                stage(kind, step - lag)
                yield
    for part in range(PLANES):
        for kind in range(5):
            sent(view(kind, part, 1 - core), core_recv.at[kind, part])
    yield
    for part in range(PLANES):
        for kind in range(5):
            sent(view(kind, part), core_send.at[kind, part])
        for number, kind in enumerate((0, 0, 3, 4)):
            sent(view(kind, part), plane_send.at[number, part])
    yield


def plane_scatter_scratch(one):
    near, far = half_shapes(one)
    single = pltpu.VMEM(one, LOW)
    buffers = [pltpu.VMEM((4, *one), LOW), pltpu.VMEM(near, LOW), pltpu.VMEM(far, LOW), single, single]
    return buffers + [dma_grid(4), dma_grid(4), dma_grid(4), dma_grid(4)]


def plane_scatter_steps(place, parts, total, rows, scratch):
    mine, diagonal_x, diagonal_y, by_x, by_y, plane_send, plane_recv, core_send, core_recv = scratch
    near, far = halves(parts.shape)
    core = place.core

    def forward(name, source, target, number):
        send(source, target, plane_send.at[number], plane_recv.at[number], place.targets[name])

    def from_core(kind):
        sent(mine.at[kind], core_recv.at[kind])

    def own(kind):
        return parts[place.chip(kind) * 2 + core]

    for kind in (3, 1, 2, 0):
        source = parts.at[place.chip(kind) * 2 + 1 - core]
        send(source, mine.at[kind], core_send.at[kind], core_recv.at[kind], place.targets["core"])
    yield
    from_core(3)
    mine[3] += own(3)
    forward("x", mine.at[(3, *near)], diagonal_x, 0)
    forward("y", mine.at[(3, *far)], diagonal_y, 1)
    yield
    from_core(1)
    mine[1] += own(1)
    sent(diagonal_y, plane_recv.at[1])
    mine[(1, *far)] += diagonal_y[...]
    forward("x", mine.at[1], by_x, 2)
    yield
    from_core(2)
    mine[2] += own(2)
    sent(diagonal_x, plane_recv.at[0])
    mine[(2, *near)] += diagonal_x[...]
    forward("y", mine.at[2], by_y, 3)
    yield
    from_core(0)
    here = own(0).astype(WIDE) + mine[0].astype(WIDE)
    sent(by_x, plane_recv.at[2])
    sent(by_y, plane_recv.at[3])
    total[rows] = here + (by_x[...].astype(WIDE) + by_y[...].astype(WIDE))
    yield
    for kind in range(4):
        sent(mine.at[kind], core_send.at[kind])
    for number, part in enumerate((diagonal_x, diagonal_y, by_x, by_y)):
        sent(part, plane_send.at[number])
    yield


def run_in_order(runs, order):
    for place in order:
        next(runs[place])
    assert all(next(run, "end") == "end" for run in runs)


def run_together(runs):
    runs = list(runs)
    while runs:
        for run in list(runs):
            if run in runs and next(run, "end") == "end":
                runs = [other for other in runs if other is not run]


IN_ROW, OUT_ROW, PROJ_ROW, VECTOR_ROW = 0, 64, 128, 64


def weight(slabs, row, height=16):
    part = slabs[:, row : row + height, :]
    return part.reshape(part.shape[0] * height, part.shape[2])


def vectors_of(slabs, row=VECTOR_ROW):
    return jnp.sum(slabs[:, row : row + 16, :].astype(WIDE), 0)


def pick_matrix(rows, columns, step, kind=LOW):
    row = lax.broadcasted_iota(jnp.int32, (rows, columns), 0)
    column = lax.broadcasted_iota(jnp.int32, (rows, columns), 1)
    return ((column >= row * step) & (column < (row + 1) * step)).astype(kind)


def every_slot(by_entry, slots):
    return jnp.concatenate([by_entry] * slots, 0)


def dot_wide(left, right, dims):
    return lax.dot_general(
        left, right, ((dims[:1], dims[1:]), ((), ())), precision=lax.Precision.HIGHEST, preferred_element_type=WIDE
    )


def normalize(values):
    center = values - jnp.mean(values, -1, keepdims=True)
    scale = lax.rsqrt(jnp.mean(center * center, -1, keepdims=True) + EPSILON)
    return center * scale, scale


def normalize_back(grad, gain, unit, scale):
    inner = grad * gain
    back = inner - jnp.mean(inner, -1, keepdims=True) - unit * jnp.mean(inner * unit, -1, keepdims=True)
    return back * scale, jnp.sum(grad * unit, 0, keepdims=True), jnp.sum(grad, 0, keepdims=True)


GELU_A, GELU_B = (2.0 / 3.141592653589793) ** 0.5, 0.044715


def gelu_tanh(values):
    return jnp.tanh(GELU_A * (values + GELU_B * values * values * values))


def head_matrix(width):
    return pick_matrix(128, width, width // HYP_HEADS)


def lengths_column(row):
    shape = (row.shape[1], row.shape[1])
    same = lax.broadcasted_iota(jnp.int32, shape, 0) == lax.broadcasted_iota(jnp.int32, shape, 1)
    return jnp.sum(jnp.where(same, row.astype(WIDE), 0.0), 1, keepdims=True)


def hyper_forward_kernel(dense, rest, rows_ref, lengths_ref, *refs):
    hyper_forward_body(dense, rest, rows_ref, lengths_column(lengths_ref[...]), *refs)


def hyper_forward_body(
    dense, rest, rows_ref, lengths, pooled_ref, normed_ref, query_ref, key_ref, value_ref, probs_ref, heads_ref, resid_ref, pre_ref
):
    count, width = rows_ref.shape
    entries = pooled_ref.shape[0]
    slots = count // entries
    vectors = vectors_of(rest)
    slot_rows = rows_ref[...]
    unit, _ = normalize(slot_rows)
    normed = (unit * vectors[0:1] + vectors[2:3]).astype(LOW)
    normed_ref[...] = normed
    query = dot(normed[:entries], weight(rest, 0), (1, 0)).astype(LOW)
    key = dot(normed, weight(rest, 16), (1, 0)).astype(LOW)
    value = dot(normed, weight(rest, 32), (1, 0)).astype(LOW)
    query_ref[...], key_ref[...], value_ref[...] = query, key, value
    heads = head_matrix(width)
    product = every_slot(query.astype(WIDE), slots) * key.astype(WIDE)
    scores = dot_wide(product, heads.astype(WIDE), (1, 1)) * (width // HYP_HEADS) ** (-0.5)
    lengths = every_slot(jnp.broadcast_to(lengths, (entries, 128)), slots).reshape(slots, entries, 128)
    slot = lax.broadcasted_iota(jnp.int32, (slots, entries, 128), 0).astype(WIDE)
    scores = jnp.where(slot < lengths, scores.reshape(slots, entries, 128), MASKED)
    grown = jnp.exp(scores - jnp.max(scores, 0, keepdims=True))
    probs = (grown / jnp.sum(grown, 0, keepdims=True)).reshape(count, 128)
    probs_ref[...] = probs
    weighted = dot(probs.astype(LOW), heads, (1, 0)) * value.astype(WIDE)
    heads_out = jnp.sum(weighted.reshape(slots, entries, width), 0).astype(LOW)
    heads_ref[...] = heads_out
    residual = slot_rows[:entries] + dot(heads_out, weight(rest, 48), (1, 0))
    resid_ref[...] = residual
    unit, _ = normalize(residual)
    normed_two = (unit * vectors[1:2] + vectors[3:4]).astype(LOW)
    out = residual + vectors[4:5]
    out_weight = weight(dense, OUT_ROW, 64)
    for turn in range(4):
        pre = dot(normed_two, weight(dense, IN_ROW + 16 * turn), (1, 0)) + vectors[5 + turn : 6 + turn]
        pre_ref[turn] = pre
        act = (0.5 * pre * (1.0 + gelu_tanh(pre))).astype(LOW)
        out += dot(act, out_weight[turn * width : (turn + 1) * width], (1, 0))
    pooled_ref[...] = out.astype(LOW)


def forward_shapes(entries, count, width):
    shapes = [
        ((entries, width), LOW),
        ((count, width), LOW),
        ((entries, width), LOW),
        ((count, width), LOW),
        ((count, width), LOW),
        ((count, 128), WIDE),
        ((entries, width), LOW),
        ((entries, width), WIDE),
        ((4, entries, width), WIDE),
    ]
    return [jax.ShapeDtypeStruct(shape, kind) for shape, kind in shapes]


def hyper_forward(dense, rest, slot_rows, lengths, entries):
    return pl.pallas_call(
        hyper_forward_kernel,
        out_shape=forward_shapes(entries, *slot_rows.shape),
        compiler_params=pltpu.CompilerParams(vmem_limit_bytes=VMEM_LIMIT),
        name="hyper_forward",
    )(dense, rest, slot_rows, lengths)


def project_rows(pooled, proj, vectors, gain, rows_ref, normed_ref):
    width = pooled.shape[1]
    square = 0.0
    for turn in range(4):
        columns = slice(turn * width, (turn + 1) * width)
        rows = dot(pooled, weight(proj, PROJ_ROW + 16 * turn), (1, 0)) + vectors[9 + turn : 10 + turn]
        rows = rows.astype(LOW)
        rows_ref[:, columns] = rows
        rows = rows.astype(WIDE)
        square += jnp.sum(rows * rows, -1, keepdims=True)
    scale = lax.rsqrt(square / (4 * width) + EPSILON)
    normed_ref[...] = (rows_ref[...].astype(WIDE) * scale * gain.astype(WIDE)).astype(LOW)


def project_kernel(pooled_ref, dense_ref, rest_ref, gain_ref, rows_ref, normed_ref):
    project_rows(pooled_ref[...], dense_ref, vectors_of(rest_ref), gain_ref[0:1], rows_ref, normed_ref)


def project(pooled, dense, rest, gain):
    entries, width = pooled.shape
    block = min(entries, 512)
    out_block = pl.BlockSpec((block, 4 * width), lambda i: (i, 0))
    result = jax.ShapeDtypeStruct((entries, 4 * width), LOW)
    in_vmem = pl.BlockSpec(memory_space=pltpu.VMEM)
    return pl.pallas_call(
        project_kernel,
        grid=(entries // block,),
        in_specs=[pl.BlockSpec((block, width), lambda i: (i, 0)), in_vmem, in_vmem, in_vmem],
        out_specs=[out_block, out_block],
        out_shape=[result, result],
        compiler_params=pltpu.CompilerParams(vmem_limit_bytes=VMEM_LIMIT),
        name="project",
    )(pooled, dense, rest, gain)


def pick_tokens(entries, core, own_ids, got_ids):
    left = jnp.where(core == 0, own_ids, got_ids)
    right = jnp.where(core == 0, got_ids, own_ids)
    entry = lax.broadcasted_iota(jnp.int32, (entries, own_ids.shape[1]), 0)
    return jnp.concatenate([(entry == left).astype(LOW), (entry == right).astype(LOW)], 1)


def first_kernel(
    gains_ref, biases_ref, attn_ref, in_ref, in_bias_ref, out_ref, proj_ref, proj_bias_ref, ids_ref, table_ref, lengths_ref, gain_ref,
    own_ids_ref, got_ids_ref, dy_ref, down_ref, query_ref, kv_ref,
    dense_out, rest_out, column_out, d_act_out, rows_out, inputs_out, qkv_out,
    dense, rest, dense_share, rest_share, parts, slot_rows, pooled_ref, normed_ref, q_ref, k_ref, v_ref, probs_ref, heads_ref, resid_ref, pre_ref,
    column_all, pooled_all, dy_all, down_buffer, act_buffer, query_weight, kv_weight, rows, normed, inputs,
    qkv, load_sems, down_sems, act_sems, out_sems, dy_send, dy_recv, *refs
):
    place = Place()
    own = lax.axis_index("dp") * 2 + place.core
    width = dense.shape[2]

    def load(source, target, number):
        copy = pltpu.make_async_copy(source, target, load_sems.at[number])
        copy.start()
        return copy

    units = down_ref.shape[0]

    def load_down(step):
        here = pl.ds(step * UNIT_BLOCK, UNIT_BLOCK)
        copy = pltpu.make_async_copy(down_ref.at[here], down_buffer.at[step % 2], down_sems.at[step % 2])
        copy.start()
        return copy

    own_dy = load(dy_ref, dy_all.at[0], 0)
    down_copy = load_down(0)
    weight_loads = [load(query_ref, query_weight, 1), load(kv_ref, kv_weight, 2)]

    rest_share[0:64] = attn_ref[...].reshape(64, width)
    for turn in range(4):
        columns = slice(turn * width, (turn + 1) * width)
        dense_share[IN_ROW + 16 * turn : IN_ROW + 16 * turn + 16] = in_ref[:, columns]
        dense_share[PROJ_ROW + 16 * turn : PROJ_ROW + 16 * turn + 16] = proj_ref[:, columns]
    dense_share[OUT_ROW : OUT_ROW + 64] = out_ref[...]

    def spread(values, length):
        count = values.shape[1]
        row = lax.broadcasted_iota(jnp.int32, (count, length), 0)
        lane = lax.broadcasted_iota(jnp.int32, (count, length), 1)
        return dot(values, (lane - own * count == row).astype(LOW), (1, 0))

    def by_rows(flat):
        return [flat[:, turn * width : (turn + 1) * width] for turn in range(4)]

    vectors = [spread(gains_ref[...], width), spread(biases_ref[...], width)]
    vectors += by_rows(spread(in_bias_ref[...], 4 * width)) + by_rows(spread(proj_bias_ref[...], 4 * width))
    vectors.append(jnp.zeros((3, width), WIDE))
    rest_share[VECTOR_ROW : VECTOR_ROW + 16] = jnp.concatenate(vectors, 0).astype(LOW)

    place.greet()
    send(dy_ref, dy_all.at[1], dy_send, dy_recv, place.targets["core"])
    dense_sems, rest_sems, small_sems, line_sems, slot_scratch = refs[:5], refs[5:12], refs[12:18], refs[18:20], refs[20:]
    pieces = table_ref.shape[0]
    groups, height = parts.shape[0], parts.shape[1] // ids_ref.shape[0]
    chunk = ids_ref.shape[1]

    def slot_steps():
        across = lax.broadcasted_iota(jnp.int32, (chunk, chunk), 1)
        down = lax.broadcasted_iota(jnp.int32, (chunk, chunk), 0)
        piece = lax.broadcasted_iota(jnp.int32, (chunk, pieces), 1).astype(WIDE) + (own * pieces).astype(WIDE)
        for turn in range(ids_ref.shape[0]):
            ids = ids_ref[turn : turn + 1].astype(WIDE)
            column = jnp.sum(jnp.where(across == down, ids, 0.0), 1, keepdims=True)
            found = dot((piece == column).astype(LOW), table_ref[...], (1, 0)).astype(LOW)
            parts[:, turn * height : (turn + 1) * height, :] = found.reshape(groups, height, width)
            yield
        yield from scatter_steps(place, parts, slot_rows, slot_scratch)

    def act_steps():
        nonlocal down_copy
        own_dy.wait()
        sent(dy_all.at[1], dy_recv)
        copies = []
        for step in range(units // UNIT_BLOCK):
            down_copy.wait()
            if (step + 1) * UNIT_BLOCK < units:
                down_copy = load_down(step + 1)
            if step >= 2:
                copies[step - 2].wait()
            tokens = dy_all[...].reshape(-1, dy_all.shape[2])
            act_buffer[step % 2] = dot(tokens, down_buffer[step % 2], (1, 1)).astype(LOW)
            here = pl.ds(step * UNIT_BLOCK, UNIT_BLOCK)
            copy = pltpu.make_async_copy(act_buffer.at[step % 2], d_act_out.at[:, here], act_sems.at[step % 2])
            copy.start()
            copies.append(copy)
            if len(copies) * UNIT_BLOCK == units:
                copies[-2].wait()
                copies[-1].wait()
                sent(dy_ref, dy_send)
            yield

    runs = [
        gather_steps(place, dense_share, dense, dense_sems),
        late_gather_steps(place, rest_share, rest, rest_sems),
        slot_steps(),
        act_steps(),
    ]
    run_in_order(runs, FIRST_ORDER)

    def store(source, target, number):
        copy = pltpu.make_async_copy(source, target, out_sems.at[number])
        copy.start()
        return copy

    stores = [store(dense, dense_out, 0), store(rest, rest_out, 1)]
    hyper_forward_body(
        dense, rest, slot_rows, lengths_column(lengths_ref[...]), pooled_ref, normed_ref, q_ref, k_ref, v_ref, probs_ref, heads_ref, resid_ref, pre_ref
    )
    small_gather(place, pooled_ref[...], pooled_all, small_sems)
    slot_count = parts.shape[1]
    column_all[place.z, :slot_count] = slot_rows[...].astype(LOW)
    lane = lax.broadcasted_iota(jnp.int32, (lengths_ref.shape[1], width), 1)
    row = lax.broadcasted_iota(jnp.int32, (lengths_ref.shape[1], width), 0)
    spread_lengths = dot(lengths_ref[...].astype(WIDE).astype(LOW), (lane == row).astype(LOW), (1, 0))
    column_all[place.z, slot_count:] = jnp.broadcast_to(spread_lengths, (16, width)).astype(LOW)
    column_run = line_share_steps(place, column_all, line_sems)
    next(column_run)
    pooled = pooled_all[...].reshape(-1, width)
    project_rows(pooled, dense, vectors_of(rest), gain_ref[0:1], rows, normed)
    stores.append(store(rows, rows_out, 2))

    entries = rows.shape[0]
    kv_width = HEAD_DIM * (KV_HEADS // 2)
    kv_columns = pl.ds(pl.multiple_of(place.core * kv_width, kv_width), kv_width)
    local = own_ids_ref.shape[1]
    pick = pick_tokens(entries, place.core, own_ids_ref[...], got_ids_ref[...])
    q_width = query_weight.shape[1]
    for copy in weight_loads:
        copy.wait()
    for start in range(0, q_width, 256):
        found = dot(normed[...], query_weight[:, start : start + 256], (1, 0)).T.astype(LOW)
        qkv[start : start + 256] = dot(found, pick, (1, 0)).astype(LOW)
    for which in range(2):
        start = q_width + which * kv_width
        found = dot(normed[...], kv_weight[which, :, kv_columns], (1, 0)).T.astype(LOW)
        qkv[start : start + kv_width] = dot(found, pick, (1, 0)).astype(LOW)
    stores.append(store(qkv, qkv_out, 3))
    own_pick = (lax.broadcasted_iota(jnp.int32, (entries, local), 0) == own_ids_ref[...]).astype(LOW)
    inputs[...] = dot(own_pick, rows[...], (0, 0)).astype(LOW)
    stores.append(store(inputs, inputs_out, 4))
    next(column_run)
    stores.append(store(column_all, column_out, 5))
    for copy in stores:
        copy.wait()


def first_exchange(weights, ids, table, lengths, gains, own_ids, got_ids, dy, down, query, kv, number):
    devices = 8 * PLANES
    width = table.shape[1]
    slots = ids.size // devices
    entries = lengths.shape[1]
    local, d_model = dy.shape
    seq_len = 2 * local
    features = query.shape[1] + kv.shape[2]
    units = down.shape[0]
    one = (slots, width)
    in_vmem, anywhere = pl.BlockSpec(memory_space=pltpu.VMEM), pl.BlockSpec(memory_space=pl.ANY)
    all_rows = devices * entries
    dense, rest = (devices, DENSE_ROWS, width), (devices, REST_ROWS, width)
    kept = forward_shapes(entries, slots, width)
    column = (PLANES, slots + 16, width)
    dma = pltpu.SemaphoreType.DMA
    return pl.pallas_call(
        first_kernel,
        in_specs=[in_vmem] * 14 + [anywhere] * 4,
        out_specs=[anywhere] * 7,
        out_shape=[
            jax.ShapeDtypeStruct(dense, LOW),
            jax.ShapeDtypeStruct(rest, LOW),
            jax.ShapeDtypeStruct(column, LOW),
            jax.ShapeDtypeStruct((2 * local, units), LOW),
            jax.ShapeDtypeStruct((all_rows, d_model), LOW),
            jax.ShapeDtypeStruct((local, d_model), LOW),
            jax.ShapeDtypeStruct((features, seq_len), LOW),
        ],
        scratch_shapes=[
            pltpu.VMEM(dense, LOW),
            pltpu.VMEM(rest, LOW),
            pltpu.VMEM(dense[1:], LOW),
            pltpu.VMEM(rest[1:], LOW),
            pltpu.VMEM((devices, *one), LOW),
            pltpu.VMEM(one, WIDE),
        ]
        + [pltpu.VMEM(array.shape, array.dtype) for array in kept]
        + [
            pltpu.VMEM(column, LOW),
            pltpu.VMEM((PLANES, 4, 2, entries, width), LOW),
            pltpu.VMEM((2, local, d_model), LOW),
            pltpu.VMEM((2, UNIT_BLOCK, d_model), LOW),
            pltpu.VMEM((2, 2 * local, UNIT_BLOCK), LOW),
            pltpu.VMEM(query.shape, LOW),
            pltpu.VMEM(kv.shape, LOW),
            pltpu.VMEM((all_rows, d_model), LOW),
            pltpu.VMEM((all_rows, d_model), LOW),
            pltpu.VMEM((local, d_model), LOW),
            pltpu.VMEM((features, seq_len), LOW),
            dma((3,)),
            dma((2,)),
            dma((2,)),
            dma((6,)),
            dma,
            dma,
        ]
        + gather_sems()
        + late_gather_sems()
        + small_gather_sems()
        + line_share_sems()
        + scatter_scratch(one),
        compiler_params=pltpu.CompilerParams(
            collective_id=number, has_side_effects=True, vmem_limit_bytes=VMEM_LIMIT
        ),
        name="first_exchange",
    )(*weights, ids, table, lengths, gains, own_ids, got_ids, dy, down, query, kv)


def greet_core(place):
    barrier = pltpu.get_barrier_semaphore()
    pl.semaphore_signal(barrier, inc=1, device_id=place.targets["core"], device_id_type=pl.DeviceIdType.MESH)
    pl.semaphore_wait(barrier, 1)


def started(source, target, sem):
    copy = pltpu.make_async_copy(source, target, sem)
    copy.start()
    return copy


def middle_kernel(
    own_hbm, other_hbm, weight_hbm, inputs_hbm, gains_ref, hidden_hbm, x_own_hbm, x_other_hbm, own, other, weight, inputs, partial, got, hidden,
    x_own, x_got, load_sems, tile_sems, send_sems, recv_sems, row_send_sems, row_recv_sems, out_sems
):
    place = Place()
    tokens, width = inputs.shape
    tiles = [slice(start, start + width // 4) for start in range(0, width, width // 4)]
    blocks = [slice(start, start + tokens // 4) for start in range(0, tokens, tokens // 4)]
    load_other = started(other_hbm, other, load_sems.at[0])
    weights = [started(weight_hbm.at[:, tile], weight.at[:, tile], tile_sems.at[n]) for n, tile in enumerate(tiles)]
    loads = [started(own_hbm, own, load_sems.at[1]), started(inputs_hbm, inputs, load_sems.at[2])]
    greet_core(place)
    target = place.targets["core"]
    load_other.wait()
    for number, tile in enumerate(tiles):
        weights[number].wait()
        partial[:, tile] = dot(other[...], weight[:, tile], (0, 0)).astype(LOW)
        send(partial.at[:, tile], got.at[:, tile], send_sems.at[number], recv_sems.at[number], target)
    for copy in loads:
        copy.wait()
    gain = gains_ref[1:2].astype(WIDE)
    stores = []
    for number, rows in enumerate(blocks):
        here = dot(own[:, rows], weight[...], (0, 0)) + inputs[rows].astype(WIDE)
        if number == 0:
            for turn, tile in enumerate(tiles):
                sent(got.at[:, tile], recv_sems.at[turn])
        here += got[rows].astype(WIDE)
        hidden[rows] = here
        stores.append(started(hidden.at[rows], hidden_hbm.at[rows], out_sems.at[0, number]))
        x_own[rows] = (here * lax.rsqrt(jnp.mean(here * here, -1, keepdims=True) + EPSILON) * gain).astype(LOW)
        send(x_own.at[rows], x_got.at[rows], row_send_sems.at[number], row_recv_sems.at[number], target)
        stores.append(started(x_own.at[rows], x_own_hbm.at[rows], out_sems.at[1, number]))
    for number, rows in enumerate(blocks):
        sent(x_got.at[rows], row_recv_sems.at[number])
        stores.append(started(x_got.at[rows], x_other_hbm.at[rows], out_sems.at[2, number]))
    for copy in stores:
        copy.wait()
    for number in range(4):
        sent(partial.at[:, tiles[number]], send_sems.at[number])
        sent(x_own.at[blocks[number]], row_send_sems.at[number])


def middle(heads_own, heads_other, weight, inputs, gains, number):
    in_vmem, anywhere = pl.BlockSpec(memory_space=pltpu.VMEM), pl.BlockSpec(memory_space=pl.ANY)
    tokens = pltpu.VMEM(inputs.shape, LOW)
    low = jax.ShapeDtypeStruct(inputs.shape, LOW)
    return pl.pallas_call(
        middle_kernel,
        in_specs=[anywhere] * 4 + [in_vmem],
        out_specs=[anywhere] * 3,
        out_shape=[jax.ShapeDtypeStruct(inputs.shape, WIDE), low, low],
        scratch_shapes=[
            pltpu.VMEM(heads_own.shape, LOW),
            pltpu.VMEM(heads_own.shape, LOW),
            pltpu.VMEM(weight.shape, LOW),
            tokens,
            tokens,
            tokens,
            pltpu.VMEM(inputs.shape, WIDE),
            tokens,
            tokens,
            dma_grid(3),
            dma_grid(4),
            dma_grid(4),
            dma_grid(4),
            dma_grid(4),
            dma_grid(4),
            dma_grid(3, 4),
        ],
        compiler_params=pltpu.CompilerParams(
            collective_id=number, has_side_effects=True, vmem_limit_bytes=VMEM_LIMIT
        ),
        name="middle",
    )(heads_own, heads_other, weight, inputs, gains)


def turn_kernel(
    hidden_hbm, dy_hbm, back_own_hbm, back_got_hbm, weight_hbm, gains_ref, grad_hbm, heads_own_hbm, heads_other_hbm, hidden, loaded, grad, got,
    weight, heads, load_sems, weight_sem, send_sems, recv_sems, out_sems
):
    place = Place()
    tokens, width = grad.shape
    count = hidden.shape[0]
    blocks = [slice(n * hidden.shape[1], (n + 1) * hidden.shape[1]) for n in range(count)]
    sources = (dy_hbm, back_own_hbm, back_got_hbm)
    loads = []
    for number, rows in enumerate(blocks):
        loads.append(
            [started(hidden_hbm.at[rows], hidden.at[number], load_sems.at[number, 3])]
            + [started(source.at[rows], loaded.at[number, n], load_sems.at[number, n]) for n, source in enumerate(sources)]
        )
        if number == 1:
            load_weight = started(weight_hbm, weight, weight_sem)
    greet_core(place)
    target = place.targets["core"]
    gain = gains_ref[1:2].astype(WIDE)
    half = tokens // 2
    for number, rows in enumerate(blocks):
        for copy in loads[number]:
            copy.wait()
        here = hidden[number]
        dy, back_own, back_got = (loaded[number, n].astype(WIDE) for n in range(3))
        scale = lax.rsqrt(jnp.mean(here * here, -1, keepdims=True) + EPSILON)
        inner = (back_own + back_got) * gain
        back = scale * inner - here * (scale * scale * scale * jnp.mean(here * inner, -1, keepdims=True))
        grad[rows] = (dy + back).astype(LOW)
        send(grad.at[rows], got.at[rows], send_sems.at[number], recv_sems.at[number], target)
    load_weight.wait()
    stores = [started(grad, grad_hbm, out_sems.at[0])]
    heads[0, :, :half] = dot(weight[...], grad[:half], (1, 1)).astype(LOW)
    heads[0, :, half:] = dot(weight[...], grad[half:], (1, 1)).astype(LOW)
    stores.append(started(heads.at[0], heads_own_hbm, out_sems.at[1]))
    for part in range(2):
        for number in range(part * count // 2, (part + 1) * count // 2):
            sent(got.at[blocks[number]], recv_sems.at[number])
        rows = slice(part * half, (part + 1) * half)
        heads[1, :, rows] = dot(weight[...], got[rows], (1, 1)).astype(LOW)
    stores.append(started(heads.at[1], heads_other_hbm, out_sems.at[2]))
    for copy in stores:
        copy.wait()
    for number, rows in enumerate(blocks):
        sent(grad.at[rows], send_sems.at[number])


def turn_around(hidden, dy, backs, weight, gains, number):
    in_vmem, anywhere = pl.BlockSpec(memory_space=pltpu.VMEM), pl.BlockSpec(memory_space=pl.ANY)
    tokens, width = dy.shape
    count = 4
    block = tokens // count
    heads = (weight.shape[0], tokens)
    return pl.pallas_call(
        turn_kernel,
        in_specs=[anywhere] * 5 + [in_vmem],
        out_specs=[anywhere] * 3,
        out_shape=[
            jax.ShapeDtypeStruct(dy.shape, LOW),
            jax.ShapeDtypeStruct(heads, LOW),
            jax.ShapeDtypeStruct(heads, LOW),
        ],
        scratch_shapes=[
            pltpu.VMEM((count, block, width), WIDE),
            pltpu.VMEM((count, 3, block, width), LOW),
            pltpu.VMEM(dy.shape, LOW),
            pltpu.VMEM(dy.shape, LOW),
            pltpu.VMEM(weight.shape, LOW),
            pltpu.VMEM((2, *heads), LOW),
            dma_grid(count, 4),
            pltpu.SemaphoreType.DMA,
            dma_grid(count),
            dma_grid(count),
            dma_grid(3),
        ],
        compiler_params=pltpu.CompilerParams(
            collective_id=number, has_side_effects=True, vmem_limit_bytes=VMEM_LIMIT
        ),
        name="turn_around",
    )(hidden, dy, *backs, weight, gains)


def outer(left, right):
    return dot(left, right, (0, 0))


def column_sum(values):
    return jnp.sum(values.astype(WIDE), 0, keepdims=True)


def own_part(ref, own, rows=slice(None)):
    if own is None:
        return ref[rows]
    size = ref.shape[1] // PLANES
    return ref[rows, pl.ds(pl.multiple_of(own * size, size), size)]


def back_dense(dense, vectors, rows_low, pooled_ref, residual, pre_ref, normed_ref, act_ref, put, own=None):
    width = pooled_ref.shape[1]
    d_pooled, proj_bias = 0.0, []
    for turn in range(4):
        rows = rows_low[:, turn * width : (turn + 1) * width]
        put(True, PROJ_ROW + 16 * turn, outer(own_part(pooled_ref, own), rows))
        d_pooled += dot(rows, weight(dense, PROJ_ROW + 16 * turn), (1, 1))
        proj_bias.append(column_sum(rows))
    ffn_low = d_pooled.astype(LOW)
    unit, scale = normalize(residual)
    normed_ref[...] = (unit * vectors[1:2] + vectors[3:4]).astype(LOW)
    out_weight = weight(dense, OUT_ROW, 64)
    d_normed, ffn_bias = 0.0, []
    for turn in range(4):
        pre = pre_ref[turn]
        bent = gelu_tanh(pre)
        act_ref[turn] = (0.5 * pre * (1.0 + bent)).astype(LOW)
        slope = 0.5 * (1.0 + bent) + 0.5 * pre * (1.0 - bent * bent) * GELU_A * (1.0 + 3.0 * GELU_B * pre * pre)
        d_act = dot(ffn_low, out_weight[turn * width : (turn + 1) * width], (1, 1))
        pre_low = (d_act * slope).astype(LOW)
        put(True, IN_ROW + 16 * turn, outer(own_part(normed_ref, own), pre_low))
        ffn_bias.append(column_sum(pre_low))
        d_normed += dot(pre_low, weight(dense, IN_ROW + 16 * turn), (1, 1))
    if own is None:
        put(True, OUT_ROW, jnp.concatenate([outer(act_ref[turn], ffn_low).astype(LOW) for turn in range(4)], 0), 64)
    else:
        put(True, OUT_ROW, outer(act_ref[own], ffn_low), 64)
    back, gain, bias = normalize_back(d_normed, vectors[1:2], unit, scale)
    return d_pooled + back, gain, bias, [column_sum(ffn_low)] + ffn_bias + proj_bias


def first_slot_plus(by_slot, by_entry):
    entries = by_entry.shape[0]
    return jnp.concatenate([by_slot[:entries] + by_entry, by_slot[entries:]], 0)


def back_attention(rest, vectors, d_resid, slot_rows, saved, put, own=None):
    normed_ref, query_ref, key_ref, value_ref, probs_ref, heads_ref = saved
    count, width = slot_rows.shape
    entries = query_ref.shape[0]
    slots = count // entries
    scale = (width // HYP_HEADS) ** (-0.5)
    attn_low = d_resid.astype(LOW)
    put(False, 48, outer(own_part(heads_ref, own), attn_low))
    d_heads = dot(attn_low, weight(rest, 48), (1, 1)).astype(LOW)
    heads = head_matrix(width)
    d_heads_all = every_slot(d_heads.astype(WIDE), slots)
    query_all = every_slot(query_ref[...].astype(WIDE), slots)
    probs = probs_ref[...]
    d_probs = dot_wide(d_heads_all * value_ref[...].astype(WIDE), heads.astype(WIDE), (1, 1))
    delta = every_slot(jnp.sum((probs * d_probs).reshape(slots, entries, 128), 0), slots)
    d_scores = dot((probs * (d_probs - delta) * scale).astype(LOW), heads, (1, 0))
    d_value = (dot(probs.astype(LOW), heads, (1, 0)) * d_heads_all).astype(LOW)
    d_key = (d_scores * query_all).astype(LOW)
    d_query = (d_scores * key_ref[...].astype(WIDE)).reshape(slots, entries, width)
    d_query = jnp.sum(d_query, 0).astype(LOW)
    put(False, 0, outer(own_part(normed_ref, own, slice(0, entries)), d_query))
    put(False, 16, outer(own_part(normed_ref, own), d_key))
    put(False, 32, outer(own_part(normed_ref, own), d_value))
    d_normed = dot(d_key, weight(rest, 16), (1, 1)) + dot(d_value, weight(rest, 32), (1, 1))
    d_normed = first_slot_plus(d_normed, dot(d_query, weight(rest, 0), (1, 1)))
    unit, inverse = normalize(slot_rows)
    back, gain, bias = normalize_back(d_normed, vectors[0:1], unit, inverse)
    return first_slot_plus(back, d_resid).astype(LOW), gain, bias


def vector_rows(gain_one, gain_two, bias_one, bias_two, rest):
    rows = [gain_one, gain_two, bias_one, bias_two] + rest
    rows.append(jnp.zeros((16 - len(rows), gain_one.shape[1]), WIDE))
    return jnp.concatenate(rows, 0).astype(LOW)


def hyper_backward_kernel(
    dense, rest, row_grad_ref, rows_ref, pooled_ref, normed_ref, query_ref, key_ref, value_ref, probs_ref, heads_ref, resid_ref, pre_ref,
    dense_grad, rest_grad, slot_ref, normed_two_ref, act_ref
):
    vectors = vectors_of(rest)
    put = putter(dense_grad, rest_grad)
    d_resid, gain_two, bias_two, sums = back_dense(
        dense, vectors, row_grad_ref[...].astype(LOW), pooled_ref, resid_ref[...], pre_ref, normed_two_ref, act_ref, put
    )
    saved = (normed_ref, query_ref, key_ref, value_ref, probs_ref, heads_ref)
    slot_ref[...], gain_one, bias_one = back_attention(rest, vectors, d_resid, rows_ref[...], saved, put)
    put_vectors(rest_grad, vector_rows(gain_one, gain_two, bias_one, bias_two, sums))


def putter(dense_grad, rest_grad):
    def put(in_dense, row, grad, height=16):
        target = dense_grad if in_dense else rest_grad
        target[:, row : row + height, :] = grad.astype(LOW).reshape(target.shape[0], height, target.shape[2])

    return put


def put_vectors(rest_grad, sums):
    rest_grad[:, VECTOR_ROW : VECTOR_ROW + 16, :] = jnp.broadcast_to(sums[None], (rest_grad.shape[0], *sums.shape))


def hyper_backward(dense, rest, row_grad, slot_rows, saved):
    return pl.pallas_call(
        hyper_backward_kernel,
        out_shape=[jax.ShapeDtypeStruct(like.shape, LOW) for like in (dense, rest, slot_rows)],
        scratch_shapes=[pltpu.VMEM(saved[0].shape, LOW), pltpu.VMEM((4, *saved[0].shape), LOW)],
        compiler_params=pltpu.CompilerParams(vmem_limit_bytes=VMEM_LIMIT),
        name="hyper_backward",
    )(dense, rest, row_grad, slot_rows, *saved)


def row_part_steps(place, hbm_refs, refs, ids_refs, gains_ref, weights, row_parts, sems):
    dq_ref, dk_ref, dv_ref, grad_ref, rows_ref, sums_ref = refs
    dq_hbm, dk_hbm, dv_hbm, query_hbm, kv_hbm, grad_hbm, rows_hbm = hbm_refs
    own_ids, got_ids = ids_refs[0][...], ids_refs[1][...]
    entries, d_model = rows_ref.shape
    q_width, kv_width = dq_ref.shape[0], dk_ref.shape[0]
    width = weights.shape[2]
    height = d_model // weights.shape[0]
    kv_columns = pl.ds(pl.multiple_of(place.core * kv_width, kv_width), kv_width)
    copies = [
        started(source, target, sems.at[number])
        for number, (source, target) in enumerate(
            (
                (dq_hbm, dq_ref),
                (dk_hbm, dk_ref),
                (dv_hbm, dv_ref),
                (query_hbm.at[:, :, :width], weights.at[:, 0:height, :]),
                (query_hbm.at[:, :, width:], weights.at[:, height : 2 * height, :]),
                (kv_hbm.at[0, :, :, kv_columns], weights.at[:, 2 * height : 3 * height, 0:kv_width]),
                (kv_hbm.at[1, :, :, kv_columns], weights.at[:, 2 * height : 3 * height, kv_width : 2 * kv_width]),
                (rows_hbm, rows_ref),
                (grad_hbm, grad_ref),
            )
        )
    ]
    yield
    pick = pick_tokens(entries, place.core, own_ids, got_ids)
    for copy in copies[:3]:
        copy.wait()
    sums_ref[:, :q_width] = dot(pick, dq_ref[...], (1, 1)).astype(LOW)
    sums_ref[:, q_width : q_width + kv_width] = dot(pick, dk_ref[...], (1, 1)).astype(LOW)
    sums_ref[:, q_width + kv_width :] = dot(pick, dv_ref[...], (1, 1)).astype(LOW)
    for copy in copies[3:]:
        copy.wait()
    gain = gains_ref[0:1].astype(WIDE)
    block = entries // 2
    group = row_parts.shape[0] // 2
    upper = lax.div(place.z, PLANES // 2)
    for number in (1 - upper, upper):
        here = pl.ds(pl.multiple_of(number * block, block), block)
        first = dot(sums_ref[here, :width], weight(weights, 0, height), (1, 1))
        first += dot(sums_ref[here, width : 2 * width], weight(weights, height, height), (1, 1))
        kv = weights[:, 2 * height : 3 * height, 0 : 2 * kv_width].reshape(d_model, 2 * kv_width)
        first += dot(sums_ref[here, q_width:], kv, (1, 1))
        rows = rows_ref[here].astype(WIDE)
        scale = lax.rsqrt(jnp.mean(rows * rows, -1, keepdims=True) + EPSILON)
        inner = first * gain
        inner = scale * inner - rows * (scale * scale * scale * jnp.mean(rows * inner, -1, keepdims=True))
        entry = lax.broadcasted_iota(jnp.int32, (block, own_ids.shape[1]), 0) + number * block
        own_pick = (entry == own_ids).astype(LOW)
        part = (inner + dot(own_pick, grad_ref[...], (1, 0))).astype(LOW)
        row_parts[pl.ds(number * group, group)] = part.reshape(group, *row_parts.shape[1:])
        yield


def last_kernel(
    dq_hbm, dk_hbm, dv_hbm, query_hbm, kv_hbm, grad_hbm, new_rows_hbm, own_ids_ref, got_ids_ref, gains_ref, ids_ref, dense_hbm, rest_hbm,
    *refs
):
    column_hbm, refs = refs[0], refs[1:]
    row_grad, dense_total, rest_total, table_grad, dense, rest, in_grad, out_grad, proj_grad, rest_grad, *refs = refs
    kept, refs = refs[:10], refs[10:]
    slot_all, rows_low, normed_two, acts, load_sems, dq_ref, dk_ref, dv_ref, grad_ref, new_rows_ref, sums_ref, row_parts, row_sems, column, *refs = refs
    row_scratch, refs = refs[:12], refs[12:]
    plane_scratch = [refs[9 * turn : 9 * turn + 9] for turn in range(4)]
    slot_sems, line_sems = refs[36:40], refs[40:42]
    place = Place()
    row_run = row_part_steps(
        place,
        (dq_hbm, dk_hbm, dv_hbm, query_hbm, kv_hbm, grad_hbm, new_rows_hbm),
        (dq_ref, dk_ref, dv_ref, grad_ref, new_rows_ref, sums_ref),
        (own_ids_ref, got_ids_ref),
        gains_ref,
        dense,
        row_parts,
        row_sems,
    )
    next(row_run)
    place.greet()
    next(row_run)
    loads = []

    def near_half():
        next(row_run)
        for number, pair in enumerate(((column_hbm, column), (rest_hbm, rest), (dense_hbm, dense))):
            loads.append(started(*pair, load_sems.at[number]))

    slot_rows, pooled, normed, query, key, value, probs, heads, resid, pre = kept
    width = dense.shape[2]
    slots = ids_ref.shape[0]
    height = slot_all.shape[1] // slots

    def forward_steps():
        for copy in loads:
            copy.wait()
        lengths = []
        for plane in range(PLANES):
            for slot in range(slots):
                here = (slot * PLANES + plane) * height
                slot_rows[here : here + height] = column[plane, slot * height : (slot + 1) * height].astype(WIDE)
            lengths.append(lengths_column(column[plane, slots * height :, :height]))
        hyper_forward_body(dense, rest, slot_rows, jnp.concatenate(lengths, 0), *kept[1:])
        yield

    def sum_steps():
        yield from scatter_steps(place, row_parts, row_grad, row_scratch, near_half)
        rows_low[place.z] = row_grad[...].astype(LOW)
        yield from line_share_steps(place, rows_low, line_sems)

    run_in_order([sum_steps(), forward_steps()], ROW_ORDER)
    vectors = vectors_of(rest)

    def put(in_dense, row, grad, height=16):
        target = (in_grad, out_grad, proj_grad)[row // 64] if in_dense else rest_grad
        row = row % 64 if in_dense else row
        target[:, row : row + height, :] = grad.astype(LOW).reshape(target.shape[0], height, width)

    d_resid, gain_two, bias_two, sums = back_dense(
        dense, vectors, rows_low[...].reshape(-1, rows_low.shape[2]), pooled, resid[...], pre, normed_two, acts, put, place.z
    )
    own = lax.axis_index("dp") * 2 + place.core

    def attention_steps():
        saved = (normed, query, key, value, probs, heads)
        slot_low, gain_one, bias_one = back_attention(rest, vectors, d_resid, slot_rows[...], saved, put, place.z)
        slot_low = slot_low.reshape(slots, PLANES, height, width)
        for plane in range(PLANES):
            slot_all[place.slot(0, plane, place.core)] = slot_low[:, plane].reshape(slots * height, width)
        put_vectors(rest_grad, vector_rows(gain_one, gain_two, bias_one, bias_two, sums))
        yield

    def table_steps():
        slots_run = plane_gather_steps(place, slot_all, slot_sems)
        for _ in range(GATHER_STEPS - 1):
            next(slots_run)
            yield
        pieces = table_grad.shape[0]
        piece = lax.broadcasted_iota(jnp.int32, (pieces, ids_ref.shape[1]), 0) + own * pieces
        for turn in range(slots):
            pick = (piece == ids_ref[turn : turn + 1]).astype(LOW)
            part = dot(pick, slot_all[:, turn * height : (turn + 1) * height, :].reshape(-1, width), (1, 0))
            if turn:
                table_grad[...] += part
            else:
                table_grad[...] = part
            yield
        next(slots_run)
        yield

    places = (slice(IN_ROW, IN_ROW + 64), slice(OUT_ROW, OUT_ROW + 64), slice(PROJ_ROW, PROJ_ROW + 64))
    runs = [
        plane_scatter_steps(place, grad, dense_total, rows, scratch)
        for grad, rows, scratch in zip((in_grad, out_grad, proj_grad), places, plane_scratch)
    ]
    runs.append(plane_scatter_steps(place, rest_grad, rest_total, slice(None), plane_scratch[3]))
    runs += [table_steps(), attention_steps()]
    run_in_order(runs, LAST_ORDER)


def last_exchange(attention, ids, gains, slot_ids, dense, rest, column, pieces, number):
    in_vmem, anywhere = pl.BlockSpec(memory_space=pltpu.VMEM), pl.BlockSpec(memory_space=pl.ANY)
    devices = 8 * PLANES
    width = dense.shape[2]
    dq, dk, dv, query, kv, grad, rows = attention
    entries, d_model = rows.shape
    groups = dense.shape[0]
    query = query.reshape(groups, -1, query.shape[1])
    kv = kv.reshape(2, groups, -1, kv.shape[2])
    one = (entries // devices, d_model)
    slots = slot_ids.size // devices
    kept = [jax.ShapeDtypeStruct((PLANES * slots, width), WIDE)]
    kept += forward_shapes(PLANES * entries // devices, PLANES * slots, width)
    pooled = kept[1].shape
    return pl.pallas_call(
        last_kernel,
        in_specs=[anywhere] * 7 + [in_vmem] * 4 + [anywhere] * 3,
        out_specs=[in_vmem] * 4,
        out_shape=[
            jax.ShapeDtypeStruct(one, WIDE),
            jax.ShapeDtypeStruct(dense.shape[1:], WIDE),
            jax.ShapeDtypeStruct(rest.shape[1:], WIDE),
            jax.ShapeDtypeStruct((pieces, width), WIDE),
        ],
        scratch_shapes=[pltpu.VMEM(dense.shape, LOW), pltpu.VMEM(rest.shape, LOW)]
        + [pltpu.VMEM((8, 64, width), LOW)] * 3
        + [pltpu.VMEM((8, *rest.shape[1:]), LOW)]
        + [pltpu.VMEM(array.shape, array.dtype) for array in kept]
        + [
            pltpu.VMEM((devices, slots, width), LOW),
            pltpu.VMEM((PLANES, *one), LOW),
            pltpu.VMEM(pooled, LOW),
            pltpu.VMEM((4, *pooled), LOW),
            dma_grid(3),
        ]
        + [pltpu.VMEM(array.shape, LOW) for array in (dq, dk, dv, grad, rows)]
        + [
            pltpu.VMEM((entries, dq.shape[0] + 2 * dk.shape[0]), LOW),
            pltpu.VMEM((devices, *one), LOW),
            dma_grid(9),
            pltpu.VMEM(column.shape, LOW),
        ]
        + scatter_scratch(one)
        + plane_scatter_scratch((64, width)) * 3
        + plane_scatter_scratch(rest.shape[1:])
        + plane_gather_sems()
        + line_share_sems(),
        compiler_params=pltpu.CompilerParams(
            collective_id=number, has_side_effects=True, vmem_limit_bytes=VMEM_LIMIT
        ),
        name="last_exchange",
    )(dq, dk, dv, query, kv, grad, rows, *ids, gains, slot_ids, dense, rest, column)


def finish_kernel(
    own_ref, dense_ref, rest_ref, row_ref, table_ref, row_out, table_out, gains_out, biases_out, attn_out, in_out, in_bias_out, out_out,
    proj_out, proj_bias_out
):
    own = own_ref[0]
    width = rest_ref.shape[1]
    row_out[...] = row_ref[...]
    table_out[...] = table_ref[...]
    attn_out[...] = rest_ref[0:64].reshape(attn_out.shape)
    for turn in range(4):
        columns = slice(turn * width, (turn + 1) * width)
        in_out[:, columns] = dense_ref[IN_ROW + 16 * turn : IN_ROW + 16 * turn + 16]
        proj_out[:, columns] = dense_ref[PROJ_ROW + 16 * turn : PROJ_ROW + 16 * turn + 16]
    out_out[...] = dense_ref[OUT_ROW : OUT_ROW + 64]
    vectors = rest_ref[VECTOR_ROW : VECTOR_ROW + 16]

    def own_lanes(rows, size, base):
        lane = lax.broadcasted_iota(jnp.int32, (width, size), 0)
        column = lax.broadcasted_iota(jnp.int32, (width, size), 1)
        return dot_wide(rows, (lane + base - own * size == column).astype(WIDE), (1, 0))

    small = own_lanes(vectors, gains_out.shape[1], 0)
    gains_out[...] = small[0:2]
    biases_out[...] = small[2:5]
    size = in_bias_out.shape[1]
    picked = [own_lanes(vectors, size, turn * width) for turn in range(4)]
    in_bias_out[...] = sum(picked[turn][5 + turn : 6 + turn] for turn in range(4))
    proj_bias_out[...] = sum(picked[turn][9 + turn : 10 + turn] for turn in range(4))


def finish(own, dense, rest, row_grad, table_grad, shapes):
    return pl.pallas_call(
        finish_kernel,
        in_specs=[pl.BlockSpec(memory_space=pltpu.SMEM)] + [pl.BlockSpec(memory_space=pltpu.VMEM)] * 4,
        out_shape=[jax.ShapeDtypeStruct(shape, WIDE) for shape in (row_grad.shape, table_grad.shape, *shapes)],
        name="finish",
        compiler_params=pltpu.CompilerParams(vmem_limit_bytes=VMEM_LIMIT),
    )(own, dense, rest, row_grad, table_grad)


def to_slabs(attn, ffn_in, ffn_out, proj, vectors):
    width = attn.shape[-1]
    groups = width // 16

    def columns(matrix):
        return matrix.reshape(groups, 16, 4, width).transpose(0, 2, 1, 3).reshape(groups, 64, width)

    dense = [columns(ffn_in), ffn_out.reshape(groups, 64, width), columns(proj)]
    rest = [
        attn.reshape(4, groups, 16, width).transpose(1, 0, 2, 3).reshape(groups, 64, width),
        jnp.pad(vectors[None], ((0, groups - 1), (0, 0), (0, 0))),
    ]
    return jnp.concatenate(dense, 1), jnp.concatenate(rest, 1)


def from_slabs(dense, rest):
    groups, _, width = dense.shape

    def columns(row):
        part = dense[:, row : row + 64].reshape(groups, 4, 16, width)
        return part.transpose(0, 2, 1, 3).reshape(groups * 16, 4 * width)

    attn = rest[:, 0:64].reshape(groups, 4, 16, width).transpose(1, 0, 2, 3).reshape(4, groups * 16, width)
    return attn, columns(IN_ROW), dense[:, OUT_ROW : OUT_ROW + 64].reshape(groups * 64, width), columns(PROJ_ROW)


def shards(
    piece_ids,
    piece_lengths,
    group_ids,
    piece_table,
    ln_gains,
    hyp_biases,
    attn_weights,
    ffn_in_weight,
    ffn_in_bias,
    ffn_out_weight,
    proj_weight,
    proj_bias,
    lm_gains,
    query_weight,
    kv_weights,
    output_weight,
    gate_up_weight,
    down_weight,
    out_grad,
):
    n_mp = lax.axis_size("mp")
    devices = lax.axis_size(BOTH)
    me = lax.axis_index("mp")
    grid = n_mp == 2 and devices == 32
    entries, slot_count = piece_lengths.shape[0], piece_ids.shape[1]
    hyp_width = piece_table.shape[1]

    def swap(value):
        return lax.ppermute(value, "mp", [(0, 1), (1, 0)])

    def whole_of(value, axis):
        return lax.all_gather(value, BOTH, axis=axis, tiled=True)

    def share_of(value, axis):
        return lax.psum_scatter(value, BOTH, scatter_dimension=axis, tiled=True).astype(WIDE)

    def gather_tokens(value):
        return lax.all_gather(value, "mp", axis=0, tiled=True)

    me_all = lax.axis_index(BOTH)
    my_place = me.astype(jnp.int32).reshape(1)
    table_rows = piece_table.shape[0]
    lengths = piece_lengths[None]
    local_len = group_ids.shape[1]
    own_ids = group_ids.reshape(-1)
    got_ids = swap(own_ids) if grid else None
    seq_len = n_mp * local_len
    q_heads = query_weight.shape[1] // HEAD_DIM
    kv_here = max(KV_HEADS // n_mp, 1)
    cosine, sine = rope_tables(seq_len)
    lm_wide = lm_gains.astype(WIDE)
    dy_low = out_grad.reshape(local_len, -1)

    def norm_first(values):
        return rms_norm(values, lm_wide[0])

    def norm_second(values):
        return rms_norm(values, lm_wide[1])

    if grid:
        weights = (
            ln_gains,
            hyp_biases,
            attn_weights,
            ffn_in_weight,
            ffn_in_bias[None],
            ffn_out_weight,
            proj_weight,
            proj_bias[None],
        )
        slot_ids = piece_ids.T
        dense, rest, column, d_act, new_rows, inputs, qkv = first_exchange(
            weights,
            slot_ids,
            piece_table,
            lengths,
            lm_gains,
            own_ids[None],
            got_ids[None],
            dy_low,
            down_weight,
            query_weight,
            kv_weights,
            0,
        )
    else:
        own_pieces = me_all * table_rows + jnp.arange(table_rows, dtype=jnp.int32)
        slot_ids = piece_ids.reshape(devices, entries, slot_count).transpose(0, 2, 1).reshape(-1)
        slot_pick = (slot_ids[:, None] == own_pieces[None, :]).astype(LOW)
        slot_parts = dot(slot_pick, piece_table, (1, 0)).astype(LOW)
        slot_rows = lax.psum_scatter(slot_parts, BOTH, scatter_dimension=0, tiled=True).astype(WIDE)
        vectors = jnp.concatenate(
            [
                whole_of(ln_gains, 1),
                whole_of(hyp_biases, 1),
                whole_of(ffn_in_bias, 0).reshape(4, hyp_width),
                whole_of(proj_bias, 0).reshape(4, hyp_width),
                jnp.zeros((3, hyp_width), LOW),
            ]
        )
        dense, rest = to_slabs(
            whole_of(attn_weights, 1),
            whole_of(ffn_in_weight, 0),
            whole_of(ffn_out_weight, 0),
            whole_of(proj_weight, 0),
            vectors,
        )
        saved = hyper_forward(dense, rest, slot_rows, lengths, entries)
        new_rows, normed_rows = project(whole_of(saved[0], 0), dense, rest, lm_gains)
        kv_start = me * q_heads // (HEADS // KV_HEADS) * HEAD_DIM
        kv_local = lax.dynamic_slice_in_dim(kv_weights, kv_start, kv_here * HEAD_DIM, 2)
        qkv_weight = jnp.concatenate([query_weight, kv_local[0], kv_local[1]], 1)
        row_ids = lax.all_gather(own_ids, "mp", axis=0, tiled=True)
        row_index = jnp.arange(new_rows.shape[0], dtype=jnp.int32)
        row_pick = (row_index[:, None] == row_ids[None, :]).astype(LOW)
        own_pick = (own_ids[:, None] == row_index[None, :]).astype(LOW)
        qkv = dot(qkv_weight, dot(row_pick, normed_rows, (0, 0)).astype(LOW), (0, 1)).astype(LOW)
        inputs = dot(own_pick, new_rows, (1, 0))
        d_act = dot(gather_tokens(dy_low), down_weight, (1, 1)).astype(LOW)
    *heads, log_total = attend(my_place, qkv, cosine, sine, q_heads, kv_here, 2 if grid else 1)

    if grid:
        hidden, x_own, x_other = middle(*heads, output_weight, inputs, lm_gains, 2)
        out_other, back_other = feed_forward(x_other, d_act, 1, gate_up_weight, down_weight)
        out_got, back_got = swap(out_other), swap(back_other)
        out_own, back_own = feed_forward(x_own, d_act, 0, gate_up_weight, down_weight)
        grad_hidden_low, *grad_heads = turn_around(hidden, dy_low, (back_own, back_got), output_weight, lm_gains, 3)
    else:
        attn_part = dot(heads[0], output_weight, (0, 0)).astype(LOW)
        attn_sum = lax.psum_scatter(attn_part, "mp", scatter_dimension=0, tiled=True).astype(WIDE)
        hidden = inputs + attn_sum
        second_low = norm_second(hidden).astype(LOW)
        out_part, back_part = feed_forward(gather_tokens(second_low), d_act, 0, gate_up_weight, down_weight)
        outs = (lax.psum_scatter(out_part, "mp", scatter_dimension=0, tiled=True),)
        backs = (lax.psum_scatter(back_part, "mp", scatter_dimension=0, tiled=True),)
        lm_out, grad_hidden_low = second_back(hidden, dy_low, lm_gains, outs, backs)
        grad_heads = [dot(output_weight, gather_tokens(grad_hidden_low), (1, 1)).astype(LOW)]
    terms = (hidden, out_own, out_got) if grid else ()
    dq, dk, dv, *sums = attend_back(my_place, qkv, heads, log_total, grad_heads, cosine, sine, q_heads, kv_here, terms)
    if grid:
        lm_out = sums[0]

    if grid:
        attention = (dq, dk, dv, query_weight, kv_weights, grad_hidden_low, new_rows)
        ids = (own_ids[None], got_ids[None])
        row_grad, dense, rest, table_grad = last_exchange(
            attention, ids, lm_gains, slot_ids, dense, rest, column, table_rows, 1
        )
        bias_shape = (1, ffn_in_bias.shape[0])
        shapes = [
            ln_gains.shape,
            hyp_biases.shape,
            attn_weights.shape,
            ffn_in_weight.shape,
            bias_shape,
            ffn_out_weight.shape,
            proj_weight.shape,
            bias_shape,
        ]
        grads = finish(me_all.astype(jnp.int32).reshape(1), dense, rest, row_grad, table_grad, shapes)
        row_grad, table_grad, gains_grad, biases_grad, attn_grad, in_grad, in_bias, out_weight_grad, proj_grad, proj_bias_grad = grads
        in_bias, proj_bias_grad = in_bias[0], proj_bias_grad[0]
    else:
        grad_qkv = dot(jnp.concatenate([dq, dk, dv], 0), row_pick, (1, 1)).astype(LOW)
        first_part = dot(grad_qkv, qkv_weight, (0, 1))
        direct_part = dot(own_pick, grad_hidden_low, (0, 0))
        _, first_back = jax.vjp(norm_first, new_rows.astype(WIDE))
        row_parts = (direct_part + first_back(first_part)[0]).astype(LOW)
        row_grad = lax.psum_scatter(row_parts, BOTH, scatter_dimension=0, tiled=True).astype(WIDE)
        dense_grad, rest_grad, slot_low = hyper_backward(dense, rest, row_grad, slot_rows, saved)
        attn_grad, *dense_grads = from_slabs(dense_grad, rest_grad)
        attn_grad = share_of(attn_grad, 1)
        in_grad, out_weight_grad, proj_grad = [share_of(grad, 0) for grad in dense_grads]
        table_grad = dot(slot_pick, whole_of(slot_low, 0), (0, 0))
        sums = lax.psum(rest_grad[0, VECTOR_ROW:], BOTH).astype(WIDE)

        def own_lanes(values, size):
            return lax.dynamic_slice_in_dim(values, me_all * size, size, 1)

        gains_grad = own_lanes(sums[0:2], ln_gains.shape[1])
        biases_grad = own_lanes(sums[2:5], ln_gains.shape[1])
        in_bias, proj_bias_grad = own_lanes(sums[5:13].reshape(2, -1), ffn_in_bias.shape[0])
    return (
        lm_out.reshape(out_grad.shape),
        row_grad,
        table_grad,
        gains_grad,
        biases_grad,
        attn_grad,
        in_grad,
        in_bias,
        out_weight_grad,
        proj_grad,
        proj_bias_grad,
    )


def solution(mesh):
    return jax.shard_map(
        shards,
        mesh=mesh,
        in_specs=(
            P(),
            P(BOTH),
            P("dp", "mp"),
            P(BOTH, None),
            P(None, BOTH),
            P(None, BOTH),
            P(None, BOTH, None),
            P(BOTH, None),
            P(BOTH),
            P(BOTH, None),
            P(BOTH, None),
            P(BOTH),
            P(),
            P(None, "mp"),
            P(),
            P("mp", None),
            P(None, None, "mp"),
            P("mp", None),
            P("dp", "mp", None),
        ),
        out_specs=(
            P("dp", "mp", None),
            P(BOTH, None),
            P(BOTH, None),
            P(None, BOTH),
            P(None, BOTH),
            P(None, BOTH, None),
            P(BOTH, None),
            P(BOTH),
            P(BOTH, None),
            P(BOTH, None),
            P(BOTH),
        ),
        check_vma=False,
    )
```

```python
import functools

import jax
import jax.numpy as jnp
from jax import lax
from jax.experimental import pallas as pl
from jax.experimental.pallas import tpu as pltpu
from jax.sharding import PartitionSpec as P

HEADS = 32
KV_HEADS = 4
HEAD_DIM = 64
HYP_HEADS = 8

EPSILON = 1e-05
ROPE_BASE = 10000.0
MASKED = -1e30
BOTH = ("dp", "mp")
LOW = jnp.bfloat16
WIDE = jnp.float32
QUERY_BLOCK = 256
MIB = 1 << 20
PLANES = 4
DENSE_ROWS, REST_ROWS = 192, 80
UNIT_BLOCK = 256
VMEM_LIMIT = 62 * MIB
FIRST_ORDER = (
    1, 0, 2, 2, 2, 2, 2, 0, 1, 0, 0, 2, 2, 0, 3, 1, 0, 2, 2, 1, 0, 2, 1, 0, 2, 3, 3, 0, 1, 2, 2, 0, 3, 2, 1, 2, 0,
    0, 1, 2, 1, 1, 2, 0, 2, 3, 3, 0, 1, 0, 0, 0, 0, 0, 1, 1, 1, 3, 1, 1, 0, 0, 2, 0, 3, 2, 2, 2, 1, 1, 0, 3, 2, 0,
    1, 1, 1, 1, 2, 1, 0, 0, 0, 2, 2, 0, 1, 3, 1, 0, 1, 0, 2, 1, 1, 2, 3, 0, 2, 2, 2, 0, 1, 0, 0, 0, 2, 2, 1, 2, 2,
    0, 2, 0, 2, 2,
)
LAST_ORDER = (
    5, 4, 4, 4, 4, 4, 0, 4, 1, 4, 4, 2, 4, 4, 4, 0, 3, 4, 4, 1, 4, 4, 2, 4, 4, 4, 4, 4, 3, 4, 1, 1, 0, 4, 4, 4, 0,
    4, 2, 4, 3, 2, 4, 4, 3, 0, 1, 0, 1, 2, 2, 4, 3, 3,
)
ROW_ORDER = (
    0, 0, 0, 0, 0, 0, 0, 0, 0, 0, 0, 0, 0, 0, 0, 0, 0, 0, 0, 0, 0, 0, 0, 0, 0, 0, 0, 0, 0, 0, 0, 1, 0,
)
HEADS_A_STEP = 4
QUERY_SCALE = HEAD_DIM ** (-0.5) * 1.4426950408889634


def rms_norm(values, gain_row):
    return values * lax.rsqrt(jnp.mean(values * values, -1, keepdims=True) + EPSILON) * gain_row


def dot(left, right, dims):
    return lax.dot_general(left, right, ((dims[:1], dims[1:]), ((), ())), preferred_element_type=WIDE)


def rope_tables(length):
    half = HEAD_DIM // 2
    frequency = ROPE_BASE ** (-2.0 * jnp.arange(half, dtype=WIDE) / HEAD_DIM)
    angles = frequency[:, None] * jnp.arange(length, dtype=WIDE)[None, :]
    return jnp.cos(angles), jnp.sin(angles)


def turn(columns, cosine, sine):
    half = HEAD_DIM // 2
    first, second = columns[:half], columns[half:]
    return jnp.concatenate([first * cosine - second * sine, second * cosine + first * sine], 0)


def turn_back(columns, cosine, sine):
    half = HEAD_DIM // 2
    first, second = columns[:half], columns[half:]
    return jnp.concatenate([first * cosine + second * sine, second * cosine - first * sine], 0)


def keep_causal(block, fill):
    key = lax.broadcasted_iota(jnp.int32, block.shape, 0)
    query = lax.broadcasted_iota(jnp.int32, block.shape, 1)
    return jnp.where(key <= query, block, fill)


def own_half(me_ref, left, right):
    first = me_ref[0] == 0
    return jnp.where(first, left, right), jnp.where(first, right, left)


def attend_kernel(per_group, me_ref, q_ref, k_ref, v_ref, cos_ref, sin_ref, *refs):
    *out_refs, log_ref, key_rows, out_all = refs
    seq_len = q_ref.shape[1]
    width = min(QUERY_BLOCK, seq_len)
    cosine, sine = cos_ref[...], sin_ref[...]
    count = q_ref.shape[0] // HEAD_DIM

    @pl.when(lax.rem(pl.program_id(0) * count, per_group) == 0)
    def _():
        key_rows[...] = turn(k_ref[...].astype(WIDE), cosine, sine).T.astype(LOW)

    queries = [
        (turn(q_ref[head * HEAD_DIM : (head + 1) * HEAD_DIM].astype(WIDE), cosine, sine) * QUERY_SCALE).astype(LOW)
        for head in range(count)
    ]

    def scores(start, head):
        q_block = queries[head][:, start : start + width]
        edge = dot(key_rows[start : start + width], q_block, (1, 0))
        return edge, dot(key_rows[:start], q_block, (1, 0)) if start else None

    def finish(start, head, edge, past):
        here = slice(start, start + width)
        lanes = slice(head * HEAD_DIM, (head + 1) * HEAD_DIM)
        edge = keep_causal(edge, MASKED)
        top = jnp.max(edge, 0, keepdims=True)
        if start:
            top = jnp.maximum(top, jnp.max(past, 0, keepdims=True))
        edge = jnp.exp2(edge - top)
        total = jnp.sum(edge, 0, keepdims=True)
        out = dot(v_ref[:, here], edge.astype(LOW), (1, 0))
        if start:
            past = jnp.exp2(past - top)
            total = total + jnp.sum(past, 0, keepdims=True)
            out = out + dot(v_ref[:, :start], past.astype(LOW), (1, 0))
        out_all[lanes, here] = (out / total).astype(LOW)
        log_ref[head, :, here] = top + jnp.log2(total)

    items = [(start, head) for start in range(0, seq_len, width) for head in range(count)]
    ready = scores(*items[0])
    for number, item in enumerate(items):
        following = scores(*items[number + 1]) if number + 1 < len(items) else None
        finish(*item, *ready)
        ready = following
    if len(out_refs) == 2:
        half = seq_len // 2
        out_refs[0][...], out_refs[1][...] = own_half(me_ref, out_all[:, :half], out_all[:, half:])
    else:
        out_refs[0][...] = out_all[...]


def attend(me, qkv, cosine, sine, q_heads, kv_heads, parts):
    per_group = q_heads // kv_heads
    seq_len = qkv.shape[1]
    column = (HEAD_DIM, seq_len)
    count = HEADS_A_STEP
    several = (count * HEAD_DIM, seq_len)
    whole = pl.BlockSpec(cosine.shape, lambda h: (0, 0))
    return pl.pallas_call(
        functools.partial(attend_kernel, per_group),
        grid=(q_heads // count,),
        in_specs=[
            pl.BlockSpec(memory_space=pltpu.SMEM),
            pl.BlockSpec(several, lambda h: (h, 0)),
            pl.BlockSpec(column, lambda h: (q_heads + h * count // per_group, 0)),
            pl.BlockSpec(column, lambda h: (q_heads + kv_heads + h * count // per_group, 0)),
            whole,
            whole,
        ],
        out_specs=[pl.BlockSpec((count * HEAD_DIM, seq_len // parts), lambda h: (h, 0))] * parts
        + [pl.BlockSpec((count, 1, seq_len), lambda h: (h, 0, 0))],
        out_shape=[jax.ShapeDtypeStruct((q_heads * HEAD_DIM, seq_len // parts), LOW)] * parts
        + [jax.ShapeDtypeStruct((q_heads, 1, seq_len), WIDE)],
        scratch_shapes=[pltpu.VMEM((seq_len, HEAD_DIM), LOW), pltpu.VMEM(several, LOW)],
        compiler_params=pltpu.CompilerParams(vmem_limit_bytes=VMEM_LIMIT),
        cost_estimate=pl.CostEstimate(
            flops=2 * q_heads * seq_len * seq_len * HEAD_DIM,
            bytes_accessed=4 * qkv.size,
            transcendentals=q_heads * seq_len * seq_len // 2,
        ),
        name="attend",
    )(me, qkv, qkv, qkv, cosine, sine)


def attend_back_kernel(per_group, parts, terms, me_ref, q_ref, k_ref, v_ref, log_ref, cos_ref, sin_ref, *refs):
    out_refs, grad_refs, refs = refs[:parts], refs[parts : 2 * parts], refs[2 * parts :]
    term_refs, refs = refs[:terms], refs[terms:]
    if terms:
        sum_ref, refs = refs[3], refs[:3] + refs[4:]
        sum_ref[...] = sum(ref[...].astype(WIDE) for ref in term_refs).astype(LOW)
    dq_ref, dk_ref, dv_ref, key_cols, key_rows, value_rows, key_sum, value_sum = refs
    seq_len = q_ref.shape[1]
    width = min(QUERY_BLOCK, seq_len)
    cosine, sine = cos_ref[...], sin_ref[...]
    count = q_ref.shape[0] // HEAD_DIM
    heads = range(count)
    member = lax.rem(pl.program_id(0) * count, per_group)

    def in_order(pieces, lanes):
        if len(pieces) == 1:
            return pieces[0][lanes]
        return jnp.concatenate(own_half(me_ref, pieces[0][lanes], pieces[1][lanes]), 1)

    @pl.when(member == 0)
    def _():
        turned = turn(k_ref[...].astype(WIDE), cosine, sine)
        key_cols[...] = turned.astype(LOW)
        key_rows[...] = turned.T.astype(LOW)
        value_rows[...] = v_ref[...].astype(WIDE).T.astype(LOW)
        key_sum[...] = jnp.zeros_like(key_sum)
        value_sum[...] = jnp.zeros_like(value_sum)

    queries, query_rows, grads, grad_rows, deltas = [], [], [], [], []
    for head in heads:
        lanes = slice(head * HEAD_DIM, (head + 1) * HEAD_DIM)
        turned = turn(q_ref[lanes].astype(WIDE), cosine, sine) * QUERY_SCALE
        queries.append(turned.astype(LOW))
        query_rows.append(turned.T.astype(LOW))
        grad = in_order(grad_refs, lanes)
        grads.append(grad)
        grad_wide = grad.astype(WIDE)
        grad_rows.append(grad_wide.T.astype(LOW))
        deltas.append(jnp.sum(grad_wide * in_order(out_refs, lanes).astype(WIDE), 0, keepdims=True))

    def pieces_of(start):
        return [slice(start, start + width)] + ([slice(0, start)] if start else [])

    def products(start):
        here = slice(start, start + width)
        return [
            [
                (dot(key_rows[keys], queries[head][:, here], (1, 0)), dot(value_rows[keys], grads[head][:, here], (1, 0)))
                for head in heads
            ]
            for keys in pieces_of(start)
        ]

    def finish(start, found):
        here = slice(start, start + width)
        dq = [0.0] * count
        for number, keys in enumerate(pieces_of(start)):
            probs, scores = [], []
            for head in heads:
                raw, grad_probs = found[number][head]
                prob = jnp.exp2(raw - log_ref[head, :, here])
                if number == 0:
                    prob = keep_causal(prob, 0.0)
                probs.append(prob.astype(LOW))
                scores.append((prob * (grad_probs - deltas[head][:, here])).astype(LOW))
                dq[head] += dot(key_cols[:, keys], scores[head], (1, 0))
            grad_part = jnp.concatenate([rows[here] for rows in grad_rows], 0)
            query_part = jnp.concatenate([rows[here] for rows in query_rows], 0)
            value_sum[keys] += dot(jnp.concatenate(probs, 1), grad_part, (1, 0))
            key_sum[keys] += dot(jnp.concatenate(scores, 1), query_part, (1, 0))
        for head in heads:
            back = turn_back(dq[head] * HEAD_DIM ** (-0.5), cosine[:, here], sine[:, here])
            dq_ref[head * HEAD_DIM : (head + 1) * HEAD_DIM, here] = back.astype(LOW)

    starts = list(range(0, seq_len, width))
    ready = products(0)
    for number, start in enumerate(starts):
        following = products(starts[number + 1]) if number + 1 < len(starts) else None
        finish(start, ready)
        ready = following

    @pl.when(member == per_group - count)
    def _():
        dk_ref[...] = turn_back(key_sum[...].T * (HEAD_DIM ** (-0.5) / QUERY_SCALE), cosine, sine).astype(LOW)
        dv_ref[...] = value_sum[...].T.astype(LOW)


def attend_back(me, qkv, outs, log_total, grads, cosine, sine, q_heads, kv_heads, terms=()):
    per_group = q_heads // kv_heads
    seq_len = qkv.shape[1]
    parts = len(outs)
    count = HEADS_A_STEP
    column = (HEAD_DIM, seq_len)
    whole = pl.BlockSpec(cosine.shape, lambda h: (0, 0))
    by_head = pl.BlockSpec((count * HEAD_DIM, seq_len), lambda h: (h, 0))
    by_group = pl.BlockSpec(column, lambda h: (h * count // per_group, 0))
    in_parts = pl.BlockSpec((count * HEAD_DIM, seq_len // parts), lambda h: (h, 0))
    steps = q_heads // count
    term_rows = [pl.BlockSpec((term.shape[0] // steps, term.shape[1]), lambda h: (h, 0)) for term in terms]
    return pl.pallas_call(
        functools.partial(attend_back_kernel, per_group, parts, len(terms)),
        grid=(q_heads // count,),
        in_specs=[
            pl.BlockSpec(memory_space=pltpu.SMEM),
            by_head,
            pl.BlockSpec(column, lambda h: (q_heads + h * count // per_group, 0)),
            pl.BlockSpec(column, lambda h: (q_heads + kv_heads + h * count // per_group, 0)),
            pl.BlockSpec((count, 1, seq_len), lambda h: (h, 0, 0)),
            whole,
            whole,
        ]
        + [in_parts] * (2 * parts)
        + term_rows,
        out_specs=[by_head, by_group, by_group] + term_rows[:1],
        out_shape=[
            jax.ShapeDtypeStruct((q_heads * HEAD_DIM, seq_len), LOW),
            jax.ShapeDtypeStruct((kv_heads * HEAD_DIM, seq_len), LOW),
            jax.ShapeDtypeStruct((kv_heads * HEAD_DIM, seq_len), LOW),
        ]
        + [jax.ShapeDtypeStruct(term.shape, LOW) for term in terms[:1]],
        scratch_shapes=[
            pltpu.VMEM((HEAD_DIM, seq_len), LOW),
            pltpu.VMEM((seq_len, HEAD_DIM), LOW),
            pltpu.VMEM((seq_len, HEAD_DIM), LOW),
            pltpu.VMEM((seq_len, HEAD_DIM), WIDE),
            pltpu.VMEM((seq_len, HEAD_DIM), WIDE),
        ],
        compiler_params=pltpu.CompilerParams(vmem_limit_bytes=VMEM_LIMIT),
        cost_estimate=pl.CostEstimate(
            flops=5 * q_heads * seq_len * seq_len * HEAD_DIM,
            bytes_accessed=8 * qkv.size,
            transcendentals=q_heads * seq_len * seq_len // 2,
        ),
        name="attend_back",
    )(me, qkv, qkv, qkv, log_total, cosine, sine, *outs, *grads, *terms)


def feed_kernel(last_block, x_ref, d_act_ref, gate_up_ref, down_ref, out_ref, back_ref, out_sum, back_sum):
    step, last = pl.program_id(0), pl.num_programs(0) - 1

    @pl.when(step == 0)
    def _():
        out_sum[...] = jnp.zeros_like(out_sum)
        back_sum[...] = jnp.zeros_like(back_sum)

    def units(size):
        x, down = x_ref[...], down_ref[:size]
        gate_weight, up_weight = gate_up_ref[0, :, :size], gate_up_ref[1, :, :size]
        gate = dot(x, gate_weight, (1, 0))
        up = dot(x, up_weight, (1, 0))
        d_act = d_act_ref[:, :size].astype(WIDE)
        sigmoid = jax.nn.sigmoid(gate)
        silu = gate * sigmoid
        act = (silu * up).astype(LOW)
        d_up = (d_act * silu).astype(LOW)
        d_gate = (d_act * up * (sigmoid + silu * (1.0 - sigmoid))).astype(LOW)
        out_sum[...] += dot(act, down, (1, 0))
        back_sum[...] += dot(d_gate, gate_weight, (1, 1))
        back_sum[...] += dot(d_up, up_weight, (1, 1))

    block = down_ref.shape[0]
    if last_block == block:
        units(block)
    else:
        pl.when(step < last)(lambda: units(block))
        pl.when(step == last)(lambda: units(last_block))

    @pl.when(step == last)
    def _():
        out_ref[...] = out_sum[...].astype(LOW)
        back_ref[...] = back_sum[...].astype(LOW)


def feed_forward(x, d_act, which, gate_up, down):
    tokens, width = x.shape
    units = down.shape[0]
    block = 2 * UNIT_BLOCK if units % UNIT_BLOCK == 0 else units
    steps = pl.cdiv(units, block)
    whole = pl.BlockSpec((tokens, width), lambda f: (0, 0))
    result = jax.ShapeDtypeStruct((tokens, width), LOW)
    return pl.pallas_call(
        functools.partial(feed_kernel, units - (steps - 1) * block),
        grid=(steps,),
        in_specs=[
            whole,
            pl.BlockSpec((tokens, block), lambda f: (which, f)),
            pl.BlockSpec((2, width, block), lambda f: (0, 0, f)),
            pl.BlockSpec((block, width), lambda f: (f, 0)),
        ],
        out_specs=[whole, whole],
        out_shape=[result, result],
        scratch_shapes=[pltpu.VMEM((tokens, width), WIDE), pltpu.VMEM((tokens, width), WIDE)],
        compiler_params=pltpu.CompilerParams(vmem_limit_bytes=VMEM_LIMIT),
        cost_estimate=pl.CostEstimate(
            flops=10 * tokens * width * units,
            bytes_accessed=6 * width * units + 8 * tokens * width,
            transcendentals=tokens * units,
        ),
        name="feed_forward",
    )(x, d_act, gate_up, down)


def second_back_kernel(hidden_ref, dy_ref, gain_ref, *refs):
    *part_refs, out_ref, grad_ref = refs
    outs, backs = part_refs[: len(part_refs) // 2], part_refs[len(part_refs) // 2 :]
    hidden = hidden_ref[...]
    out_ref[...] = (hidden + sum(ref[...].astype(WIDE) for ref in outs)).astype(LOW)
    scale = lax.rsqrt(jnp.mean(hidden * hidden, -1, keepdims=True) + EPSILON)
    inner = sum(ref[...].astype(WIDE) for ref in backs) * gain_ref[1:2].astype(WIDE)
    mean = jnp.mean(hidden * inner, -1, keepdims=True)
    back = scale * inner - hidden * (scale * scale * scale * mean)
    grad_ref[...] = (dy_ref[...].astype(WIDE) + back).astype(LOW)


def second_back(hidden, dy, gains, outs, backs):
    tokens, width = hidden.shape
    block = min(64, tokens)
    rows = pl.BlockSpec((block, width), lambda i: (i, 0))
    result = jax.ShapeDtypeStruct(hidden.shape, LOW)
    return pl.pallas_call(
        second_back_kernel,
        grid=(tokens // block,),
        in_specs=[rows, rows, pl.BlockSpec((2, width), lambda i: (0, 0))] + [rows] * (len(outs) + len(backs)),
        out_specs=[rows, rows],
        out_shape=[result, result],
        compiler_params=pltpu.CompilerParams(vmem_limit_bytes=VMEM_LIMIT),
        cost_estimate=pl.CostEstimate(flops=12 * hidden.size, bytes_accessed=18 * hidden.size, transcendentals=0),
        name="second_back",
    )(hidden, dy, gains, *outs, *backs)


class Place:
    def __init__(self):
        chip, self.core = lax.axis_index("dp"), lax.axis_index("mp")
        self.z = lax.div(chip, 4)
        self.y, self.x = lax.rem(lax.div(chip, 2), 2), lax.rem(chip, 2)
        self.below, self.above = self.z > 0, self.z < PLANES - 1
        z, y, x, core = self.z, self.y, self.x, self.core
        self.others = (z + 1 - 2 * lax.rem(z, 2), lax.rem(z + 2, PLANES), PLANES - 1 - z)
        self.targets = {
            "x": self.device(z, y, 1 - x, core),
            "y": self.device(z, 1 - y, x, core),
            "diagonal": self.device(z, 1 - y, 1 - x, core),
            "core": self.device(z, y, x, 1 - core),
            "up": self.device(z + 1, y, x, core),
            "down": self.device(z - 1, y, x, core),
        }
        for turn, plane in enumerate(self.others):
            self.targets[turn] = self.device(plane, y, x, core)

    def device(self, plane, y, x, core):
        return {"dp": (plane * 2 + y) * 2 + x, "mp": core}

    def chip(self, kind):
        y = 1 - self.y if kind in (2, 3) else self.y
        x = 1 - self.x if kind in (1, 3) else self.x
        return y * 2 + x

    def slot(self, kind, plane, core):
        return (plane * 4 + self.chip(kind)) * 2 + core

    def levels(self, distance):
        if distance == 0:
            return [(0, self.z, None)]
        return [
            (1, self.z + distance, self.z + distance < PLANES),
            (-1, self.z - distance, self.z >= distance),
        ]

    def at(self, distance, step):
        for sign, plane, valid in self.levels(distance):
            if valid is None:
                step(sign, plane)
            else:
                pl.when(valid)(functools.partial(step, sign, plane))

    def steps_at(self, distance, step):
        for sign, plane, valid in self.levels(distance):
            if valid is None:
                step(sign, plane)
            else:
                pl.when(valid)(functools.partial(step, sign, plane))
            yield

    def greet(self):
        barrier = pltpu.get_barrier_semaphore()
        names = ("x", "y", "diagonal", "core", 0, 1, 2)
        for name in names:
            pl.semaphore_signal(barrier, inc=1, device_id=self.targets[name], device_id_type=pl.DeviceIdType.MESH)
        pl.semaphore_wait(barrier, len(names))


def halves(shape):
    rows, columns = shape[-2:]
    if rows >= 32:
        cut = rows // 32 * 16
        return (slice(0, cut), slice(None)), (slice(cut, rows), slice(None))
    cut = columns // 2
    return (slice(None), slice(0, cut)), (slice(None), slice(cut, columns))


def send(source, target, send_sem, recv_sem, device):
    pltpu.make_async_remote_copy(
        src_ref=source,
        dst_ref=target,
        send_sem=send_sem,
        recv_sem=recv_sem,
        device_id=device,
        device_id_type=pl.DeviceIdType.MESH,
    ).start()


def sent(view, sem):
    pltpu.make_async_copy(view, view, sem).wait()


def dma_grid(*shape):
    return pltpu.SemaphoreType.DMA(shape)


def gather_sems():
    return [pltpu.SemaphoreType.DMA, dma_grid(6, PLANES), dma_grid(5, PLANES), dma_grid(5, PLANES), dma_grid(5, PLANES)]


def gather_steps(place, share, whole, sems):
    own_sem, link_send, link_recv, core_send, core_recv = sems
    near, far = halves(share.shape)
    z, core = place.z, place.core

    def view(kind, plane, whose=None):
        whose = core if whose is None else whose
        if kind >= 3:
            return whole.at[(place.slot(3, plane, whose), *(near if kind == 3 else far))]
        return whole.at[place.slot(kind, plane, whose)]

    def forward(name, source, target, number, kind, plane):
        send(source, target, link_send.at[number, plane], link_recv.at[kind, plane], place.targets[name])

    def to_core(source, kind, plane):
        send(source, view(kind, plane), core_send.at[kind, plane], core_recv.at[kind, plane], place.targets["core"])

    def column(sign, plane):
        target = view(0, plane)
        source = target if sign else share
        if sign:
            sent(target, link_recv.at[0, plane])
        if sign <= 0:
            pl.when(place.above)(lambda: forward("up", source, target, 4, 0, plane))
        if sign >= 0:
            pl.when(place.below)(lambda: forward("down", source, target, 5, 0, plane))
        forward("x", source, target, 0, 1, plane)
        forward("y", source, target, 1, 2, plane)
        to_core(source, 0, plane)

    def side_x(sign, plane):
        sent(view(1, plane), link_recv.at[1, plane])
        part = whole.at[(place.slot(1, plane, core), *far)]
        forward("y", part, part, 3, 4, plane)
        to_core(view(1, plane), 1, plane)

    def side_y(sign, plane):
        sent(view(2, plane), link_recv.at[2, plane])
        part = whole.at[(place.slot(2, plane, core), *near)]
        forward("x", part, part, 2, 3, plane)
        to_core(view(2, plane), 2, plane)

    def diagonal(kind, sign, plane):
        sent(view(kind, plane), link_recv.at[kind, plane])
        to_core(view(kind, plane), kind, plane)

    diagonal_x, diagonal_y = functools.partial(diagonal, 3), functools.partial(diagonal, 4)
    keep = pltpu.make_async_copy(share, view(0, z), own_sem)
    keep.start()
    for step in range(PLANES + 2):
        for stage, lag in ((column, 0), (side_x, 1), (side_y, 1), (diagonal_x, 2), (diagonal_y, 2)):
            if 0 <= step - lag < PLANES:
                yield from place.steps_at(step - lag, stage)
    keep.wait()
    for plane in range(PLANES):
        for kind in range(5):
            sent(view(kind, plane, 1 - core), core_recv.at[kind, plane])
    yield
    for plane in range(PLANES):
        for kind in range(5):
            sent(view(kind, plane), core_send.at[kind, plane])
        for number, part in enumerate((share, share, share.at[near], share.at[far])):
            sent(part, link_send.at[number, plane])
        pl.when((plane <= z) & place.above)(lambda: sent(share, link_send.at[4, plane]))
        pl.when((plane >= z) & place.below)(lambda: sent(share, link_send.at[5, plane]))
    yield


def late_gather_sems():
    return [
        pltpu.SemaphoreType.DMA,
        dma_grid(4),
        dma_grid(4),
        dma_grid(2, 4, PLANES),
        dma_grid(4, PLANES),
        dma_grid(4, PLANES),
        dma_grid(4, PLANES),
    ]


def late_gather_steps(place, share, whole, sems):
    own_sem, plane_send, plane_recv, line_send, line_recv, core_send, core_recv = sems
    near, far = halves(share.shape)
    z, core = place.z, place.core

    def view(kind, plane, whose=None):
        return whole.at[place.slot(kind, plane, core if whose is None else whose)]

    def part(kind, half):
        return whole.at[(place.slot(kind, z, core), *half)]

    def forward(name, source, target, number):
        send(source, target, plane_send.at[number], plane_recv.at[number], place.targets[name])

    def on_line(name, source, kind, plane):
        which = 0 if name == "up" else 1
        send(
            source, view(kind, plane), line_send.at[which, kind, plane], line_recv.at[kind, plane], place.targets[name]
        )

    def own_plane(source, kind):
        pl.when(place.above)(lambda: on_line("up", source, kind, z))
        pl.when(place.below)(lambda: on_line("down", source, kind, z))
        send(source, view(kind, z), core_send.at[kind, z], core_recv.at[kind, z], place.targets["core"])

    def line(kind, sign, plane):
        target = view(kind, plane)
        sent(target, line_recv.at[kind, plane])
        if sign < 0:
            pl.when(place.above)(lambda: on_line("up", target, kind, plane))
        else:
            pl.when(place.below)(lambda: on_line("down", target, kind, plane))
        send(target, target, core_send.at[kind, plane], core_recv.at[kind, plane], place.targets["core"])

    keep = pltpu.make_async_copy(share, view(0, z), own_sem)
    keep.start()
    forward("x", share, view(0, z), 0)
    forward("y", share, view(0, z), 1)
    own_plane(share, 0)
    yield
    sent(view(1, z), plane_recv.at[0])
    forward("y", part(1, far), part(1, far), 3)
    own_plane(view(1, z), 1)
    yield
    sent(view(2, z), plane_recv.at[1])
    forward("x", part(2, near), part(2, near), 2)
    own_plane(view(2, z), 2)
    yield
    for distance in range(1, PLANES):
        for kind in range(4):
            if distance == 1 and kind == 3:
                sent(part(3, near), plane_recv.at[2])
                sent(part(3, far), plane_recv.at[3])
                own_plane(view(3, z), 3)
                yield
            yield from place.steps_at(distance, functools.partial(line, kind))
    keep.wait()
    for plane in range(PLANES):
        for kind in range(4):
            sent(view(kind, plane, 1 - core), core_recv.at[kind, plane])
    yield
    for number, sent_part in enumerate((share, share, share.at[near], share.at[far])):
        sent(sent_part, plane_send.at[number])
    for plane in range(PLANES):
        for kind in range(4):
            sent(share, core_send.at[kind, plane])
            up, down = line_send.at[0, kind, plane], line_send.at[1, kind, plane]
            pl.when((plane <= z) & place.above)(functools.partial(sent, share, up))
            pl.when((plane >= z) & place.below)(functools.partial(sent, share, down))
    yield


def half_shapes(one):
    return [tuple(len(range(*cut.indices(size))) for cut, size in zip(half, one)) for half in halves(one)]


def scatter_scratch(one):
    near, far = half_shapes(one)
    line = pltpu.VMEM((PLANES, *one), LOW)
    buffers = [
        pltpu.VMEM((4, PLANES, *one), LOW),
        line,
        line,
        pltpu.VMEM((PLANES, *near), LOW),
        pltpu.VMEM((PLANES, *far), LOW),
        line,
        line,
        pltpu.VMEM(one, WIDE),
    ]
    return buffers + [dma_grid(6, PLANES), dma_grid(6, PLANES), dma_grid(4, PLANES), dma_grid(4, PLANES)]


def from_other_core(place, parts, mine, core_send, core_recv, between=None):
    def start(plane):
        for kind in (3, 1, 2, 0):
            send(
                parts.at[place.slot(kind, plane, 1 - place.core)],
                mine.at[kind, plane],
                core_send.at[kind, plane],
                core_recv.at[kind, plane],
                place.targets["core"],
            )

    if between is None:
        for step in range(PLANES):
            place.at(PLANES - 1 - step, lambda sign, plane: start(plane))
    else:
        start(place.others[2])
        start(place.others[1])
        between()
        start(place.others[0])
        start(place.z)


def scatter_steps(place, parts, total, scratch, between=None):
    mine, by_x, by_y, diagonal_x, diagonal_y, line_up, line_down, wide, *sems = scratch
    link_send, link_recv, core_send, core_recv = sems
    near, far = halves(parts.shape)
    z, core, last = place.z, place.core, PLANES - 1

    def own(kind, plane):
        return parts[place.slot(kind, plane, core)]

    def forward(name, source, target, number, plane):
        send(source, target, link_send.at[number, plane], link_recv.at[number, plane], place.targets[name])

    def arrived(view, number, plane):
        sent(view, link_recv.at[number, plane])

    def from_core(kind, plane):
        sent(mine.at[kind, plane], core_recv.at[kind, plane])

    def diagonal(sign, plane):
        from_core(3, plane)
        mine[3, plane] += own(3, plane)
        forward("x", mine.at[(3, plane, *near)], diagonal_x.at[plane], 0, plane)
        forward("y", mine.at[(3, plane, *far)], diagonal_y.at[plane], 1, plane)

    def side_x(sign, plane):
        from_core(1, plane)
        mine[1, plane] += own(1, plane)
        arrived(diagonal_y.at[plane], 1, plane)
        mine[(1, plane, *far)] += diagonal_y[plane]
        forward("x", mine.at[1, plane], by_x.at[plane], 2, plane)

    def side_y(sign, plane):
        from_core(2, plane)
        mine[2, plane] += own(2, plane)
        arrived(diagonal_x.at[plane], 0, plane)
        mine[(2, plane, *near)] += diagonal_x[plane]
        forward("y", mine.at[2, plane], by_y.at[plane], 3, plane)

    def column(sign, plane):
        from_core(0, plane)
        arrived(by_x.at[plane], 2, plane)
        arrived(by_y.at[plane], 3, plane)
        wide[...] = (own(0, plane).astype(WIDE) + mine[0, plane].astype(WIDE)) + (
            by_x[plane].astype(WIDE) + by_y[plane].astype(WIDE)
        )

        def add(line, number):
            arrived(line.at[plane], number, plane)
            wide[...] += line[plane].astype(WIDE)

        if sign >= 0:
            pl.when(place.below)(lambda: add(line_up, 4))
        if sign <= 0:
            pl.when(place.above)(lambda: add(line_down, 5))
        if sign == 0:
            total[...] = wide[...]
        else:
            mine[0, plane] = wide[...].astype(LOW)
        if sign > 0:
            forward("up", mine.at[0, plane], line_up.at[plane], 4, plane)
        if sign < 0:
            forward("down", mine.at[0, plane], line_down.at[plane], 5, plane)

    from_other_core(place, parts, mine, core_send, core_recv, between)
    yield
    for step in range(PLANES + 2):
        for stage, lag in ((diagonal, 0), (side_x, 1), (side_y, 1), (column, 2)):
            if 0 <= step - lag < PLANES:
                yield from place.steps_at(last - (step - lag), stage)
    for plane in range(PLANES):
        for kind in range(4):
            sent(mine.at[kind, plane], core_send.at[kind, plane])
        views = (diagonal_x.at[plane], diagonal_y.at[plane], by_x.at[plane], by_y.at[plane])
        for number, part in enumerate(views):
            sent(part, link_send.at[number, plane])
        pl.when(plane > z)(lambda: sent(mine.at[0, plane], link_send.at[4, plane]))
        pl.when(plane < z)(lambda: sent(mine.at[0, plane], link_send.at[5, plane]))
    yield


def line_share_sems():
    return [dma_grid(3), dma_grid(3)]


def line_share_steps(place, buffer, sems):
    line_send, line_recv = sems
    own = buffer.at[place.z]
    for turn in range(3):
        send(own, own, line_send.at[turn], line_recv.at[turn], place.targets[turn])
    yield
    for turn, plane in enumerate(place.others):
        sent(buffer.at[plane], line_recv.at[turn])
    for turn in range(3):
        sent(own, line_send.at[turn])
    yield


def small_gather_sems():
    return [dma_grid(3), dma_grid(3), dma_grid(3), dma_grid(3), pltpu.SemaphoreType.DMA, pltpu.SemaphoreType.DMA]


def small_gather(place, share, whole, sems):
    line_send, line_recv, plane_send, plane_recv, core_send, core_recv = sems
    here, core = place.chip(0), place.core
    whole[place.z, here, core] = share
    own = whole.at[place.z, here, core]
    for turn in range(3):
        send(own, own, line_send.at[turn], line_recv.at[turn], place.targets[turn])
    for turn, plane in enumerate(place.others):
        sent(whole.at[plane, here, core], line_recv.at[turn])
    column = whole.at[:, here, core]
    names = ("x", "y", "diagonal")
    for turn, name in enumerate(names):
        send(column, column, plane_send.at[turn], plane_recv.at[turn], place.targets[name])
    for turn in range(3):
        sent(whole.at[:, place.chip(turn + 1), core], plane_recv.at[turn])
    mine = whole.at[:, :, core]
    send(mine, mine, core_send, core_recv, place.targets["core"])
    sent(whole.at[:, :, 1 - core], core_recv)
    for turn in range(3):
        sent(own, line_send.at[turn])
        sent(column, plane_send.at[turn])
    sent(mine, core_send)


def plane_gather_sems():
    return [dma_grid(4, PLANES), dma_grid(4, PLANES), dma_grid(5, PLANES), dma_grid(5, PLANES)]


def plane_gather_steps(place, whole, sems):
    plane_send, plane_recv, core_send, core_recv = sems
    near, far = halves(whole.shape)
    core = place.core

    def view(kind, part, whose=None):
        whose = core if whose is None else whose
        if kind >= 3:
            return whole.at[(place.slot(3, part, whose), *(near if kind == 3 else far))]
        return whole.at[place.slot(kind, part, whose)]

    def forward(name, view, number, part):
        send(view, view, plane_send.at[number, part], plane_recv.at[number, part], place.targets[name])

    def to_core(kind, part):
        here = view(kind, part)
        send(here, here, core_send.at[kind, part], core_recv.at[kind, part], place.targets["core"])

    def start(part):
        forward("x", view(0, part), 0, part)
        forward("y", view(0, part), 1, part)
        to_core(0, part)

    def side(kind, part):
        sent(view(kind, part), plane_recv.at[kind - 1, part])
        half = whole.at[(place.slot(kind, part, core), *(far if kind == 1 else near))]
        forward("y" if kind == 1 else "x", half, 3 if kind == 1 else 2, part)
        to_core(kind, part)

    def diagonal(kind, part):
        sent(view(kind, part), plane_recv.at[kind - 1, part])
        to_core(kind, part)

    for part in range(PLANES):
        start(part)
        yield
    for step in range(PLANES + 2):
        for stage, kind, lag in ((side, 1, 0), (side, 2, 0), (diagonal, 3, 1), (diagonal, 4, 1)):
            if 0 <= step - lag < PLANES:
                stage(kind, step - lag)
                yield
        if step >= 2:
            part = step - 2
            for kind in range(5):
                sent(view(kind, part, 1 - core), core_recv.at[kind, part])
            yield part
    for part in range(PLANES):
        for kind in range(5):
            sent(view(kind, part), core_send.at[kind, part])
        for number, kind in enumerate((0, 0, 3, 4)):
            sent(view(kind, part), plane_send.at[number, part])
    yield


def plane_scatter_scratch(one):
    near, far = half_shapes(one)
    single = pltpu.VMEM(one, LOW)
    buffers = [pltpu.VMEM((4, *one), LOW), pltpu.VMEM(near, LOW), pltpu.VMEM(far, LOW), single, single]
    return buffers + [dma_grid(4), dma_grid(4), dma_grid(4), dma_grid(4)]


def plane_scatter_steps(place, parts, total, rows, scratch):
    mine, diagonal_x, diagonal_y, by_x, by_y, plane_send, plane_recv, core_send, core_recv = scratch
    near, far = halves(parts.shape)
    core = place.core

    def forward(name, source, target, number):
        send(source, target, plane_send.at[number], plane_recv.at[number], place.targets[name])

    def from_core(kind):
        sent(mine.at[kind], core_recv.at[kind])

    def own(kind):
        return parts[place.chip(kind) * 2 + core]

    for kind in (3, 1, 2, 0):
        source = parts.at[place.chip(kind) * 2 + 1 - core]
        send(source, mine.at[kind], core_send.at[kind], core_recv.at[kind], place.targets["core"])
    yield
    from_core(3)
    mine[3] += own(3)
    forward("x", mine.at[(3, *near)], diagonal_x, 0)
    forward("y", mine.at[(3, *far)], diagonal_y, 1)
    yield
    from_core(1)
    mine[1] += own(1)
    sent(diagonal_y, plane_recv.at[1])
    mine[(1, *far)] += diagonal_y[...]
    forward("x", mine.at[1], by_x, 2)
    yield
    from_core(2)
    mine[2] += own(2)
    sent(diagonal_x, plane_recv.at[0])
    mine[(2, *near)] += diagonal_x[...]
    forward("y", mine.at[2], by_y, 3)
    yield
    from_core(0)
    here = own(0).astype(WIDE) + mine[0].astype(WIDE)
    sent(by_x, plane_recv.at[2])
    sent(by_y, plane_recv.at[3])
    total[rows] = here + (by_x[...].astype(WIDE) + by_y[...].astype(WIDE))
    yield
    for kind in range(4):
        sent(mine.at[kind], core_send.at[kind])
    for number, part in enumerate((diagonal_x, diagonal_y, by_x, by_y)):
        sent(part, plane_send.at[number])
    yield


def run_in_order(runs, order):
    for place in order:
        next(runs[place])
    assert all(next(run, "end") == "end" for run in runs)


def run_together(runs):
    runs = list(runs)
    while runs:
        for run in list(runs):
            if run in runs and next(run, "end") == "end":
                runs = [other for other in runs if other is not run]


IN_ROW, OUT_ROW, PROJ_ROW, VECTOR_ROW = 0, 64, 128, 64


def weight(slabs, row, height=16):
    part = slabs[:, row : row + height, :]
    return part.reshape(part.shape[0] * height, part.shape[2])


def vectors_of(slabs, row=VECTOR_ROW):
    return jnp.sum(slabs[:, row : row + 16, :].astype(WIDE), 0)


def pick_matrix(rows, columns, step, kind=LOW):
    row = lax.broadcasted_iota(jnp.int32, (rows, columns), 0)
    column = lax.broadcasted_iota(jnp.int32, (rows, columns), 1)
    return ((column >= row * step) & (column < (row + 1) * step)).astype(kind)


def every_slot(by_entry, slots):
    return jnp.concatenate([by_entry] * slots, 0)


def dot_wide(left, right, dims):
    return lax.dot_general(
        left, right, ((dims[:1], dims[1:]), ((), ())), precision=lax.Precision.HIGHEST, preferred_element_type=WIDE
    )


def normalize(values):
    center = values - jnp.mean(values, -1, keepdims=True)
    scale = lax.rsqrt(jnp.mean(center * center, -1, keepdims=True) + EPSILON)
    return center * scale, scale


def normalize_back(grad, gain, unit, scale):
    inner = grad * gain
    back = inner - jnp.mean(inner, -1, keepdims=True) - unit * jnp.mean(inner * unit, -1, keepdims=True)
    return back * scale, jnp.sum(grad * unit, 0, keepdims=True), jnp.sum(grad, 0, keepdims=True)


GELU_A, GELU_B = (2.0 / 3.141592653589793) ** 0.5, 0.044715


def gelu_tanh(values):
    return jnp.tanh(GELU_A * (values + GELU_B * values * values * values))


def head_matrix(width):
    return pick_matrix(128, width, width // HYP_HEADS)


def lengths_column(row):
    shape = (row.shape[1], row.shape[1])
    same = lax.broadcasted_iota(jnp.int32, shape, 0) == lax.broadcasted_iota(jnp.int32, shape, 1)
    return jnp.sum(jnp.where(same, row.astype(WIDE), 0.0), 1, keepdims=True)


def hyper_forward_kernel(dense, rest, rows_ref, lengths_ref, *refs):
    hyper_forward_body(dense, rest, rows_ref, lengths_column(lengths_ref[...]), *refs)


def hyper_forward_body(
    dense, rest, rows_ref, lengths, pooled_ref, normed_ref, query_ref, key_ref, value_ref, probs_ref, heads_ref, resid_ref, pre_ref
):
    count, width = rows_ref.shape
    entries = pooled_ref.shape[0]
    slots = count // entries
    vectors = vectors_of(rest)
    slot_rows = rows_ref[...]
    unit, _ = normalize(slot_rows)
    normed = (unit * vectors[0:1] + vectors[2:3]).astype(LOW)
    normed_ref[...] = normed
    query = dot(normed[:entries], weight(rest, 0), (1, 0)).astype(LOW)
    key = dot(normed, weight(rest, 16), (1, 0)).astype(LOW)
    value = dot(normed, weight(rest, 32), (1, 0)).astype(LOW)
    query_ref[...], key_ref[...], value_ref[...] = query, key, value
    heads = head_matrix(width)
    product = every_slot(query.astype(WIDE), slots) * key.astype(WIDE)
    scores = dot_wide(product, heads.astype(WIDE), (1, 1)) * (width // HYP_HEADS) ** (-0.5)
    lengths = every_slot(jnp.broadcast_to(lengths, (entries, 128)), slots).reshape(slots, entries, 128)
    slot = lax.broadcasted_iota(jnp.int32, (slots, entries, 128), 0).astype(WIDE)
    scores = jnp.where(slot < lengths, scores.reshape(slots, entries, 128), MASKED)
    grown = jnp.exp(scores - jnp.max(scores, 0, keepdims=True))
    probs = (grown / jnp.sum(grown, 0, keepdims=True)).reshape(count, 128)
    probs_ref[...] = probs
    weighted = dot(probs.astype(LOW), heads, (1, 0)) * value.astype(WIDE)
    heads_out = jnp.sum(weighted.reshape(slots, entries, width), 0).astype(LOW)
    heads_ref[...] = heads_out
    residual = slot_rows[:entries] + dot(heads_out, weight(rest, 48), (1, 0))
    resid_ref[...] = residual
    unit, _ = normalize(residual)
    normed_two = (unit * vectors[1:2] + vectors[3:4]).astype(LOW)
    out = residual + vectors[4:5]
    out_weight = weight(dense, OUT_ROW, 64)
    for turn in range(4):
        pre = dot(normed_two, weight(dense, IN_ROW + 16 * turn), (1, 0)) + vectors[5 + turn : 6 + turn]
        pre_ref[turn] = pre
        act = (0.5 * pre * (1.0 + gelu_tanh(pre))).astype(LOW)
        out += dot(act, out_weight[turn * width : (turn + 1) * width], (1, 0))
    pooled_ref[...] = out.astype(LOW)


def forward_shapes(entries, count, width):
    shapes = [
        ((entries, width), LOW),
        ((count, width), LOW),
        ((entries, width), LOW),
        ((count, width), LOW),
        ((count, width), LOW),
        ((count, 128), WIDE),
        ((entries, width), LOW),
        ((entries, width), WIDE),
        ((4, entries, width), WIDE),
    ]
    return [jax.ShapeDtypeStruct(shape, kind) for shape, kind in shapes]


def hyper_forward(dense, rest, slot_rows, lengths, entries):
    return pl.pallas_call(
        hyper_forward_kernel,
        out_shape=forward_shapes(entries, *slot_rows.shape),
        compiler_params=pltpu.CompilerParams(vmem_limit_bytes=VMEM_LIMIT),
        name="hyper_forward",
    )(dense, rest, slot_rows, lengths)


def project_rows(pooled, proj, vectors, gain, rows_ref, normed_ref):
    width = pooled.shape[1]
    square = 0.0
    for turn in range(4):
        columns = slice(turn * width, (turn + 1) * width)
        rows = dot(pooled, weight(proj, PROJ_ROW + 16 * turn), (1, 0)) + vectors[9 + turn : 10 + turn]
        rows = rows.astype(LOW)
        rows_ref[:, columns] = rows
        rows = rows.astype(WIDE)
        square += jnp.sum(rows * rows, -1, keepdims=True)
    scale = lax.rsqrt(square / (4 * width) + EPSILON)
    normed_ref[...] = (rows_ref[...].astype(WIDE) * scale * gain.astype(WIDE)).astype(LOW)


def project_kernel(pooled_ref, dense_ref, rest_ref, gain_ref, rows_ref, normed_ref):
    project_rows(pooled_ref[...], dense_ref, vectors_of(rest_ref), gain_ref[0:1], rows_ref, normed_ref)


def project(pooled, dense, rest, gain):
    entries, width = pooled.shape
    block = min(entries, 512)
    out_block = pl.BlockSpec((block, 4 * width), lambda i: (i, 0))
    result = jax.ShapeDtypeStruct((entries, 4 * width), LOW)
    in_vmem = pl.BlockSpec(memory_space=pltpu.VMEM)
    return pl.pallas_call(
        project_kernel,
        grid=(entries // block,),
        in_specs=[pl.BlockSpec((block, width), lambda i: (i, 0)), in_vmem, in_vmem, in_vmem],
        out_specs=[out_block, out_block],
        out_shape=[result, result],
        compiler_params=pltpu.CompilerParams(vmem_limit_bytes=VMEM_LIMIT),
        name="project",
    )(pooled, dense, rest, gain)


def pick_tokens(entries, core, own_ids, got_ids):
    left = jnp.where(core == 0, own_ids, got_ids)
    right = jnp.where(core == 0, got_ids, own_ids)
    entry = lax.broadcasted_iota(jnp.int32, (entries, own_ids.shape[1]), 0)
    return jnp.concatenate([(entry == left).astype(LOW), (entry == right).astype(LOW)], 1)


def first_kernel(
    gains_ref, biases_ref, attn_ref, in_ref, in_bias_ref, out_ref, proj_ref, proj_bias_ref, ids_ref, table_ref, lengths_ref, gain_ref,
    own_ids_ref, got_ids_ref, dy_ref, down_ref, query_ref, kv_ref,
    dense_out, rest_out, column_out, d_act_out, rows_out, inputs_out, qkv_out,
    dense, rest, dense_share, rest_share, parts, slot_rows, pooled_ref, normed_ref, q_ref, k_ref, v_ref, probs_ref, heads_ref, resid_ref, pre_ref,
    column_all, pooled_all, dy_all, down_buffer, act_buffer, query_weight, kv_weight, rows, normed, inputs,
    qkv, load_sems, down_sems, act_sems, out_sems, dy_send, dy_recv, *refs
):
    place = Place()
    own = lax.axis_index("dp") * 2 + place.core
    width = dense.shape[2]

    def load(source, target, number):
        copy = pltpu.make_async_copy(source, target, load_sems.at[number])
        copy.start()
        return copy

    units = down_ref.shape[0]

    def load_down(step):
        here = pl.ds(step * UNIT_BLOCK, UNIT_BLOCK)
        copy = pltpu.make_async_copy(down_ref.at[here], down_buffer.at[step % 2], down_sems.at[step % 2])
        copy.start()
        return copy

    own_dy = load(dy_ref, dy_all.at[0], 0)
    down_copy = load_down(0)
    weight_loads = [load(query_ref, query_weight, 1), load(kv_ref, kv_weight, 2)]

    rest_share[0:64] = attn_ref[...].reshape(64, width)
    for turn in range(4):
        columns = slice(turn * width, (turn + 1) * width)
        dense_share[IN_ROW + 16 * turn : IN_ROW + 16 * turn + 16] = in_ref[:, columns]
        dense_share[PROJ_ROW + 16 * turn : PROJ_ROW + 16 * turn + 16] = proj_ref[:, columns]
    dense_share[OUT_ROW : OUT_ROW + 64] = out_ref[...]

    def spread(values, length):
        count = values.shape[1]
        row = lax.broadcasted_iota(jnp.int32, (count, length), 0)
        lane = lax.broadcasted_iota(jnp.int32, (count, length), 1)
        return dot(values, (lane - own * count == row).astype(LOW), (1, 0))

    def by_rows(flat):
        return [flat[:, turn * width : (turn + 1) * width] for turn in range(4)]

    vectors = [spread(gains_ref[...], width), spread(biases_ref[...], width)]
    vectors += by_rows(spread(in_bias_ref[...], 4 * width)) + by_rows(spread(proj_bias_ref[...], 4 * width))
    vectors.append(jnp.zeros((3, width), WIDE))
    rest_share[VECTOR_ROW : VECTOR_ROW + 16] = jnp.concatenate(vectors, 0).astype(LOW)

    place.greet()
    send(dy_ref, dy_all.at[1], dy_send, dy_recv, place.targets["core"])
    dense_sems, rest_sems, small_sems, line_sems, slot_scratch = refs[:5], refs[5:12], refs[12:18], refs[18:20], refs[20:]
    pieces = table_ref.shape[0]
    groups, height = parts.shape[0], parts.shape[1] // ids_ref.shape[0]
    chunk = ids_ref.shape[1]

    def slot_steps():
        across = lax.broadcasted_iota(jnp.int32, (chunk, chunk), 1)
        down = lax.broadcasted_iota(jnp.int32, (chunk, chunk), 0)
        piece = lax.broadcasted_iota(jnp.int32, (chunk, pieces), 1).astype(WIDE) + (own * pieces).astype(WIDE)
        for turn in range(ids_ref.shape[0]):
            ids = ids_ref[turn : turn + 1].astype(WIDE)
            column = jnp.sum(jnp.where(across == down, ids, 0.0), 1, keepdims=True)
            found = dot((piece == column).astype(LOW), table_ref[...], (1, 0)).astype(LOW)
            parts[:, turn * height : (turn + 1) * height, :] = found.reshape(groups, height, width)
            yield
        yield from scatter_steps(place, parts, slot_rows, slot_scratch)

    def act_steps():
        nonlocal down_copy
        own_dy.wait()
        sent(dy_all.at[1], dy_recv)
        copies = []
        for step in range(units // UNIT_BLOCK):
            down_copy.wait()
            if (step + 1) * UNIT_BLOCK < units:
                down_copy = load_down(step + 1)
            if step >= 2:
                copies[step - 2].wait()
            tokens = dy_all[...].reshape(-1, dy_all.shape[2])
            act_buffer[step % 2] = dot(tokens, down_buffer[step % 2], (1, 1)).astype(LOW)
            here = pl.ds(step * UNIT_BLOCK, UNIT_BLOCK)
            copy = pltpu.make_async_copy(act_buffer.at[step % 2], d_act_out.at[:, here], act_sems.at[step % 2])
            copy.start()
            copies.append(copy)
            if len(copies) * UNIT_BLOCK == units:
                copies[-2].wait()
                copies[-1].wait()
                sent(dy_ref, dy_send)
            yield

    runs = [
        gather_steps(place, dense_share, dense, dense_sems),
        late_gather_steps(place, rest_share, rest, rest_sems),
        slot_steps(),
        act_steps(),
    ]
    run_in_order(runs, FIRST_ORDER)

    def store(source, target, number):
        copy = pltpu.make_async_copy(source, target, out_sems.at[number])
        copy.start()
        return copy

    stores = [store(dense, dense_out, 0), store(rest, rest_out, 1)]
    hyper_forward_body(
        dense, rest, slot_rows, lengths_column(lengths_ref[...]), pooled_ref, normed_ref, q_ref, k_ref, v_ref, probs_ref, heads_ref, resid_ref, pre_ref
    )
    small_gather(place, pooled_ref[...], pooled_all, small_sems)
    slot_count = parts.shape[1]
    column_all[place.z, :slot_count] = slot_rows[...].astype(LOW)
    lane = lax.broadcasted_iota(jnp.int32, (lengths_ref.shape[1], width), 1)
    row = lax.broadcasted_iota(jnp.int32, (lengths_ref.shape[1], width), 0)
    spread_lengths = dot(lengths_ref[...].astype(WIDE).astype(LOW), (lane == row).astype(LOW), (1, 0))
    column_all[place.z, slot_count:] = jnp.broadcast_to(spread_lengths, (16, width)).astype(LOW)
    column_run = line_share_steps(place, column_all, line_sems)
    next(column_run)
    pooled = pooled_all[...].reshape(-1, width)
    project_rows(pooled, dense, vectors_of(rest), gain_ref[0:1], rows, normed)
    stores.append(store(rows, rows_out, 2))

    entries = rows.shape[0]
    kv_width = HEAD_DIM * (KV_HEADS // 2)
    kv_columns = pl.ds(pl.multiple_of(place.core * kv_width, kv_width), kv_width)
    local = own_ids_ref.shape[1]
    pick = pick_tokens(entries, place.core, own_ids_ref[...], got_ids_ref[...])
    q_width = query_weight.shape[1]
    for copy in weight_loads:
        copy.wait()
    for start in range(0, q_width, 256):
        found = dot(normed[...], query_weight[:, start : start + 256], (1, 0)).T.astype(LOW)
        qkv[start : start + 256] = dot(found, pick, (1, 0)).astype(LOW)
    for which in range(2):
        start = q_width + which * kv_width
        found = dot(normed[...], kv_weight[which, :, kv_columns], (1, 0)).T.astype(LOW)
        qkv[start : start + kv_width] = dot(found, pick, (1, 0)).astype(LOW)
    stores.append(store(qkv, qkv_out, 3))
    own_pick = (lax.broadcasted_iota(jnp.int32, (entries, local), 0) == own_ids_ref[...]).astype(LOW)
    inputs[...] = dot(own_pick, rows[...], (0, 0)).astype(LOW)
    stores.append(store(inputs, inputs_out, 4))
    next(column_run)
    stores.append(store(column_all, column_out, 5))
    for copy in stores:
        copy.wait()


def first_exchange(weights, ids, table, lengths, gains, own_ids, got_ids, dy, down, query, kv, number):
    devices = 8 * PLANES
    width = table.shape[1]
    slots = ids.size // devices
    entries = lengths.shape[1]
    local, d_model = dy.shape
    seq_len = 2 * local
    features = query.shape[1] + kv.shape[2]
    units = down.shape[0]
    one = (slots, width)
    in_vmem, anywhere = pl.BlockSpec(memory_space=pltpu.VMEM), pl.BlockSpec(memory_space=pl.ANY)
    all_rows = devices * entries
    dense, rest = (devices, DENSE_ROWS, width), (devices, REST_ROWS, width)
    kept = forward_shapes(entries, slots, width)
    column = (PLANES, slots + 16, width)
    dma = pltpu.SemaphoreType.DMA
    return pl.pallas_call(
        first_kernel,
        in_specs=[in_vmem] * 14 + [anywhere] * 4,
        out_specs=[anywhere] * 7,
        out_shape=[
            jax.ShapeDtypeStruct(dense, LOW),
            jax.ShapeDtypeStruct(rest, LOW),
            jax.ShapeDtypeStruct(column, LOW),
            jax.ShapeDtypeStruct((2 * local, units), LOW),
            jax.ShapeDtypeStruct((all_rows, d_model), LOW),
            jax.ShapeDtypeStruct((local, d_model), LOW),
            jax.ShapeDtypeStruct((features, seq_len), LOW),
        ],
        scratch_shapes=[
            pltpu.VMEM(dense, LOW),
            pltpu.VMEM(rest, LOW),
            pltpu.VMEM(dense[1:], LOW),
            pltpu.VMEM(rest[1:], LOW),
            pltpu.VMEM((devices, *one), LOW),
            pltpu.VMEM(one, WIDE),
        ]
        + [pltpu.VMEM(array.shape, array.dtype) for array in kept]
        + [
            pltpu.VMEM(column, LOW),
            pltpu.VMEM((PLANES, 4, 2, entries, width), LOW),
            pltpu.VMEM((2, local, d_model), LOW),
            pltpu.VMEM((2, UNIT_BLOCK, d_model), LOW),
            pltpu.VMEM((2, 2 * local, UNIT_BLOCK), LOW),
            pltpu.VMEM(query.shape, LOW),
            pltpu.VMEM(kv.shape, LOW),
            pltpu.VMEM((all_rows, d_model), LOW),
            pltpu.VMEM((all_rows, d_model), LOW),
            pltpu.VMEM((local, d_model), LOW),
            pltpu.VMEM((features, seq_len), LOW),
            dma((3,)),
            dma((2,)),
            dma((2,)),
            dma((6,)),
            dma,
            dma,
        ]
        + gather_sems()
        + late_gather_sems()
        + small_gather_sems()
        + line_share_sems()
        + scatter_scratch(one),
        compiler_params=pltpu.CompilerParams(
            collective_id=number, has_side_effects=True, vmem_limit_bytes=VMEM_LIMIT
        ),
        name="first_exchange",
    )(*weights, ids, table, lengths, gains, own_ids, got_ids, dy, down, query, kv)


def greet_core(place):
    barrier = pltpu.get_barrier_semaphore()
    pl.semaphore_signal(barrier, inc=1, device_id=place.targets["core"], device_id_type=pl.DeviceIdType.MESH)
    pl.semaphore_wait(barrier, 1)


def started(source, target, sem):
    copy = pltpu.make_async_copy(source, target, sem)
    copy.start()
    return copy


def middle_kernel(
    own_hbm, other_hbm, weight_hbm, inputs_hbm, gains_ref, hidden_hbm, x_own_hbm, x_other_hbm, own, other, weight, inputs, partial, got, hidden,
    x_own, x_got, load_sems, tile_sems, send_sems, recv_sems, row_send_sems, row_recv_sems, out_sems
):
    place = Place()
    tokens, width = inputs.shape
    tiles = [slice(start, start + width // 4) for start in range(0, width, width // 4)]
    blocks = [slice(start, start + tokens // 4) for start in range(0, tokens, tokens // 4)]
    load_other = started(other_hbm, other, load_sems.at[0])
    weights = [started(weight_hbm.at[:, tile], weight.at[:, tile], tile_sems.at[n]) for n, tile in enumerate(tiles)]
    loads = [started(own_hbm, own, load_sems.at[1]), started(inputs_hbm, inputs, load_sems.at[2])]
    greet_core(place)
    target = place.targets["core"]
    load_other.wait()
    for number, tile in enumerate(tiles):
        weights[number].wait()
        partial[:, tile] = dot(other[...], weight[:, tile], (0, 0)).astype(LOW)
        send(partial.at[:, tile], got.at[:, tile], send_sems.at[number], recv_sems.at[number], target)
    for copy in loads:
        copy.wait()
    gain = gains_ref[1:2].astype(WIDE)
    stores = []
    for number, rows in enumerate(blocks):
        here = dot(own[:, rows], weight[...], (0, 0)) + inputs[rows].astype(WIDE)
        if number == 0:
            for turn, tile in enumerate(tiles):
                sent(got.at[:, tile], recv_sems.at[turn])
        here += got[rows].astype(WIDE)
        hidden[rows] = here
        stores.append(started(hidden.at[rows], hidden_hbm.at[rows], out_sems.at[0, number]))
        x_own[rows] = (here * lax.rsqrt(jnp.mean(here * here, -1, keepdims=True) + EPSILON) * gain).astype(LOW)
        send(x_own.at[rows], x_got.at[rows], row_send_sems.at[number], row_recv_sems.at[number], target)
        stores.append(started(x_own.at[rows], x_own_hbm.at[rows], out_sems.at[1, number]))
    for number, rows in enumerate(blocks):
        sent(x_got.at[rows], row_recv_sems.at[number])
        stores.append(started(x_got.at[rows], x_other_hbm.at[rows], out_sems.at[2, number]))
    for copy in stores:
        copy.wait()
    for number in range(4):
        sent(partial.at[:, tiles[number]], send_sems.at[number])
        sent(x_own.at[blocks[number]], row_send_sems.at[number])


def middle(heads_own, heads_other, weight, inputs, gains, number):
    in_vmem, anywhere = pl.BlockSpec(memory_space=pltpu.VMEM), pl.BlockSpec(memory_space=pl.ANY)
    tokens = pltpu.VMEM(inputs.shape, LOW)
    low = jax.ShapeDtypeStruct(inputs.shape, LOW)
    return pl.pallas_call(
        middle_kernel,
        in_specs=[anywhere] * 4 + [in_vmem],
        out_specs=[anywhere] * 3,
        out_shape=[jax.ShapeDtypeStruct(inputs.shape, WIDE), low, low],
        scratch_shapes=[
            pltpu.VMEM(heads_own.shape, LOW),
            pltpu.VMEM(heads_own.shape, LOW),
            pltpu.VMEM(weight.shape, LOW),
            tokens,
            tokens,
            tokens,
            pltpu.VMEM(inputs.shape, WIDE),
            tokens,
            tokens,
            dma_grid(3),
            dma_grid(4),
            dma_grid(4),
            dma_grid(4),
            dma_grid(4),
            dma_grid(4),
            dma_grid(3, 4),
        ],
        compiler_params=pltpu.CompilerParams(
            collective_id=number, has_side_effects=True, vmem_limit_bytes=VMEM_LIMIT
        ),
        name="middle",
    )(heads_own, heads_other, weight, inputs, gains)


def turn_kernel(
    hidden_hbm, dy_hbm, back_own_hbm, back_got_hbm, weight_hbm, gains_ref, grad_hbm, heads_own_hbm, heads_other_hbm, hidden, loaded, grad, got,
    weight, heads, load_sems, weight_sem, send_sems, recv_sems, out_sems
):
    place = Place()
    tokens, width = grad.shape
    count = hidden.shape[0]
    blocks = [slice(n * hidden.shape[1], (n + 1) * hidden.shape[1]) for n in range(count)]
    sources = (dy_hbm, back_own_hbm, back_got_hbm)
    loads = []
    for number, rows in enumerate(blocks):
        loads.append(
            [started(hidden_hbm.at[rows], hidden.at[number], load_sems.at[number, 3])]
            + [started(source.at[rows], loaded.at[number, n], load_sems.at[number, n]) for n, source in enumerate(sources)]
        )
        if number == 1:
            load_weight = started(weight_hbm, weight, weight_sem)
    greet_core(place)
    target = place.targets["core"]
    gain = gains_ref[1:2].astype(WIDE)
    half = tokens // 2
    for number, rows in enumerate(blocks):
        for copy in loads[number]:
            copy.wait()
        here = hidden[number]
        dy, back_own, back_got = (loaded[number, n].astype(WIDE) for n in range(3))
        scale = lax.rsqrt(jnp.mean(here * here, -1, keepdims=True) + EPSILON)
        inner = (back_own + back_got) * gain
        back = scale * inner - here * (scale * scale * scale * jnp.mean(here * inner, -1, keepdims=True))
        grad[rows] = (dy + back).astype(LOW)
        send(grad.at[rows], got.at[rows], send_sems.at[number], recv_sems.at[number], target)
        if number == count // 2 - 1:
            load_weight.wait()
            heads[0, :, :half] = dot(weight[...], grad[:half], (1, 1)).astype(LOW)
    stores = [started(grad, grad_hbm, out_sems.at[0])]
    heads[0, :, half:] = dot(weight[...], grad[half:], (1, 1)).astype(LOW)
    stores.append(started(heads.at[0], heads_own_hbm, out_sems.at[1]))
    for part in range(2):
        for number in range(part * count // 2, (part + 1) * count // 2):
            sent(got.at[blocks[number]], recv_sems.at[number])
        rows = slice(part * half, (part + 1) * half)
        heads[1, :, rows] = dot(weight[...], got[rows], (1, 1)).astype(LOW)
    stores.append(started(heads.at[1], heads_other_hbm, out_sems.at[2]))
    for copy in stores:
        copy.wait()
    for number, rows in enumerate(blocks):
        sent(grad.at[rows], send_sems.at[number])


def turn_around(hidden, dy, backs, weight, gains, number):
    in_vmem, anywhere = pl.BlockSpec(memory_space=pltpu.VMEM), pl.BlockSpec(memory_space=pl.ANY)
    tokens, width = dy.shape
    count = 4
    block = tokens // count
    heads = (weight.shape[0], tokens)
    return pl.pallas_call(
        turn_kernel,
        in_specs=[anywhere] * 5 + [in_vmem],
        out_specs=[anywhere] * 3,
        out_shape=[
            jax.ShapeDtypeStruct(dy.shape, LOW),
            jax.ShapeDtypeStruct(heads, LOW),
            jax.ShapeDtypeStruct(heads, LOW),
        ],
        scratch_shapes=[
            pltpu.VMEM((count, block, width), WIDE),
            pltpu.VMEM((count, 3, block, width), LOW),
            pltpu.VMEM(dy.shape, LOW),
            pltpu.VMEM(dy.shape, LOW),
            pltpu.VMEM(weight.shape, LOW),
            pltpu.VMEM((2, *heads), LOW),
            dma_grid(count, 4),
            pltpu.SemaphoreType.DMA,
            dma_grid(count),
            dma_grid(count),
            dma_grid(3),
        ],
        compiler_params=pltpu.CompilerParams(
            collective_id=number, has_side_effects=True, vmem_limit_bytes=VMEM_LIMIT
        ),
        name="turn_around",
    )(hidden, dy, *backs, weight, gains)


def outer(left, right):
    return dot(left, right, (0, 0))


def column_sum(values):
    return jnp.sum(values.astype(WIDE), 0, keepdims=True)


def own_part(ref, own, rows=slice(None)):
    if own is None:
        return ref[rows]
    size = ref.shape[1] // PLANES
    return ref[rows, pl.ds(pl.multiple_of(own * size, size), size)]


def back_dense(dense, vectors, rows_low, pooled_ref, residual, pre_ref, normed_ref, act_ref, put, own=None):
    width = pooled_ref.shape[1]
    d_pooled, proj_bias = 0.0, []
    for turn in range(4):
        rows = rows_low[:, turn * width : (turn + 1) * width]
        put(True, PROJ_ROW + 16 * turn, outer(own_part(pooled_ref, own), rows))
        d_pooled += dot(rows, weight(dense, PROJ_ROW + 16 * turn), (1, 1))
        proj_bias.append(column_sum(rows))
    ffn_low = d_pooled.astype(LOW)
    unit, scale = normalize(residual)
    normed_ref[...] = (unit * vectors[1:2] + vectors[3:4]).astype(LOW)
    out_weight = weight(dense, OUT_ROW, 64)
    d_normed, ffn_bias = 0.0, []
    for turn in range(4):
        pre = pre_ref[turn]
        bent = gelu_tanh(pre)
        act_ref[turn] = (0.5 * pre * (1.0 + bent)).astype(LOW)
        slope = 0.5 * (1.0 + bent) + 0.5 * pre * (1.0 - bent * bent) * GELU_A * (1.0 + 3.0 * GELU_B * pre * pre)
        d_act = dot(ffn_low, out_weight[turn * width : (turn + 1) * width], (1, 1))
        pre_low = (d_act * slope).astype(LOW)
        put(True, IN_ROW + 16 * turn, outer(own_part(normed_ref, own), pre_low))
        ffn_bias.append(column_sum(pre_low))
        d_normed += dot(pre_low, weight(dense, IN_ROW + 16 * turn), (1, 1))
    if own is None:
        put(True, OUT_ROW, jnp.concatenate([outer(act_ref[turn], ffn_low).astype(LOW) for turn in range(4)], 0), 64)
    else:
        put(True, OUT_ROW, outer(act_ref[own], ffn_low), 64)
    back, gain, bias = normalize_back(d_normed, vectors[1:2], unit, scale)
    return d_pooled + back, gain, bias, [column_sum(ffn_low)] + ffn_bias + proj_bias


def first_slot_plus(by_slot, by_entry):
    entries = by_entry.shape[0]
    return jnp.concatenate([by_slot[:entries] + by_entry, by_slot[entries:]], 0)


def back_attention(rest, vectors, d_resid, slot_rows, saved, put, own=None):
    normed_ref, query_ref, key_ref, value_ref, probs_ref, heads_ref = saved
    count, width = slot_rows.shape
    entries = query_ref.shape[0]
    slots = count // entries
    scale = (width // HYP_HEADS) ** (-0.5)
    attn_low = d_resid.astype(LOW)
    put(False, 48, outer(own_part(heads_ref, own), attn_low))
    d_heads = dot(attn_low, weight(rest, 48), (1, 1)).astype(LOW)
    heads = head_matrix(width)
    d_heads_all = every_slot(d_heads.astype(WIDE), slots)
    query_all = every_slot(query_ref[...].astype(WIDE), slots)
    probs = probs_ref[...]
    d_probs = dot_wide(d_heads_all * value_ref[...].astype(WIDE), heads.astype(WIDE), (1, 1))
    delta = every_slot(jnp.sum((probs * d_probs).reshape(slots, entries, 128), 0), slots)
    d_scores = dot((probs * (d_probs - delta) * scale).astype(LOW), heads, (1, 0))
    d_value = (dot(probs.astype(LOW), heads, (1, 0)) * d_heads_all).astype(LOW)
    d_key = (d_scores * query_all).astype(LOW)
    d_query = (d_scores * key_ref[...].astype(WIDE)).reshape(slots, entries, width)
    d_query = jnp.sum(d_query, 0).astype(LOW)
    put(False, 0, outer(own_part(normed_ref, own, slice(0, entries)), d_query))
    put(False, 16, outer(own_part(normed_ref, own), d_key))
    put(False, 32, outer(own_part(normed_ref, own), d_value))
    d_normed = dot(d_key, weight(rest, 16), (1, 1)) + dot(d_value, weight(rest, 32), (1, 1))
    d_normed = first_slot_plus(d_normed, dot(d_query, weight(rest, 0), (1, 1)))
    unit, inverse = normalize(slot_rows)
    back, gain, bias = normalize_back(d_normed, vectors[0:1], unit, inverse)
    return first_slot_plus(back, d_resid).astype(LOW), gain, bias


def vector_rows(gain_one, gain_two, bias_one, bias_two, rest):
    rows = [gain_one, gain_two, bias_one, bias_two] + rest
    rows.append(jnp.zeros((16 - len(rows), gain_one.shape[1]), WIDE))
    return jnp.concatenate(rows, 0).astype(LOW)


def hyper_backward_kernel(
    dense, rest, row_grad_ref, rows_ref, pooled_ref, normed_ref, query_ref, key_ref, value_ref, probs_ref, heads_ref, resid_ref, pre_ref,
    dense_grad, rest_grad, slot_ref, normed_two_ref, act_ref
):
    vectors = vectors_of(rest)
    put = putter(dense_grad, rest_grad)
    d_resid, gain_two, bias_two, sums = back_dense(
        dense, vectors, row_grad_ref[...].astype(LOW), pooled_ref, resid_ref[...], pre_ref, normed_two_ref, act_ref, put
    )
    saved = (normed_ref, query_ref, key_ref, value_ref, probs_ref, heads_ref)
    slot_ref[...], gain_one, bias_one = back_attention(rest, vectors, d_resid, rows_ref[...], saved, put)
    put_vectors(rest_grad, vector_rows(gain_one, gain_two, bias_one, bias_two, sums))


def putter(dense_grad, rest_grad):
    def put(in_dense, row, grad, height=16):
        target = dense_grad if in_dense else rest_grad
        target[:, row : row + height, :] = grad.astype(LOW).reshape(target.shape[0], height, target.shape[2])

    return put


def put_vectors(rest_grad, sums):
    rest_grad[:, VECTOR_ROW : VECTOR_ROW + 16, :] = jnp.broadcast_to(sums[None], (rest_grad.shape[0], *sums.shape))


def hyper_backward(dense, rest, row_grad, slot_rows, saved):
    return pl.pallas_call(
        hyper_backward_kernel,
        out_shape=[jax.ShapeDtypeStruct(like.shape, LOW) for like in (dense, rest, slot_rows)],
        scratch_shapes=[pltpu.VMEM(saved[0].shape, LOW), pltpu.VMEM((4, *saved[0].shape), LOW)],
        compiler_params=pltpu.CompilerParams(vmem_limit_bytes=VMEM_LIMIT),
        name="hyper_backward",
    )(dense, rest, row_grad, slot_rows, *saved)


def row_part_steps(place, hbm_refs, refs, ids_refs, gains_ref, weights, row_parts, sems):
    dq_ref, dk_ref, dv_ref, grad_ref, rows_ref, sums_ref = refs
    dq_hbm, dk_hbm, dv_hbm, query_hbm, kv_hbm, grad_hbm, rows_hbm = hbm_refs
    own_ids, got_ids = ids_refs[0][...], ids_refs[1][...]
    entries, d_model = rows_ref.shape
    q_width, kv_width = dq_ref.shape[0], dk_ref.shape[0]
    width = weights.shape[2]
    height = d_model // weights.shape[0]
    kv_columns = pl.ds(pl.multiple_of(place.core * kv_width, kv_width), kv_width)
    copies = [
        started(source, target, sems.at[number])
        for number, (source, target) in enumerate(
            (
                (dq_hbm, dq_ref),
                (dk_hbm, dk_ref),
                (dv_hbm, dv_ref),
                (query_hbm.at[:, :, :width], weights.at[:, 0:height, :]),
                (query_hbm.at[:, :, width:], weights.at[:, height : 2 * height, :]),
                (kv_hbm.at[0, :, :, kv_columns], weights.at[:, 2 * height : 3 * height, 0:kv_width]),
                (kv_hbm.at[1, :, :, kv_columns], weights.at[:, 2 * height : 3 * height, kv_width : 2 * kv_width]),
                (rows_hbm, rows_ref),
                (grad_hbm, grad_ref),
            )
        )
    ]
    yield
    pick = pick_tokens(entries, place.core, own_ids, got_ids)
    for copy in copies[:3]:
        copy.wait()
    sums_ref[:, :q_width] = dot(pick, dq_ref[...], (1, 1)).astype(LOW)
    sums_ref[:, q_width : q_width + kv_width] = dot(pick, dk_ref[...], (1, 1)).astype(LOW)
    sums_ref[:, q_width + kv_width :] = dot(pick, dv_ref[...], (1, 1)).astype(LOW)
    for copy in copies[3:]:
        copy.wait()
    gain = gains_ref[0:1].astype(WIDE)
    block = entries // 2
    group = row_parts.shape[0] // 2
    upper = lax.div(place.z, PLANES // 2)
    for number in (1 - upper, upper):
        here = pl.ds(pl.multiple_of(number * block, block), block)
        first = dot(sums_ref[here, :width], weight(weights, 0, height), (1, 1))
        first += dot(sums_ref[here, width : 2 * width], weight(weights, height, height), (1, 1))
        kv = weights[:, 2 * height : 3 * height, 0 : 2 * kv_width].reshape(d_model, 2 * kv_width)
        first += dot(sums_ref[here, q_width:], kv, (1, 1))
        rows = rows_ref[here].astype(WIDE)
        scale = lax.rsqrt(jnp.mean(rows * rows, -1, keepdims=True) + EPSILON)
        inner = first * gain
        inner = scale * inner - rows * (scale * scale * scale * jnp.mean(rows * inner, -1, keepdims=True))
        entry = lax.broadcasted_iota(jnp.int32, (block, own_ids.shape[1]), 0) + number * block
        own_pick = (entry == own_ids).astype(LOW)
        part = (inner + dot(own_pick, grad_ref[...], (1, 0))).astype(LOW)
        row_parts[pl.ds(number * group, group)] = part.reshape(group, *row_parts.shape[1:])
        yield


def last_kernel(
    dq_hbm, dk_hbm, dv_hbm, query_hbm, kv_hbm, grad_hbm, new_rows_hbm, own_ids_ref, got_ids_ref, gains_ref, ids_ref, dense_hbm, rest_hbm,
    *refs
):
    column_hbm, refs = refs[0], refs[1:]
    row_grad, dense_total, rest_total, table_grad, dense, rest, in_grad, out_grad, proj_grad, rest_grad, *refs = refs
    kept, refs = refs[:10], refs[10:]
    slot_all, rows_low, normed_two, acts, load_sems, dq_ref, dk_ref, dv_ref, grad_ref, new_rows_ref, sums_ref, row_parts, row_sems, column, *refs = refs
    row_scratch, refs = refs[:12], refs[12:]
    plane_scratch = [refs[9 * turn : 9 * turn + 9] for turn in range(4)]
    slot_sems, line_sems = refs[36:40], refs[40:42]
    place = Place()
    row_run = row_part_steps(
        place,
        (dq_hbm, dk_hbm, dv_hbm, query_hbm, kv_hbm, grad_hbm, new_rows_hbm),
        (dq_ref, dk_ref, dv_ref, grad_ref, new_rows_ref, sums_ref),
        (own_ids_ref, got_ids_ref),
        gains_ref,
        dense,
        row_parts,
        row_sems,
    )
    next(row_run)
    place.greet()
    next(row_run)
    loads = []

    def near_half():
        next(row_run)
        for number, pair in enumerate(((column_hbm, column), (rest_hbm, rest), (dense_hbm, dense))):
            loads.append(started(*pair, load_sems.at[number]))

    slot_rows, pooled, normed, query, key, value, probs, heads, resid, pre = kept
    width = dense.shape[2]
    slots = ids_ref.shape[0]
    height = slot_all.shape[1] // slots

    def forward_steps():
        for copy in loads:
            copy.wait()
        lengths = []
        for plane in range(PLANES):
            for slot in range(slots):
                here = (slot * PLANES + plane) * height
                slot_rows[here : here + height] = column[plane, slot * height : (slot + 1) * height].astype(WIDE)
            lengths.append(lengths_column(column[plane, slots * height :, :height]))
        hyper_forward_body(dense, rest, slot_rows, jnp.concatenate(lengths, 0), *kept[1:])
        yield

    def sum_steps():
        yield from scatter_steps(place, row_parts, row_grad, row_scratch, near_half)
        rows_low[place.z] = row_grad[...].astype(LOW)
        yield from line_share_steps(place, rows_low, line_sems)

    run_in_order([sum_steps(), forward_steps()], ROW_ORDER)
    vectors = vectors_of(rest)

    def put(in_dense, row, grad, height=16):
        target = (in_grad, out_grad, proj_grad)[row // 64] if in_dense else rest_grad
        row = row % 64 if in_dense else row
        target[:, row : row + height, :] = grad.astype(LOW).reshape(target.shape[0], height, width)

    d_resid, gain_two, bias_two, sums = back_dense(
        dense, vectors, rows_low[...].reshape(-1, rows_low.shape[2]), pooled, resid[...], pre, normed_two, acts, put, place.z
    )
    own = lax.axis_index("dp") * 2 + place.core

    def attention_steps():
        saved = (normed, query, key, value, probs, heads)
        slot_low, gain_one, bias_one = back_attention(rest, vectors, d_resid, slot_rows[...], saved, put, place.z)
        slot_low = slot_low.reshape(slots, PLANES, height, width)
        for plane in range(PLANES):
            slot_all[place.slot(0, plane, place.core)] = slot_low[:, plane].reshape(slots * height, width)
        put_vectors(rest_grad, vector_rows(gain_one, gain_two, bias_one, bias_two, sums))
        yield

    def table_steps():
        pieces, chunk = table_grad.shape[0], ids_ref.shape[1] // PLANES
        groups = slot_all.shape[0] // PLANES
        piece = lax.broadcasted_iota(jnp.int32, (pieces, slots * chunk), 0) + own * pieces
        for part in plane_gather_steps(place, slot_all, slot_sems):
            yield
            if part is None:
                continue
            lanes, here = slice(part * chunk, (part + 1) * chunk), slice(part * groups, (part + 1) * groups)
            ids = jnp.concatenate([ids_ref[turn : turn + 1, lanes] for turn in range(slots)], 1)
            rows = [slot_all[here, turn * height : (turn + 1) * height, :].reshape(chunk, width) for turn in range(slots)]
            found = dot((piece == ids).astype(LOW), jnp.concatenate(rows, 0), (1, 0))
            if part:
                table_grad[...] += found
            else:
                table_grad[...] = found
            yield

    places = (slice(IN_ROW, IN_ROW + 64), slice(OUT_ROW, OUT_ROW + 64), slice(PROJ_ROW, PROJ_ROW + 64))
    runs = [
        plane_scatter_steps(place, grad, dense_total, rows, scratch)
        for grad, rows, scratch in zip((in_grad, out_grad, proj_grad), places, plane_scratch)
    ]
    runs.append(plane_scatter_steps(place, rest_grad, rest_total, slice(None), plane_scratch[3]))
    runs += [table_steps(), attention_steps()]
    run_in_order(runs, LAST_ORDER)


def last_exchange(attention, ids, gains, slot_ids, dense, rest, column, pieces, number):
    in_vmem, anywhere = pl.BlockSpec(memory_space=pltpu.VMEM), pl.BlockSpec(memory_space=pl.ANY)
    devices = 8 * PLANES
    width = dense.shape[2]
    dq, dk, dv, query, kv, grad, rows = attention
    entries, d_model = rows.shape
    groups = dense.shape[0]
    query = query.reshape(groups, -1, query.shape[1])
    kv = kv.reshape(2, groups, -1, kv.shape[2])
    one = (entries // devices, d_model)
    slots = slot_ids.size // devices
    kept = [jax.ShapeDtypeStruct((PLANES * slots, width), WIDE)]
    kept += forward_shapes(PLANES * entries // devices, PLANES * slots, width)
    pooled = kept[1].shape
    return pl.pallas_call(
        last_kernel,
        in_specs=[anywhere] * 7 + [in_vmem] * 4 + [anywhere] * 3,
        out_specs=[in_vmem] * 4,
        out_shape=[
            jax.ShapeDtypeStruct(one, WIDE),
            jax.ShapeDtypeStruct(dense.shape[1:], WIDE),
            jax.ShapeDtypeStruct(rest.shape[1:], WIDE),
            jax.ShapeDtypeStruct((pieces, width), WIDE),
        ],
        scratch_shapes=[pltpu.VMEM(dense.shape, LOW), pltpu.VMEM(rest.shape, LOW)]
        + [pltpu.VMEM((8, 64, width), LOW)] * 3
        + [pltpu.VMEM((8, *rest.shape[1:]), LOW)]
        + [pltpu.VMEM(array.shape, array.dtype) for array in kept]
        + [
            pltpu.VMEM((devices, slots, width), LOW),
            pltpu.VMEM((PLANES, *one), LOW),
            pltpu.VMEM(pooled, LOW),
            pltpu.VMEM((4, *pooled), LOW),
            dma_grid(3),
        ]
        + [pltpu.VMEM(array.shape, LOW) for array in (dq, dk, dv, grad, rows)]
        + [
            pltpu.VMEM((entries, dq.shape[0] + 2 * dk.shape[0]), LOW),
            pltpu.VMEM((devices, *one), LOW),
            dma_grid(9),
            pltpu.VMEM(column.shape, LOW),
        ]
        + scatter_scratch(one)
        + plane_scatter_scratch((64, width)) * 3
        + plane_scatter_scratch(rest.shape[1:])
        + plane_gather_sems()
        + line_share_sems(),
        compiler_params=pltpu.CompilerParams(
            collective_id=number, has_side_effects=True, vmem_limit_bytes=VMEM_LIMIT
        ),
        name="last_exchange",
    )(dq, dk, dv, query, kv, grad, rows, *ids, gains, slot_ids, dense, rest, column)


def finish_kernel(
    own_ref, dense_ref, rest_ref, row_ref, table_ref, row_out, table_out, gains_out, biases_out, attn_out, in_out, in_bias_out, out_out,
    proj_out, proj_bias_out
):
    own = own_ref[0]
    width = rest_ref.shape[1]
    row_out[...] = row_ref[...]
    table_out[...] = table_ref[...]
    attn_out[...] = rest_ref[0:64].reshape(attn_out.shape)
    for turn in range(4):
        columns = slice(turn * width, (turn + 1) * width)
        in_out[:, columns] = dense_ref[IN_ROW + 16 * turn : IN_ROW + 16 * turn + 16]
        proj_out[:, columns] = dense_ref[PROJ_ROW + 16 * turn : PROJ_ROW + 16 * turn + 16]
    out_out[...] = dense_ref[OUT_ROW : OUT_ROW + 64]
    vectors = rest_ref[VECTOR_ROW : VECTOR_ROW + 16]

    def own_lanes(rows, size, base):
        lane = lax.broadcasted_iota(jnp.int32, (width, size), 0)
        column = lax.broadcasted_iota(jnp.int32, (width, size), 1)
        return dot_wide(rows, (lane + base - own * size == column).astype(WIDE), (1, 0))

    small = own_lanes(vectors, gains_out.shape[1], 0)
    gains_out[...] = small[0:2]
    biases_out[...] = small[2:5]
    size = in_bias_out.shape[1]
    picked = [own_lanes(vectors, size, turn * width) for turn in range(4)]
    in_bias_out[...] = sum(picked[turn][5 + turn : 6 + turn] for turn in range(4))
    proj_bias_out[...] = sum(picked[turn][9 + turn : 10 + turn] for turn in range(4))


def finish(own, dense, rest, row_grad, table_grad, shapes):
    return pl.pallas_call(
        finish_kernel,
        in_specs=[pl.BlockSpec(memory_space=pltpu.SMEM)] + [pl.BlockSpec(memory_space=pltpu.VMEM)] * 4,
        out_shape=[jax.ShapeDtypeStruct(shape, WIDE) for shape in (row_grad.shape, table_grad.shape, *shapes)],
        name="finish",
        compiler_params=pltpu.CompilerParams(vmem_limit_bytes=VMEM_LIMIT),
    )(own, dense, rest, row_grad, table_grad)


def to_slabs(attn, ffn_in, ffn_out, proj, vectors):
    width = attn.shape[-1]
    groups = width // 16

    def columns(matrix):
        return matrix.reshape(groups, 16, 4, width).transpose(0, 2, 1, 3).reshape(groups, 64, width)

    dense = [columns(ffn_in), ffn_out.reshape(groups, 64, width), columns(proj)]
    rest = [
        attn.reshape(4, groups, 16, width).transpose(1, 0, 2, 3).reshape(groups, 64, width),
        jnp.pad(vectors[None], ((0, groups - 1), (0, 0), (0, 0))),
    ]
    return jnp.concatenate(dense, 1), jnp.concatenate(rest, 1)


def from_slabs(dense, rest):
    groups, _, width = dense.shape

    def columns(row):
        part = dense[:, row : row + 64].reshape(groups, 4, 16, width)
        return part.transpose(0, 2, 1, 3).reshape(groups * 16, 4 * width)

    attn = rest[:, 0:64].reshape(groups, 4, 16, width).transpose(1, 0, 2, 3).reshape(4, groups * 16, width)
    return attn, columns(IN_ROW), dense[:, OUT_ROW : OUT_ROW + 64].reshape(groups * 64, width), columns(PROJ_ROW)


def shards(
    piece_ids,
    piece_lengths,
    group_ids,
    piece_table,
    ln_gains,
    hyp_biases,
    attn_weights,
    ffn_in_weight,
    ffn_in_bias,
    ffn_out_weight,
    proj_weight,
    proj_bias,
    lm_gains,
    query_weight,
    kv_weights,
    output_weight,
    gate_up_weight,
    down_weight,
    out_grad,
):
    n_mp = lax.axis_size("mp")
    devices = lax.axis_size(BOTH)
    me = lax.axis_index("mp")
    grid = n_mp == 2 and devices == 32
    entries, slot_count = piece_lengths.shape[0], piece_ids.shape[1]
    hyp_width = piece_table.shape[1]

    def swap(value):
        return lax.ppermute(value, "mp", [(0, 1), (1, 0)])

    def whole_of(value, axis):
        return lax.all_gather(value, BOTH, axis=axis, tiled=True)

    def share_of(value, axis):
        return lax.psum_scatter(value, BOTH, scatter_dimension=axis, tiled=True).astype(WIDE)

    def gather_tokens(value):
        return lax.all_gather(value, "mp", axis=0, tiled=True)

    me_all = lax.axis_index(BOTH)
    my_place = me.astype(jnp.int32).reshape(1)
    table_rows = piece_table.shape[0]
    lengths = piece_lengths[None]
    local_len = group_ids.shape[1]
    own_ids = group_ids.reshape(-1)
    got_ids = swap(own_ids) if grid else None
    seq_len = n_mp * local_len
    q_heads = query_weight.shape[1] // HEAD_DIM
    kv_here = max(KV_HEADS // n_mp, 1)
    cosine, sine = rope_tables(seq_len)
    lm_wide = lm_gains.astype(WIDE)
    dy_low = out_grad.reshape(local_len, -1)

    def norm_first(values):
        return rms_norm(values, lm_wide[0])

    def norm_second(values):
        return rms_norm(values, lm_wide[1])

    if grid:
        weights = (
            ln_gains,
            hyp_biases,
            attn_weights,
            ffn_in_weight,
            ffn_in_bias[None],
            ffn_out_weight,
            proj_weight,
            proj_bias[None],
        )
        slot_ids = piece_ids.T
        dense, rest, column, d_act, new_rows, inputs, qkv = first_exchange(
            weights,
            slot_ids,
            piece_table,
            lengths,
            lm_gains,
            own_ids[None],
            got_ids[None],
            dy_low,
            down_weight,
            query_weight,
            kv_weights,
            0,
        )
    else:
        own_pieces = me_all * table_rows + jnp.arange(table_rows, dtype=jnp.int32)
        slot_ids = piece_ids.reshape(devices, entries, slot_count).transpose(0, 2, 1).reshape(-1)
        slot_pick = (slot_ids[:, None] == own_pieces[None, :]).astype(LOW)
        slot_parts = dot(slot_pick, piece_table, (1, 0)).astype(LOW)
        slot_rows = lax.psum_scatter(slot_parts, BOTH, scatter_dimension=0, tiled=True).astype(WIDE)
        vectors = jnp.concatenate(
            [
                whole_of(ln_gains, 1),
                whole_of(hyp_biases, 1),
                whole_of(ffn_in_bias, 0).reshape(4, hyp_width),
                whole_of(proj_bias, 0).reshape(4, hyp_width),
                jnp.zeros((3, hyp_width), LOW),
            ]
        )
        dense, rest = to_slabs(
            whole_of(attn_weights, 1),
            whole_of(ffn_in_weight, 0),
            whole_of(ffn_out_weight, 0),
            whole_of(proj_weight, 0),
            vectors,
        )
        saved = hyper_forward(dense, rest, slot_rows, lengths, entries)
        new_rows, normed_rows = project(whole_of(saved[0], 0), dense, rest, lm_gains)
        kv_start = me * q_heads // (HEADS // KV_HEADS) * HEAD_DIM
        kv_local = lax.dynamic_slice_in_dim(kv_weights, kv_start, kv_here * HEAD_DIM, 2)
        qkv_weight = jnp.concatenate([query_weight, kv_local[0], kv_local[1]], 1)
        row_ids = lax.all_gather(own_ids, "mp", axis=0, tiled=True)
        row_index = jnp.arange(new_rows.shape[0], dtype=jnp.int32)
        row_pick = (row_index[:, None] == row_ids[None, :]).astype(LOW)
        own_pick = (own_ids[:, None] == row_index[None, :]).astype(LOW)
        qkv = dot(qkv_weight, dot(row_pick, normed_rows, (0, 0)).astype(LOW), (0, 1)).astype(LOW)
        inputs = dot(own_pick, new_rows, (1, 0))
        d_act = dot(gather_tokens(dy_low), down_weight, (1, 1)).astype(LOW)
    *heads, log_total = attend(my_place, qkv, cosine, sine, q_heads, kv_here, 2 if grid else 1)

    if grid:
        hidden, x_own, x_other = middle(*heads, output_weight, inputs, lm_gains, 2)
        out_other, back_other = feed_forward(x_other, d_act, 1, gate_up_weight, down_weight)
        out_got, back_got = swap(out_other), swap(back_other)
        out_own, back_own = feed_forward(x_own, d_act, 0, gate_up_weight, down_weight)
        grad_hidden_low, *grad_heads = turn_around(hidden, dy_low, (back_own, back_got), output_weight, lm_gains, 3)
    else:
        attn_part = dot(heads[0], output_weight, (0, 0)).astype(LOW)
        attn_sum = lax.psum_scatter(attn_part, "mp", scatter_dimension=0, tiled=True).astype(WIDE)
        hidden = inputs + attn_sum
        second_low = norm_second(hidden).astype(LOW)
        out_part, back_part = feed_forward(gather_tokens(second_low), d_act, 0, gate_up_weight, down_weight)
        outs = (lax.psum_scatter(out_part, "mp", scatter_dimension=0, tiled=True),)
        backs = (lax.psum_scatter(back_part, "mp", scatter_dimension=0, tiled=True),)
        lm_out, grad_hidden_low = second_back(hidden, dy_low, lm_gains, outs, backs)
        grad_heads = [dot(output_weight, gather_tokens(grad_hidden_low), (1, 1)).astype(LOW)]
    terms = (hidden, out_own, out_got) if grid else ()
    dq, dk, dv, *sums = attend_back(my_place, qkv, heads, log_total, grad_heads, cosine, sine, q_heads, kv_here, terms)
    if grid:
        lm_out = sums[0]

    if grid:
        attention = (dq, dk, dv, query_weight, kv_weights, grad_hidden_low, new_rows)
        ids = (own_ids[None], got_ids[None])
        row_grad, dense, rest, table_grad = last_exchange(
            attention, ids, lm_gains, slot_ids, dense, rest, column, table_rows, 1
        )
        bias_shape = (1, ffn_in_bias.shape[0])
        shapes = [
            ln_gains.shape,
            hyp_biases.shape,
            attn_weights.shape,
            ffn_in_weight.shape,
            bias_shape,
            ffn_out_weight.shape,
            proj_weight.shape,
            bias_shape,
        ]
        grads = finish(me_all.astype(jnp.int32).reshape(1), dense, rest, row_grad, table_grad, shapes)
        row_grad, table_grad, gains_grad, biases_grad, attn_grad, in_grad, in_bias, out_weight_grad, proj_grad, proj_bias_grad = grads
        in_bias, proj_bias_grad = in_bias[0], proj_bias_grad[0]
    else:
        grad_qkv = dot(jnp.concatenate([dq, dk, dv], 0), row_pick, (1, 1)).astype(LOW)
        first_part = dot(grad_qkv, qkv_weight, (0, 1))
        direct_part = dot(own_pick, grad_hidden_low, (0, 0))
        _, first_back = jax.vjp(norm_first, new_rows.astype(WIDE))
        row_parts = (direct_part + first_back(first_part)[0]).astype(LOW)
        row_grad = lax.psum_scatter(row_parts, BOTH, scatter_dimension=0, tiled=True).astype(WIDE)
        dense_grad, rest_grad, slot_low = hyper_backward(dense, rest, row_grad, slot_rows, saved)
        attn_grad, *dense_grads = from_slabs(dense_grad, rest_grad)
        attn_grad = share_of(attn_grad, 1)
        in_grad, out_weight_grad, proj_grad = [share_of(grad, 0) for grad in dense_grads]
        table_grad = dot(slot_pick, whole_of(slot_low, 0), (0, 0))
        sums = lax.psum(rest_grad[0, VECTOR_ROW:], BOTH).astype(WIDE)

        def own_lanes(values, size):
            return lax.dynamic_slice_in_dim(values, me_all * size, size, 1)

        gains_grad = own_lanes(sums[0:2], ln_gains.shape[1])
        biases_grad = own_lanes(sums[2:5], ln_gains.shape[1])
        in_bias, proj_bias_grad = own_lanes(sums[5:13].reshape(2, -1), ffn_in_bias.shape[0])
    return (
        lm_out.reshape(out_grad.shape),
        row_grad,
        table_grad,
        gains_grad,
        biases_grad,
        attn_grad,
        in_grad,
        in_bias,
        out_weight_grad,
        proj_grad,
        proj_bias_grad,
    )


def solution(mesh):
    return jax.shard_map(
        shards,
        mesh=mesh,
        in_specs=(
            P(),
            P(BOTH),
            P("dp", "mp"),
            P(BOTH, None),
            P(None, BOTH),
            P(None, BOTH),
            P(None, BOTH, None),
            P(BOTH, None),
            P(BOTH),
            P(BOTH, None),
            P(BOTH, None),
            P(BOTH),
            P(),
            P(None, "mp"),
            P(),
            P("mp", None),
            P(None, None, "mp"),
            P("mp", None),
            P("dp", "mp", None),
        ),
        out_specs=(
            P("dp", "mp", None),
            P(BOTH, None),
            P(BOTH, None),
            P(None, BOTH),
            P(None, BOTH),
            P(None, BOTH, None),
            P(BOTH, None),
            P(BOTH),
            P(BOTH, None),
            P(BOTH, None),
            P(BOTH),
        ),
        check_vma=False,
    )
```

```python
import functools

import jax
import jax.numpy as jnp
import numpy as np
from jax import lax
from jax.experimental import pallas as pl
from jax.experimental.pallas import tpu as pltpu
from jax.sharding import PartitionSpec as P

HEADS = 32
KV_HEADS = 4
HEAD_DIM = 64
HYP_HEADS = 8

EPSILON = 1e-05
ROPE_BASE = 10000.0
MASKED = -1e30
BOTH = ("dp", "mp")
LOW = jnp.bfloat16
WIDE = jnp.float32
QUERY_BLOCK = 256
MIB = 1 << 20
PLANES = 4
DENSE_ROWS, REST_ROWS = 192, 80
UNIT_BLOCK = 256
VMEM_LIMIT = 62 * MIB
FIRST_ORDER = (
    1, 0, 2, 2, 2, 2, 2, 0, 1, 0, 0, 2, 2, 0, 3, 1, 0, 2, 2, 1, 0, 2, 1, 0, 2, 3, 3, 0, 1, 2, 2, 0, 3, 2, 1, 2, 0,
    0, 1, 2, 1, 1, 2, 0, 2, 3, 3, 0, 1, 0, 0, 0, 0, 0, 1, 1, 1, 3, 1, 1, 0, 0, 2, 0, 3, 2, 2, 2, 1, 1, 0, 3, 2, 0,
    1, 1, 1, 1, 2, 1, 0, 0, 0, 2, 2, 0, 1, 3, 1, 0, 1, 0, 2, 1, 1, 2, 3, 0, 2, 2, 2, 0, 1, 0, 0, 0, 2, 2, 1, 2, 2,
    0, 2, 0, 2, 2,
)
LAST_ORDER = (
    5, 4, 4, 4, 4, 4, 0, 4, 1, 4, 4, 2, 4, 4, 4, 0, 3, 4, 4, 1, 4, 4, 2, 4, 4, 4, 4, 4, 3, 4, 1, 1, 0, 4, 4, 4, 0,
    4, 2, 4, 3, 2, 4, 4, 3, 0, 1, 0, 1, 2, 2, 4, 3, 3,
)
ROW_ORDER = (
    0, 0, 0, 0, 0, 0, 0, 0, 0, 0, 0, 0, 0, 0, 0, 0, 0, 0, 0, 0, 0, 0, 0, 0, 0, 0, 0, 0, 0, 0, 0, 1, 0,
)
HEADS_A_STEP = 4
QUERY_SCALE = HEAD_DIM ** (-0.5) * 1.4426950408889634


def rms_norm(values, gain_row):
    return values * lax.rsqrt(jnp.mean(values * values, -1, keepdims=True) + EPSILON) * gain_row


def dot(left, right, dims):
    return lax.dot_general(left, right, ((dims[:1], dims[1:]), ((), ())), preferred_element_type=WIDE)


def rope_tables(length):
    half = HEAD_DIM // 2
    frequency = np.float32(ROPE_BASE) ** (np.float32(-2.0) * np.arange(half, dtype=np.float32) / np.float32(HEAD_DIM))
    angles = frequency.astype(np.float32)[:, None] * np.arange(length, dtype=np.float32)[None, :]
    return jnp.asarray(np.cos(angles)), jnp.asarray(np.sin(angles))


def turn(columns, cosine, sine):
    half = HEAD_DIM // 2
    first, second = columns[:half], columns[half:]
    return jnp.concatenate([first * cosine - second * sine, second * cosine + first * sine], 0)


def turn_back(columns, cosine, sine):
    half = HEAD_DIM // 2
    first, second = columns[:half], columns[half:]
    return jnp.concatenate([first * cosine + second * sine, second * cosine - first * sine], 0)


def keep_causal(block, fill):
    key = lax.broadcasted_iota(jnp.int32, block.shape, 0)
    query = lax.broadcasted_iota(jnp.int32, block.shape, 1)
    return jnp.where(key <= query, block, fill)


def own_half(me_ref, left, right):
    first = me_ref[0] == 0
    return jnp.where(first, left, right), jnp.where(first, right, left)


def attend_kernel(per_group, me_ref, q_ref, k_ref, v_ref, cos_ref, sin_ref, *refs):
    *out_refs, log_ref, key_rows, out_all = refs
    seq_len = q_ref.shape[1]
    width = min(QUERY_BLOCK, seq_len)
    cosine, sine = cos_ref[...], sin_ref[...]
    count = q_ref.shape[0] // HEAD_DIM

    @pl.when(lax.rem(pl.program_id(0) * count, per_group) == 0)
    def _():
        key_rows[...] = turn(k_ref[...].astype(WIDE), cosine, sine).T.astype(LOW)

    queries = [
        (turn(q_ref[head * HEAD_DIM : (head + 1) * HEAD_DIM].astype(WIDE), cosine, sine) * QUERY_SCALE).astype(LOW)
        for head in range(count)
    ]

    def scores(start, head):
        q_block = queries[head][:, start : start + width]
        edge = dot(key_rows[start : start + width], q_block, (1, 0))
        return edge, dot(key_rows[:start], q_block, (1, 0)) if start else None

    def finish(start, head, edge, past):
        here = slice(start, start + width)
        lanes = slice(head * HEAD_DIM, (head + 1) * HEAD_DIM)
        edge = keep_causal(edge, MASKED)
        top = jnp.max(edge, 0, keepdims=True)
        if start:
            top = jnp.maximum(top, jnp.max(past, 0, keepdims=True))
        edge = jnp.exp2(edge - top)
        total = jnp.sum(edge, 0, keepdims=True)
        out = dot(v_ref[:, here], edge.astype(LOW), (1, 0))
        if start:
            past = jnp.exp2(past - top)
            total = total + jnp.sum(past, 0, keepdims=True)
            out = out + dot(v_ref[:, :start], past.astype(LOW), (1, 0))
        out_all[lanes, here] = (out / total).astype(LOW)
        log_ref[head, :, here] = top + jnp.log2(total)

    items = [(start, head) for start in range(0, seq_len, width) for head in range(count)]
    ready = scores(*items[0])
    for number, item in enumerate(items):
        following = scores(*items[number + 1]) if number + 1 < len(items) else None
        finish(*item, *ready)
        ready = following
    if len(out_refs) == 2:
        half = seq_len // 2
        out_refs[0][...], out_refs[1][...] = own_half(me_ref, out_all[:, :half], out_all[:, half:])
    else:
        out_refs[0][...] = out_all[...]


def attend(me, qkv, cosine, sine, q_heads, kv_heads, parts):
    per_group = q_heads // kv_heads
    seq_len = qkv.shape[1]
    column = (HEAD_DIM, seq_len)
    count = HEADS_A_STEP
    several = (count * HEAD_DIM, seq_len)
    whole = pl.BlockSpec(cosine.shape, lambda h: (0, 0))
    return pl.pallas_call(
        functools.partial(attend_kernel, per_group),
        grid=(q_heads // count,),
        in_specs=[
            pl.BlockSpec(memory_space=pltpu.SMEM),
            pl.BlockSpec(several, lambda h: (h, 0)),
            pl.BlockSpec(column, lambda h: (q_heads + h * count // per_group, 0)),
            pl.BlockSpec(column, lambda h: (q_heads + kv_heads + h * count // per_group, 0)),
            whole,
            whole,
        ],
        out_specs=[pl.BlockSpec((count * HEAD_DIM, seq_len // parts), lambda h: (h, 0))] * parts
        + [pl.BlockSpec((count, 1, seq_len), lambda h: (h, 0, 0))],
        out_shape=[jax.ShapeDtypeStruct((q_heads * HEAD_DIM, seq_len // parts), LOW)] * parts
        + [jax.ShapeDtypeStruct((q_heads, 1, seq_len), WIDE)],
        scratch_shapes=[pltpu.VMEM((seq_len, HEAD_DIM), LOW), pltpu.VMEM(several, LOW)],
        compiler_params=pltpu.CompilerParams(vmem_limit_bytes=VMEM_LIMIT),
        cost_estimate=pl.CostEstimate(
            flops=2 * q_heads * seq_len * seq_len * HEAD_DIM,
            bytes_accessed=4 * qkv.size,
            transcendentals=q_heads * seq_len * seq_len // 2,
        ),
        name="attend",
    )(me, qkv, qkv, qkv, cosine, sine)


def attend_back_kernel(per_group, parts, terms, me_ref, q_ref, k_ref, v_ref, log_ref, cos_ref, sin_ref, *refs):
    out_refs, grad_refs, refs = refs[:parts], refs[parts : 2 * parts], refs[2 * parts :]
    term_refs, refs = refs[:terms], refs[terms:]
    if terms:
        sum_ref, refs = refs[3], refs[:3] + refs[4:]
        sum_ref[...] = sum(ref[...].astype(WIDE) for ref in term_refs).astype(LOW)
    dq_ref, dk_ref, dv_ref, key_cols, key_rows, value_rows, key_sum, value_sum = refs
    seq_len = q_ref.shape[1]
    width = min(QUERY_BLOCK, seq_len)
    cosine, sine = cos_ref[...], sin_ref[...]
    count = q_ref.shape[0] // HEAD_DIM
    heads = range(count)
    member = lax.rem(pl.program_id(0) * count, per_group)

    def in_order(pieces, lanes):
        if len(pieces) == 1:
            return pieces[0][lanes]
        return jnp.concatenate(own_half(me_ref, pieces[0][lanes], pieces[1][lanes]), 1)

    @pl.when(member == 0)
    def _():
        turned = turn(k_ref[...].astype(WIDE), cosine, sine)
        key_cols[...] = turned.astype(LOW)
        key_rows[...] = turned.T.astype(LOW)
        value_rows[...] = v_ref[...].astype(WIDE).T.astype(LOW)
        key_sum[...] = jnp.zeros_like(key_sum)
        value_sum[...] = jnp.zeros_like(value_sum)

    queries, query_rows, grads, grad_rows, deltas = [], [], [], [], []
    for head in heads:
        lanes = slice(head * HEAD_DIM, (head + 1) * HEAD_DIM)
        turned = turn(q_ref[lanes].astype(WIDE), cosine, sine) * QUERY_SCALE
        queries.append(turned.astype(LOW))
        query_rows.append(turned.T.astype(LOW))
        grad = in_order(grad_refs, lanes)
        grads.append(grad)
        grad_wide = grad.astype(WIDE)
        grad_rows.append(grad_wide.T.astype(LOW))
        deltas.append(jnp.sum(grad_wide * in_order(out_refs, lanes).astype(WIDE), 0, keepdims=True))

    def pieces_of(start):
        return [slice(start, start + width)] + ([slice(0, start)] if start else [])

    def products(start):
        here = slice(start, start + width)
        return [
            [
                (dot(key_rows[keys], queries[head][:, here], (1, 0)), dot(value_rows[keys], grads[head][:, here], (1, 0)))
                for head in heads
            ]
            for keys in pieces_of(start)
        ]

    def finish(start, found):
        here = slice(start, start + width)
        dq = [0.0] * count
        for number, keys in enumerate(pieces_of(start)):
            probs, scores = [], []
            for head in heads:
                raw, grad_probs = found[number][head]
                prob = jnp.exp2(raw - log_ref[head, :, here])
                if number == 0:
                    prob = keep_causal(prob, 0.0)
                probs.append(prob.astype(LOW))
                scores.append((prob * (grad_probs - deltas[head][:, here])).astype(LOW))
                dq[head] += dot(key_cols[:, keys], scores[head], (1, 0))
            grad_part = jnp.concatenate([rows[here] for rows in grad_rows], 0)
            query_part = jnp.concatenate([rows[here] for rows in query_rows], 0)
            value_sum[keys] += dot(jnp.concatenate(probs, 1), grad_part, (1, 0))
            key_sum[keys] += dot(jnp.concatenate(scores, 1), query_part, (1, 0))
        for head in heads:
            back = turn_back(dq[head] * HEAD_DIM ** (-0.5), cosine[:, here], sine[:, here])
            dq_ref[head * HEAD_DIM : (head + 1) * HEAD_DIM, here] = back.astype(LOW)

    starts = list(range(0, seq_len, width))
    ready = products(0)
    for number, start in enumerate(starts):
        following = products(starts[number + 1]) if number + 1 < len(starts) else None
        finish(start, ready)
        ready = following

    @pl.when(member == per_group - count)
    def _():
        dk_ref[...] = turn_back(key_sum[...].T * (HEAD_DIM ** (-0.5) / QUERY_SCALE), cosine, sine).astype(LOW)
        dv_ref[...] = value_sum[...].T.astype(LOW)


def attend_back(me, qkv, outs, log_total, grads, cosine, sine, q_heads, kv_heads, terms=()):
    per_group = q_heads // kv_heads
    seq_len = qkv.shape[1]
    parts = len(outs)
    count = HEADS_A_STEP
    column = (HEAD_DIM, seq_len)
    whole = pl.BlockSpec(cosine.shape, lambda h: (0, 0))
    by_head = pl.BlockSpec((count * HEAD_DIM, seq_len), lambda h: (h, 0))
    by_group = pl.BlockSpec(column, lambda h: (h * count // per_group, 0))
    in_parts = pl.BlockSpec((count * HEAD_DIM, seq_len // parts), lambda h: (h, 0))
    steps = q_heads // count
    term_rows = [pl.BlockSpec((term.shape[0] // steps, term.shape[1]), lambda h: (h, 0)) for term in terms]
    return pl.pallas_call(
        functools.partial(attend_back_kernel, per_group, parts, len(terms)),
        grid=(q_heads // count,),
        in_specs=[
            pl.BlockSpec(memory_space=pltpu.SMEM),
            by_head,
            pl.BlockSpec(column, lambda h: (q_heads + h * count // per_group, 0)),
            pl.BlockSpec(column, lambda h: (q_heads + kv_heads + h * count // per_group, 0)),
            pl.BlockSpec((count, 1, seq_len), lambda h: (h, 0, 0)),
            whole,
            whole,
        ]
        + [in_parts] * (2 * parts)
        + term_rows,
        out_specs=[by_head, by_group, by_group] + term_rows[:1],
        out_shape=[
            jax.ShapeDtypeStruct((q_heads * HEAD_DIM, seq_len), LOW),
            jax.ShapeDtypeStruct((kv_heads * HEAD_DIM, seq_len), LOW),
            jax.ShapeDtypeStruct((kv_heads * HEAD_DIM, seq_len), LOW),
        ]
        + [jax.ShapeDtypeStruct(term.shape, LOW) for term in terms[:1]],
        scratch_shapes=[
            pltpu.VMEM((HEAD_DIM, seq_len), LOW),
            pltpu.VMEM((seq_len, HEAD_DIM), LOW),
            pltpu.VMEM((seq_len, HEAD_DIM), LOW),
            pltpu.VMEM((seq_len, HEAD_DIM), WIDE),
            pltpu.VMEM((seq_len, HEAD_DIM), WIDE),
        ],
        compiler_params=pltpu.CompilerParams(vmem_limit_bytes=VMEM_LIMIT),
        cost_estimate=pl.CostEstimate(
            flops=5 * q_heads * seq_len * seq_len * HEAD_DIM,
            bytes_accessed=8 * qkv.size,
            transcendentals=q_heads * seq_len * seq_len // 2,
        ),
        name="attend_back",
    )(me, qkv, qkv, qkv, log_total, cosine, sine, *outs, *grads, *terms)


def feed_kernel(last_block, x_ref, d_act_ref, gate_up_ref, down_ref, out_ref, back_ref, out_sum, back_sum):
    step, last = pl.program_id(0), pl.num_programs(0) - 1

    @pl.when(step == 0)
    def _():
        out_sum[...] = jnp.zeros_like(out_sum)
        back_sum[...] = jnp.zeros_like(back_sum)

    def units(size):
        x, down = x_ref[...], down_ref[:size]
        gate_weight, up_weight = gate_up_ref[0, :, :size], gate_up_ref[1, :, :size]
        gate = dot(x, gate_weight, (1, 0))
        up = dot(x, up_weight, (1, 0))
        d_act = d_act_ref[:, :size].astype(WIDE)
        sigmoid = jax.nn.sigmoid(gate)
        silu = gate * sigmoid
        act = (silu * up).astype(LOW)
        d_up = (d_act * silu).astype(LOW)
        d_gate = (d_act * up * (sigmoid + silu * (1.0 - sigmoid))).astype(LOW)
        out_sum[...] += dot(act, down, (1, 0))
        back_sum[...] += dot(d_gate, gate_weight, (1, 1))
        back_sum[...] += dot(d_up, up_weight, (1, 1))

    block = down_ref.shape[0]
    if last_block == block:
        units(block)
    else:
        pl.when(step < last)(lambda: units(block))
        pl.when(step == last)(lambda: units(last_block))

    @pl.when(step == last)
    def _():
        out_ref[...] = out_sum[...].astype(LOW)
        back_ref[...] = back_sum[...].astype(LOW)


def feed_forward(x, d_act, which, gate_up, down):
    tokens, width = x.shape
    units = down.shape[0]
    block = 2 * UNIT_BLOCK if units % UNIT_BLOCK == 0 else units
    steps = pl.cdiv(units, block)
    whole = pl.BlockSpec((tokens, width), lambda f: (0, 0))
    result = jax.ShapeDtypeStruct((tokens, width), LOW)
    return pl.pallas_call(
        functools.partial(feed_kernel, units - (steps - 1) * block),
        grid=(steps,),
        in_specs=[
            whole,
            pl.BlockSpec((tokens, block), lambda f: (which, f)),
            pl.BlockSpec((2, width, block), lambda f: (0, 0, f)),
            pl.BlockSpec((block, width), lambda f: (f, 0)),
        ],
        out_specs=[whole, whole],
        out_shape=[result, result],
        scratch_shapes=[pltpu.VMEM((tokens, width), WIDE), pltpu.VMEM((tokens, width), WIDE)],
        compiler_params=pltpu.CompilerParams(vmem_limit_bytes=VMEM_LIMIT),
        cost_estimate=pl.CostEstimate(
            flops=10 * tokens * width * units,
            bytes_accessed=6 * width * units + 8 * tokens * width,
            transcendentals=tokens * units,
        ),
        name="feed_forward",
    )(x, d_act, gate_up, down)


def second_back_kernel(hidden_ref, dy_ref, gain_ref, *refs):
    *part_refs, out_ref, grad_ref = refs
    outs, backs = part_refs[: len(part_refs) // 2], part_refs[len(part_refs) // 2 :]
    hidden = hidden_ref[...]
    out_ref[...] = (hidden + sum(ref[...].astype(WIDE) for ref in outs)).astype(LOW)
    scale = lax.rsqrt(jnp.mean(hidden * hidden, -1, keepdims=True) + EPSILON)
    inner = sum(ref[...].astype(WIDE) for ref in backs) * gain_ref[1:2].astype(WIDE)
    mean = jnp.mean(hidden * inner, -1, keepdims=True)
    back = scale * inner - hidden * (scale * scale * scale * mean)
    grad_ref[...] = (dy_ref[...].astype(WIDE) + back).astype(LOW)


def second_back(hidden, dy, gains, outs, backs):
    tokens, width = hidden.shape
    block = min(64, tokens)
    rows = pl.BlockSpec((block, width), lambda i: (i, 0))
    result = jax.ShapeDtypeStruct(hidden.shape, LOW)
    return pl.pallas_call(
        second_back_kernel,
        grid=(tokens // block,),
        in_specs=[rows, rows, pl.BlockSpec((2, width), lambda i: (0, 0))] + [rows] * (len(outs) + len(backs)),
        out_specs=[rows, rows],
        out_shape=[result, result],
        compiler_params=pltpu.CompilerParams(vmem_limit_bytes=VMEM_LIMIT),
        cost_estimate=pl.CostEstimate(flops=12 * hidden.size, bytes_accessed=18 * hidden.size, transcendentals=0),
        name="second_back",
    )(hidden, dy, gains, *outs, *backs)


class Place:
    def __init__(self):
        chip, self.core = lax.axis_index("dp"), lax.axis_index("mp")
        self.z = lax.div(chip, 4)
        self.y, self.x = lax.rem(lax.div(chip, 2), 2), lax.rem(chip, 2)
        self.below, self.above = self.z > 0, self.z < PLANES - 1
        z, y, x, core = self.z, self.y, self.x, self.core
        self.others = (z + 1 - 2 * lax.rem(z, 2), lax.rem(z + 2, PLANES), PLANES - 1 - z)
        self.targets = {
            "x": self.device(z, y, 1 - x, core),
            "y": self.device(z, 1 - y, x, core),
            "diagonal": self.device(z, 1 - y, 1 - x, core),
            "core": self.device(z, y, x, 1 - core),
            "up": self.device(z + 1, y, x, core),
            "down": self.device(z - 1, y, x, core),
        }
        for turn, plane in enumerate(self.others):
            self.targets[turn] = self.device(plane, y, x, core)

    def device(self, plane, y, x, core):
        return {"dp": (plane * 2 + y) * 2 + x, "mp": core}

    def chip(self, kind):
        y = 1 - self.y if kind in (2, 3) else self.y
        x = 1 - self.x if kind in (1, 3) else self.x
        return y * 2 + x

    def slot(self, kind, plane, core):
        return (plane * 4 + self.chip(kind)) * 2 + core

    def levels(self, distance):
        if distance == 0:
            return [(0, self.z, None)]
        return [
            (1, self.z + distance, self.z + distance < PLANES),
            (-1, self.z - distance, self.z >= distance),
        ]

    def at(self, distance, step):
        for sign, plane, valid in self.levels(distance):
            if valid is None:
                step(sign, plane)
            else:
                pl.when(valid)(functools.partial(step, sign, plane))

    def steps_at(self, distance, step):
        for sign, plane, valid in self.levels(distance):
            if valid is None:
                step(sign, plane)
            else:
                pl.when(valid)(functools.partial(step, sign, plane))
            yield

    def greet(self):
        barrier = pltpu.get_barrier_semaphore()
        names = ("x", "y", "diagonal", "core", 0, 1, 2)
        for name in names:
            pl.semaphore_signal(barrier, inc=1, device_id=self.targets[name], device_id_type=pl.DeviceIdType.MESH)
        pl.semaphore_wait(barrier, len(names))


def halves(shape):
    rows, columns = shape[-2:]
    if rows >= 32:
        cut = rows // 32 * 16
        return (slice(0, cut), slice(None)), (slice(cut, rows), slice(None))
    cut = columns // 2
    return (slice(None), slice(0, cut)), (slice(None), slice(cut, columns))


def send(source, target, send_sem, recv_sem, device):
    pltpu.make_async_remote_copy(
        src_ref=source,
        dst_ref=target,
        send_sem=send_sem,
        recv_sem=recv_sem,
        device_id=device,
        device_id_type=pl.DeviceIdType.MESH,
    ).start()


def sent(view, sem):
    pltpu.make_async_copy(view, view, sem).wait()


def dma_grid(*shape):
    return pltpu.SemaphoreType.DMA(shape)


def gather_sems():
    return [pltpu.SemaphoreType.DMA, dma_grid(6, PLANES), dma_grid(5, PLANES), dma_grid(5, PLANES), dma_grid(5, PLANES)]


def gather_steps(place, share, whole, sems):
    own_sem, link_send, link_recv, core_send, core_recv = sems
    near, far = halves(share.shape)
    z, core = place.z, place.core

    def view(kind, plane, whose=None):
        whose = core if whose is None else whose
        if kind >= 3:
            return whole.at[(place.slot(3, plane, whose), *(near if kind == 3 else far))]
        return whole.at[place.slot(kind, plane, whose)]

    def forward(name, source, target, number, kind, plane):
        send(source, target, link_send.at[number, plane], link_recv.at[kind, plane], place.targets[name])

    def to_core(source, kind, plane):
        send(source, view(kind, plane), core_send.at[kind, plane], core_recv.at[kind, plane], place.targets["core"])

    def column(sign, plane):
        target = view(0, plane)
        source = target if sign else share
        if sign:
            sent(target, link_recv.at[0, plane])
        if sign <= 0:
            pl.when(place.above)(lambda: forward("up", source, target, 4, 0, plane))
        if sign >= 0:
            pl.when(place.below)(lambda: forward("down", source, target, 5, 0, plane))
        forward("x", source, target, 0, 1, plane)
        forward("y", source, target, 1, 2, plane)
        to_core(source, 0, plane)

    def side_x(sign, plane):
        sent(view(1, plane), link_recv.at[1, plane])
        part = whole.at[(place.slot(1, plane, core), *far)]
        forward("y", part, part, 3, 4, plane)
        to_core(view(1, plane), 1, plane)

    def side_y(sign, plane):
        sent(view(2, plane), link_recv.at[2, plane])
        part = whole.at[(place.slot(2, plane, core), *near)]
        forward("x", part, part, 2, 3, plane)
        to_core(view(2, plane), 2, plane)

    def diagonal(kind, sign, plane):
        sent(view(kind, plane), link_recv.at[kind, plane])
        to_core(view(kind, plane), kind, plane)

    diagonal_x, diagonal_y = functools.partial(diagonal, 3), functools.partial(diagonal, 4)
    keep = pltpu.make_async_copy(share, view(0, z), own_sem)
    keep.start()
    for step in range(PLANES + 2):
        for stage, lag in ((column, 0), (side_x, 1), (side_y, 1), (diagonal_x, 2), (diagonal_y, 2)):
            if 0 <= step - lag < PLANES:
                yield from place.steps_at(step - lag, stage)
    keep.wait()
    for plane in range(PLANES):
        for kind in range(5):
            sent(view(kind, plane, 1 - core), core_recv.at[kind, plane])
    yield
    for plane in range(PLANES):
        for kind in range(5):
            sent(view(kind, plane), core_send.at[kind, plane])
        for number, part in enumerate((share, share, share.at[near], share.at[far])):
            sent(part, link_send.at[number, plane])
        pl.when((plane <= z) & place.above)(lambda: sent(share, link_send.at[4, plane]))
        pl.when((plane >= z) & place.below)(lambda: sent(share, link_send.at[5, plane]))
    yield


def late_gather_sems():
    return [
        pltpu.SemaphoreType.DMA,
        dma_grid(4),
        dma_grid(4),
        dma_grid(2, 4, PLANES),
        dma_grid(4, PLANES),
        dma_grid(4, PLANES),
        dma_grid(4, PLANES),
    ]


def late_gather_steps(place, share, whole, sems):
    own_sem, plane_send, plane_recv, line_send, line_recv, core_send, core_recv = sems
    near, far = halves(share.shape)
    z, core = place.z, place.core

    def view(kind, plane, whose=None):
        return whole.at[place.slot(kind, plane, core if whose is None else whose)]

    def part(kind, half):
        return whole.at[(place.slot(kind, z, core), *half)]

    def forward(name, source, target, number):
        send(source, target, plane_send.at[number], plane_recv.at[number], place.targets[name])

    def on_line(name, source, kind, plane):
        which = 0 if name == "up" else 1
        send(
            source, view(kind, plane), line_send.at[which, kind, plane], line_recv.at[kind, plane], place.targets[name]
        )

    def own_plane(source, kind):
        pl.when(place.above)(lambda: on_line("up", source, kind, z))
        pl.when(place.below)(lambda: on_line("down", source, kind, z))
        send(source, view(kind, z), core_send.at[kind, z], core_recv.at[kind, z], place.targets["core"])

    def line(kind, sign, plane):
        target = view(kind, plane)
        sent(target, line_recv.at[kind, plane])
        if sign < 0:
            pl.when(place.above)(lambda: on_line("up", target, kind, plane))
        else:
            pl.when(place.below)(lambda: on_line("down", target, kind, plane))
        send(target, target, core_send.at[kind, plane], core_recv.at[kind, plane], place.targets["core"])

    keep = pltpu.make_async_copy(share, view(0, z), own_sem)
    keep.start()
    forward("x", share, view(0, z), 0)
    forward("y", share, view(0, z), 1)
    own_plane(share, 0)
    yield
    sent(view(1, z), plane_recv.at[0])
    forward("y", part(1, far), part(1, far), 3)
    own_plane(view(1, z), 1)
    yield
    sent(view(2, z), plane_recv.at[1])
    forward("x", part(2, near), part(2, near), 2)
    own_plane(view(2, z), 2)
    yield
    for distance in range(1, PLANES):
        for kind in range(4):
            if distance == 1 and kind == 3:
                sent(part(3, near), plane_recv.at[2])
                sent(part(3, far), plane_recv.at[3])
                own_plane(view(3, z), 3)
                yield
            yield from place.steps_at(distance, functools.partial(line, kind))
    keep.wait()
    for plane in range(PLANES):
        for kind in range(4):
            sent(view(kind, plane, 1 - core), core_recv.at[kind, plane])
    yield
    for number, sent_part in enumerate((share, share, share.at[near], share.at[far])):
        sent(sent_part, plane_send.at[number])
    for plane in range(PLANES):
        for kind in range(4):
            sent(share, core_send.at[kind, plane])
            up, down = line_send.at[0, kind, plane], line_send.at[1, kind, plane]
            pl.when((plane <= z) & place.above)(functools.partial(sent, share, up))
            pl.when((plane >= z) & place.below)(functools.partial(sent, share, down))
    yield


def half_shapes(one):
    return [tuple(len(range(*cut.indices(size))) for cut, size in zip(half, one)) for half in halves(one)]


def scatter_scratch(one):
    near, far = half_shapes(one)
    line = pltpu.VMEM((PLANES, *one), LOW)
    buffers = [
        pltpu.VMEM((4, PLANES, *one), LOW),
        line,
        line,
        pltpu.VMEM((PLANES, *near), LOW),
        pltpu.VMEM((PLANES, *far), LOW),
        line,
        line,
        pltpu.VMEM(one, WIDE),
    ]
    return buffers + [dma_grid(6, PLANES), dma_grid(6, PLANES), dma_grid(4, PLANES), dma_grid(4, PLANES)]


def from_other_core(place, parts, mine, core_send, core_recv, between=None):
    def start(plane):
        for kind in (3, 1, 2, 0):
            send(
                parts.at[place.slot(kind, plane, 1 - place.core)],
                mine.at[kind, plane],
                core_send.at[kind, plane],
                core_recv.at[kind, plane],
                place.targets["core"],
            )

    if between is None:
        for step in range(PLANES):
            place.at(PLANES - 1 - step, lambda sign, plane: start(plane))
    else:
        start(place.others[2])
        start(place.others[1])
        between()
        start(place.others[0])
        start(place.z)


def scatter_steps(place, parts, total, scratch, between=None):
    mine, by_x, by_y, diagonal_x, diagonal_y, line_up, line_down, wide, *sems = scratch
    link_send, link_recv, core_send, core_recv = sems
    near, far = halves(parts.shape)
    z, core, last = place.z, place.core, PLANES - 1

    def own(kind, plane):
        return parts[place.slot(kind, plane, core)]

    def forward(name, source, target, number, plane):
        send(source, target, link_send.at[number, plane], link_recv.at[number, plane], place.targets[name])

    def arrived(view, number, plane):
        sent(view, link_recv.at[number, plane])

    def from_core(kind, plane):
        sent(mine.at[kind, plane], core_recv.at[kind, plane])

    def diagonal(sign, plane):
        from_core(3, plane)
        mine[3, plane] += own(3, plane)
        forward("x", mine.at[(3, plane, *near)], diagonal_x.at[plane], 0, plane)
        forward("y", mine.at[(3, plane, *far)], diagonal_y.at[plane], 1, plane)

    def side_x(sign, plane):
        from_core(1, plane)
        mine[1, plane] += own(1, plane)
        arrived(diagonal_y.at[plane], 1, plane)
        mine[(1, plane, *far)] += diagonal_y[plane]
        forward("x", mine.at[1, plane], by_x.at[plane], 2, plane)

    def side_y(sign, plane):
        from_core(2, plane)
        mine[2, plane] += own(2, plane)
        arrived(diagonal_x.at[plane], 0, plane)
        mine[(2, plane, *near)] += diagonal_x[plane]
        forward("y", mine.at[2, plane], by_y.at[plane], 3, plane)

    def column(sign, plane):
        from_core(0, plane)
        arrived(by_x.at[plane], 2, plane)
        arrived(by_y.at[plane], 3, plane)
        wide[...] = (own(0, plane).astype(WIDE) + mine[0, plane].astype(WIDE)) + (
            by_x[plane].astype(WIDE) + by_y[plane].astype(WIDE)
        )

        def add(line, number):
            arrived(line.at[plane], number, plane)
            wide[...] += line[plane].astype(WIDE)

        if sign >= 0:
            pl.when(place.below)(lambda: add(line_up, 4))
        if sign <= 0:
            pl.when(place.above)(lambda: add(line_down, 5))
        if sign == 0:
            total[...] = wide[...]
        else:
            mine[0, plane] = wide[...].astype(LOW)
        if sign > 0:
            forward("up", mine.at[0, plane], line_up.at[plane], 4, plane)
        if sign < 0:
            forward("down", mine.at[0, plane], line_down.at[plane], 5, plane)

    from_other_core(place, parts, mine, core_send, core_recv, between)
    yield
    for step in range(PLANES + 2):
        for stage, lag in ((diagonal, 0), (side_x, 1), (side_y, 1), (column, 2)):
            if 0 <= step - lag < PLANES:
                yield from place.steps_at(last - (step - lag), stage)
    for plane in range(PLANES):
        for kind in range(4):
            sent(mine.at[kind, plane], core_send.at[kind, plane])
        views = (diagonal_x.at[plane], diagonal_y.at[plane], by_x.at[plane], by_y.at[plane])
        for number, part in enumerate(views):
            sent(part, link_send.at[number, plane])
        pl.when(plane > z)(lambda: sent(mine.at[0, plane], link_send.at[4, plane]))
        pl.when(plane < z)(lambda: sent(mine.at[0, plane], link_send.at[5, plane]))
    yield


def line_share_sems():
    return [dma_grid(3), dma_grid(3)]


def line_share_steps(place, buffer, sems):
    line_send, line_recv = sems
    own = buffer.at[place.z]
    for turn in range(3):
        send(own, own, line_send.at[turn], line_recv.at[turn], place.targets[turn])
    yield
    for turn, plane in enumerate(place.others):
        sent(buffer.at[plane], line_recv.at[turn])
    for turn in range(3):
        sent(own, line_send.at[turn])
    yield


def small_gather_sems():
    return [dma_grid(3), dma_grid(3), dma_grid(3), dma_grid(3), pltpu.SemaphoreType.DMA, pltpu.SemaphoreType.DMA]


def small_gather(place, share, whole, sems):
    line_send, line_recv, plane_send, plane_recv, core_send, core_recv = sems
    here, core = place.chip(0), place.core
    whole[place.z, here, core] = share
    own = whole.at[place.z, here, core]
    for turn in range(3):
        send(own, own, line_send.at[turn], line_recv.at[turn], place.targets[turn])
    for turn, plane in enumerate(place.others):
        sent(whole.at[plane, here, core], line_recv.at[turn])
    column = whole.at[:, here, core]
    names = ("x", "y", "diagonal")
    for turn, name in enumerate(names):
        send(column, column, plane_send.at[turn], plane_recv.at[turn], place.targets[name])
    for turn in range(3):
        sent(whole.at[:, place.chip(turn + 1), core], plane_recv.at[turn])
    mine = whole.at[:, :, core]
    send(mine, mine, core_send, core_recv, place.targets["core"])
    sent(whole.at[:, :, 1 - core], core_recv)
    for turn in range(3):
        sent(own, line_send.at[turn])
        sent(column, plane_send.at[turn])
    sent(mine, core_send)


def plane_gather_sems():
    return [dma_grid(4, PLANES), dma_grid(4, PLANES), dma_grid(5, PLANES), dma_grid(5, PLANES)]


def plane_gather_steps(place, whole, sems):
    plane_send, plane_recv, core_send, core_recv = sems
    near, far = halves(whole.shape)
    core = place.core

    def view(kind, part, whose=None):
        whose = core if whose is None else whose
        if kind >= 3:
            return whole.at[(place.slot(3, part, whose), *(near if kind == 3 else far))]
        return whole.at[place.slot(kind, part, whose)]

    def forward(name, view, number, part):
        send(view, view, plane_send.at[number, part], plane_recv.at[number, part], place.targets[name])

    def to_core(kind, part):
        here = view(kind, part)
        send(here, here, core_send.at[kind, part], core_recv.at[kind, part], place.targets["core"])

    def start(part):
        forward("x", view(0, part), 0, part)
        forward("y", view(0, part), 1, part)
        to_core(0, part)

    def side(kind, part):
        sent(view(kind, part), plane_recv.at[kind - 1, part])
        half = whole.at[(place.slot(kind, part, core), *(far if kind == 1 else near))]
        forward("y" if kind == 1 else "x", half, 3 if kind == 1 else 2, part)
        to_core(kind, part)

    def diagonal(kind, part):
        sent(view(kind, part), plane_recv.at[kind - 1, part])
        to_core(kind, part)

    for part in range(PLANES):
        start(part)
        yield
    for step in range(PLANES + 2):
        for stage, kind, lag in ((side, 1, 0), (side, 2, 0), (diagonal, 3, 1), (diagonal, 4, 1)):
            if 0 <= step - lag < PLANES:
                stage(kind, step - lag)
                yield
        if step >= 2:
            part = step - 2
            for kind in range(5):
                sent(view(kind, part, 1 - core), core_recv.at[kind, part])
            yield part
    for part in range(PLANES):
        for kind in range(5):
            sent(view(kind, part), core_send.at[kind, part])
        for number, kind in enumerate((0, 0, 3, 4)):
            sent(view(kind, part), plane_send.at[number, part])
    yield


def plane_scatter_scratch(one):
    near, far = half_shapes(one)
    single = pltpu.VMEM(one, LOW)
    buffers = [pltpu.VMEM((4, *one), LOW), pltpu.VMEM(near, LOW), pltpu.VMEM(far, LOW), single, single]
    return buffers + [dma_grid(4), dma_grid(4), dma_grid(4), dma_grid(4)]


def plane_scatter_steps(place, parts, total, rows, scratch):
    mine, diagonal_x, diagonal_y, by_x, by_y, plane_send, plane_recv, core_send, core_recv = scratch
    near, far = halves(parts.shape)
    core = place.core

    def forward(name, source, target, number):
        send(source, target, plane_send.at[number], plane_recv.at[number], place.targets[name])

    def from_core(kind):
        sent(mine.at[kind], core_recv.at[kind])

    def own(kind):
        return parts[place.chip(kind) * 2 + core]

    for kind in (3, 1, 2, 0):
        source = parts.at[place.chip(kind) * 2 + 1 - core]
        send(source, mine.at[kind], core_send.at[kind], core_recv.at[kind], place.targets["core"])
    yield
    from_core(3)
    mine[3] += own(3)
    forward("x", mine.at[(3, *near)], diagonal_x, 0)
    forward("y", mine.at[(3, *far)], diagonal_y, 1)
    yield
    from_core(1)
    mine[1] += own(1)
    sent(diagonal_y, plane_recv.at[1])
    mine[(1, *far)] += diagonal_y[...]
    forward("x", mine.at[1], by_x, 2)
    yield
    from_core(2)
    mine[2] += own(2)
    sent(diagonal_x, plane_recv.at[0])
    mine[(2, *near)] += diagonal_x[...]
    forward("y", mine.at[2], by_y, 3)
    yield
    from_core(0)
    here = own(0).astype(WIDE) + mine[0].astype(WIDE)
    sent(by_x, plane_recv.at[2])
    sent(by_y, plane_recv.at[3])
    total[rows] = here + (by_x[...].astype(WIDE) + by_y[...].astype(WIDE))
    yield
    for kind in range(4):
        sent(mine.at[kind], core_send.at[kind])
    for number, part in enumerate((diagonal_x, diagonal_y, by_x, by_y)):
        sent(part, plane_send.at[number])
    yield


def run_in_order(runs, order):
    for place in order:
        next(runs[place])
    assert all(next(run, "end") == "end" for run in runs)


def run_together(runs):
    runs = list(runs)
    while runs:
        for run in list(runs):
            if run in runs and next(run, "end") == "end":
                runs = [other for other in runs if other is not run]


IN_ROW, OUT_ROW, PROJ_ROW, VECTOR_ROW = 0, 64, 128, 64


def weight(slabs, row, height=16):
    part = slabs[:, row : row + height, :]
    return part.reshape(part.shape[0] * height, part.shape[2])


def vectors_of(slabs, row=VECTOR_ROW):
    return jnp.sum(slabs[:, row : row + 16, :].astype(WIDE), 0)


def pick_matrix(rows, columns, step, kind=LOW):
    row = lax.broadcasted_iota(jnp.int32, (rows, columns), 0)
    column = lax.broadcasted_iota(jnp.int32, (rows, columns), 1)
    return ((column >= row * step) & (column < (row + 1) * step)).astype(kind)


def every_slot(by_entry, slots):
    return jnp.concatenate([by_entry] * slots, 0)


def dot_wide(left, right, dims):
    return lax.dot_general(
        left, right, ((dims[:1], dims[1:]), ((), ())), precision=lax.Precision.HIGHEST, preferred_element_type=WIDE
    )


def normalize(values):
    center = values - jnp.mean(values, -1, keepdims=True)
    scale = lax.rsqrt(jnp.mean(center * center, -1, keepdims=True) + EPSILON)
    return center * scale, scale


def normalize_back(grad, gain, unit, scale):
    inner = grad * gain
    back = inner - jnp.mean(inner, -1, keepdims=True) - unit * jnp.mean(inner * unit, -1, keepdims=True)
    return back * scale, jnp.sum(grad * unit, 0, keepdims=True), jnp.sum(grad, 0, keepdims=True)


GELU_A, GELU_B = (2.0 / 3.141592653589793) ** 0.5, 0.044715


def gelu_tanh(values):
    return jnp.tanh(GELU_A * (values + GELU_B * values * values * values))


def head_matrix(width):
    return pick_matrix(128, width, width // HYP_HEADS)


def lengths_column(row):
    shape = (row.shape[1], row.shape[1])
    same = lax.broadcasted_iota(jnp.int32, shape, 0) == lax.broadcasted_iota(jnp.int32, shape, 1)
    return jnp.sum(jnp.where(same, row.astype(WIDE), 0.0), 1, keepdims=True)


def hyper_forward_kernel(dense, rest, rows_ref, lengths_ref, *refs):
    hyper_forward_body(dense, rest, rows_ref, lengths_column(lengths_ref[...]), *refs)


def hyper_forward_body(
    dense, rest, rows_ref, lengths, pooled_ref, normed_ref, query_ref, key_ref, value_ref, probs_ref, heads_ref, resid_ref, pre_ref
):
    count, width = rows_ref.shape
    entries = pooled_ref.shape[0]
    slots = count // entries
    vectors = vectors_of(rest)
    slot_rows = rows_ref[...]
    unit, _ = normalize(slot_rows)
    normed = (unit * vectors[0:1] + vectors[2:3]).astype(LOW)
    normed_ref[...] = normed
    query = dot(normed[:entries], weight(rest, 0), (1, 0)).astype(LOW)
    key = dot(normed, weight(rest, 16), (1, 0)).astype(LOW)
    value = dot(normed, weight(rest, 32), (1, 0)).astype(LOW)
    query_ref[...], key_ref[...], value_ref[...] = query, key, value
    heads = head_matrix(width)
    product = every_slot(query.astype(WIDE), slots) * key.astype(WIDE)
    scores = dot_wide(product, heads.astype(WIDE), (1, 1)) * (width // HYP_HEADS) ** (-0.5)
    lengths = every_slot(jnp.broadcast_to(lengths, (entries, 128)), slots).reshape(slots, entries, 128)
    slot = lax.broadcasted_iota(jnp.int32, (slots, entries, 128), 0).astype(WIDE)
    scores = jnp.where(slot < lengths, scores.reshape(slots, entries, 128), MASKED)
    grown = jnp.exp(scores - jnp.max(scores, 0, keepdims=True))
    probs = (grown / jnp.sum(grown, 0, keepdims=True)).reshape(count, 128)
    probs_ref[...] = probs
    weighted = dot(probs.astype(LOW), heads, (1, 0)) * value.astype(WIDE)
    heads_out = jnp.sum(weighted.reshape(slots, entries, width), 0).astype(LOW)
    heads_ref[...] = heads_out
    residual = slot_rows[:entries] + dot(heads_out, weight(rest, 48), (1, 0))
    resid_ref[...] = residual
    unit, _ = normalize(residual)
    normed_two = (unit * vectors[1:2] + vectors[3:4]).astype(LOW)
    out = residual + vectors[4:5]
    out_weight = weight(dense, OUT_ROW, 64)
    for turn in range(4):
        pre = dot(normed_two, weight(dense, IN_ROW + 16 * turn), (1, 0)) + vectors[5 + turn : 6 + turn]
        pre_ref[turn] = pre
        act = (0.5 * pre * (1.0 + gelu_tanh(pre))).astype(LOW)
        out += dot(act, out_weight[turn * width : (turn + 1) * width], (1, 0))
    pooled_ref[...] = out.astype(LOW)


def forward_shapes(entries, count, width):
    shapes = [
        ((entries, width), LOW),
        ((count, width), LOW),
        ((entries, width), LOW),
        ((count, width), LOW),
        ((count, width), LOW),
        ((count, 128), WIDE),
        ((entries, width), LOW),
        ((entries, width), WIDE),
        ((4, entries, width), WIDE),
    ]
    return [jax.ShapeDtypeStruct(shape, kind) for shape, kind in shapes]


def hyper_forward(dense, rest, slot_rows, lengths, entries):
    return pl.pallas_call(
        hyper_forward_kernel,
        out_shape=forward_shapes(entries, *slot_rows.shape),
        compiler_params=pltpu.CompilerParams(vmem_limit_bytes=VMEM_LIMIT),
        name="hyper_forward",
    )(dense, rest, slot_rows, lengths)


def project_rows(pooled, proj, vectors, gain, rows_ref, normed_ref):
    width = pooled.shape[1]
    square = 0.0
    for turn in range(4):
        columns = slice(turn * width, (turn + 1) * width)
        rows = dot(pooled, weight(proj, PROJ_ROW + 16 * turn), (1, 0)) + vectors[9 + turn : 10 + turn]
        rows = rows.astype(LOW)
        rows_ref[:, columns] = rows
        rows = rows.astype(WIDE)
        square += jnp.sum(rows * rows, -1, keepdims=True)
    scale = lax.rsqrt(square / (4 * width) + EPSILON)
    normed_ref[...] = (rows_ref[...].astype(WIDE) * scale * gain.astype(WIDE)).astype(LOW)


def project_kernel(pooled_ref, dense_ref, rest_ref, gain_ref, rows_ref, normed_ref):
    project_rows(pooled_ref[...], dense_ref, vectors_of(rest_ref), gain_ref[0:1], rows_ref, normed_ref)


def project(pooled, dense, rest, gain):
    entries, width = pooled.shape
    block = min(entries, 512)
    out_block = pl.BlockSpec((block, 4 * width), lambda i: (i, 0))
    result = jax.ShapeDtypeStruct((entries, 4 * width), LOW)
    in_vmem = pl.BlockSpec(memory_space=pltpu.VMEM)
    return pl.pallas_call(
        project_kernel,
        grid=(entries // block,),
        in_specs=[pl.BlockSpec((block, width), lambda i: (i, 0)), in_vmem, in_vmem, in_vmem],
        out_specs=[out_block, out_block],
        out_shape=[result, result],
        compiler_params=pltpu.CompilerParams(vmem_limit_bytes=VMEM_LIMIT),
        name="project",
    )(pooled, dense, rest, gain)


def pick_tokens(entries, core, own_ids, got_ids):
    left = jnp.where(core == 0, own_ids, got_ids)
    right = jnp.where(core == 0, got_ids, own_ids)
    entry = lax.broadcasted_iota(jnp.int32, (entries, own_ids.shape[1]), 0)
    return jnp.concatenate([(entry == left).astype(LOW), (entry == right).astype(LOW)], 1)


def first_kernel(
    gains_ref, biases_ref, attn_ref, in_ref, in_bias_ref, out_ref, proj_ref, proj_bias_ref, ids_ref, table_ref, lengths_ref, gain_ref,
    own_ids_ref, got_ids_ref, dy_ref, down_ref, query_ref, kv_ref,
    dense_out, rest_out, column_out, d_act_out, rows_out, inputs_out, qkv_out,
    dense, rest, dense_share, rest_share, parts, slot_rows, pooled_ref, normed_ref, q_ref, k_ref, v_ref, probs_ref, heads_ref, resid_ref, pre_ref,
    column_all, pooled_all, dy_all, down_buffer, act_buffer, query_weight, kv_weight, rows, normed, inputs,
    qkv, load_sems, down_sems, act_sems, out_sems, dy_send, dy_recv, *refs
):
    place = Place()
    own = lax.axis_index("dp") * 2 + place.core
    width = dense.shape[2]

    def load(source, target, number):
        copy = pltpu.make_async_copy(source, target, load_sems.at[number])
        copy.start()
        return copy

    units = down_ref.shape[0]

    def load_down(step):
        here = pl.ds(step * UNIT_BLOCK, UNIT_BLOCK)
        copy = pltpu.make_async_copy(down_ref.at[here], down_buffer.at[step % 2], down_sems.at[step % 2])
        copy.start()
        return copy

    own_dy = load(dy_ref, dy_all.at[0], 0)
    down_copy = load_down(0)
    weight_loads = [load(query_ref, query_weight, 1), load(kv_ref, kv_weight, 2)]

    rest_share[0:64] = attn_ref[...].reshape(64, width)
    for turn in range(4):
        columns = slice(turn * width, (turn + 1) * width)
        dense_share[IN_ROW + 16 * turn : IN_ROW + 16 * turn + 16] = in_ref[:, columns]
        dense_share[PROJ_ROW + 16 * turn : PROJ_ROW + 16 * turn + 16] = proj_ref[:, columns]
    dense_share[OUT_ROW : OUT_ROW + 64] = out_ref[...]

    def spread(values, length):
        count = values.shape[1]
        row = lax.broadcasted_iota(jnp.int32, (count, length), 0)
        lane = lax.broadcasted_iota(jnp.int32, (count, length), 1)
        return dot(values, (lane - own * count == row).astype(LOW), (1, 0))

    def by_rows(flat):
        return [flat[:, turn * width : (turn + 1) * width] for turn in range(4)]

    vectors = [spread(gains_ref[...], width), spread(biases_ref[...], width)]
    vectors += by_rows(spread(in_bias_ref[...], 4 * width)) + by_rows(spread(proj_bias_ref[...], 4 * width))
    vectors.append(jnp.zeros((3, width), WIDE))
    rest_share[VECTOR_ROW : VECTOR_ROW + 16] = jnp.concatenate(vectors, 0).astype(LOW)

    place.greet()
    send(dy_ref, dy_all.at[1], dy_send, dy_recv, place.targets["core"])
    dense_sems, rest_sems, small_sems, line_sems, slot_scratch = refs[:5], refs[5:12], refs[12:18], refs[18:20], refs[20:]
    pieces = table_ref.shape[0]
    groups, height = parts.shape[0], parts.shape[1] // ids_ref.shape[0]
    chunk = ids_ref.shape[1]

    def slot_steps():
        across = lax.broadcasted_iota(jnp.int32, (chunk, chunk), 1)
        down = lax.broadcasted_iota(jnp.int32, (chunk, chunk), 0)
        piece = lax.broadcasted_iota(jnp.int32, (chunk, pieces), 1).astype(WIDE) + (own * pieces).astype(WIDE)
        for turn in range(ids_ref.shape[0]):
            ids = ids_ref[turn : turn + 1].astype(WIDE)
            column = jnp.sum(jnp.where(across == down, ids, 0.0), 1, keepdims=True)
            found = dot((piece == column).astype(LOW), table_ref[...], (1, 0)).astype(LOW)
            parts[:, turn * height : (turn + 1) * height, :] = found.reshape(groups, height, width)
            yield
        yield from scatter_steps(place, parts, slot_rows, slot_scratch)

    def act_steps():
        nonlocal down_copy
        own_dy.wait()
        sent(dy_all.at[1], dy_recv)
        copies = []
        for step in range(units // UNIT_BLOCK):
            down_copy.wait()
            if (step + 1) * UNIT_BLOCK < units:
                down_copy = load_down(step + 1)
            if step >= 2:
                copies[step - 2].wait()
            tokens = dy_all[...].reshape(-1, dy_all.shape[2])
            act_buffer[step % 2] = dot(tokens, down_buffer[step % 2], (1, 1)).astype(LOW)
            here = pl.ds(step * UNIT_BLOCK, UNIT_BLOCK)
            copy = pltpu.make_async_copy(act_buffer.at[step % 2], d_act_out.at[:, here], act_sems.at[step % 2])
            copy.start()
            copies.append(copy)
            if len(copies) * UNIT_BLOCK == units:
                copies[-2].wait()
                copies[-1].wait()
                sent(dy_ref, dy_send)
            yield

    runs = [
        gather_steps(place, dense_share, dense, dense_sems),
        late_gather_steps(place, rest_share, rest, rest_sems),
        slot_steps(),
        act_steps(),
    ]
    run_in_order(runs, FIRST_ORDER)

    def store(source, target, number):
        copy = pltpu.make_async_copy(source, target, out_sems.at[number])
        copy.start()
        return copy

    stores = [store(dense, dense_out, 0), store(rest, rest_out, 1)]
    hyper_forward_body(
        dense, rest, slot_rows, lengths_column(lengths_ref[...]), pooled_ref, normed_ref, q_ref, k_ref, v_ref, probs_ref, heads_ref, resid_ref, pre_ref
    )
    small_gather(place, pooled_ref[...], pooled_all, small_sems)
    slot_count = parts.shape[1]
    column_all[place.z, :slot_count] = slot_rows[...].astype(LOW)
    lane = lax.broadcasted_iota(jnp.int32, (lengths_ref.shape[1], width), 1)
    row = lax.broadcasted_iota(jnp.int32, (lengths_ref.shape[1], width), 0)
    spread_lengths = dot(lengths_ref[...].astype(WIDE).astype(LOW), (lane == row).astype(LOW), (1, 0))
    column_all[place.z, slot_count:] = jnp.broadcast_to(spread_lengths, (16, width)).astype(LOW)
    column_run = line_share_steps(place, column_all, line_sems)
    next(column_run)
    pooled = pooled_all[...].reshape(-1, width)
    project_rows(pooled, dense, vectors_of(rest), gain_ref[0:1], rows, normed)
    stores.append(store(rows, rows_out, 2))

    entries = rows.shape[0]
    kv_width = HEAD_DIM * (KV_HEADS // 2)
    kv_columns = pl.ds(pl.multiple_of(place.core * kv_width, kv_width), kv_width)
    local = own_ids_ref.shape[1]
    pick = pick_tokens(entries, place.core, own_ids_ref[...], got_ids_ref[...])
    q_width = query_weight.shape[1]
    for copy in weight_loads:
        copy.wait()
    for start in range(0, q_width, 256):
        found = dot(normed[...], query_weight[:, start : start + 256], (1, 0)).T.astype(LOW)
        qkv[start : start + 256] = dot(found, pick, (1, 0)).astype(LOW)
    for which in range(2):
        start = q_width + which * kv_width
        found = dot(normed[...], kv_weight[which, :, kv_columns], (1, 0)).T.astype(LOW)
        qkv[start : start + kv_width] = dot(found, pick, (1, 0)).astype(LOW)
    stores.append(store(qkv, qkv_out, 3))
    own_pick = (lax.broadcasted_iota(jnp.int32, (entries, local), 0) == own_ids_ref[...]).astype(LOW)
    inputs[...] = dot(own_pick, rows[...], (0, 0)).astype(LOW)
    stores.append(store(inputs, inputs_out, 4))
    next(column_run)
    stores.append(store(column_all, column_out, 5))
    for copy in stores:
        copy.wait()


def first_exchange(weights, ids, table, lengths, gains, own_ids, got_ids, dy, down, query, kv, number):
    devices = 8 * PLANES
    width = table.shape[1]
    slots = ids.size // devices
    entries = lengths.shape[1]
    local, d_model = dy.shape
    seq_len = 2 * local
    features = query.shape[1] + kv.shape[2]
    units = down.shape[0]
    one = (slots, width)
    in_vmem, anywhere = pl.BlockSpec(memory_space=pltpu.VMEM), pl.BlockSpec(memory_space=pl.ANY)
    all_rows = devices * entries
    dense, rest = (devices, DENSE_ROWS, width), (devices, REST_ROWS, width)
    kept = forward_shapes(entries, slots, width)
    column = (PLANES, slots + 16, width)
    dma = pltpu.SemaphoreType.DMA
    return pl.pallas_call(
        first_kernel,
        in_specs=[in_vmem] * 14 + [anywhere] * 4,
        out_specs=[anywhere] * 7,
        out_shape=[
            jax.ShapeDtypeStruct(dense, LOW),
            jax.ShapeDtypeStruct(rest, LOW),
            jax.ShapeDtypeStruct(column, LOW),
            jax.ShapeDtypeStruct((2 * local, units), LOW),
            jax.ShapeDtypeStruct((all_rows, d_model), LOW),
            jax.ShapeDtypeStruct((local, d_model), LOW),
            jax.ShapeDtypeStruct((features, seq_len), LOW),
        ],
        scratch_shapes=[
            pltpu.VMEM(dense, LOW),
            pltpu.VMEM(rest, LOW),
            pltpu.VMEM(dense[1:], LOW),
            pltpu.VMEM(rest[1:], LOW),
            pltpu.VMEM((devices, *one), LOW),
            pltpu.VMEM(one, WIDE),
        ]
        + [pltpu.VMEM(array.shape, array.dtype) for array in kept]
        + [
            pltpu.VMEM(column, LOW),
            pltpu.VMEM((PLANES, 4, 2, entries, width), LOW),
            pltpu.VMEM((2, local, d_model), LOW),
            pltpu.VMEM((2, UNIT_BLOCK, d_model), LOW),
            pltpu.VMEM((2, 2 * local, UNIT_BLOCK), LOW),
            pltpu.VMEM(query.shape, LOW),
            pltpu.VMEM(kv.shape, LOW),
            pltpu.VMEM((all_rows, d_model), LOW),
            pltpu.VMEM((all_rows, d_model), LOW),
            pltpu.VMEM((local, d_model), LOW),
            pltpu.VMEM((features, seq_len), LOW),
            dma((3,)),
            dma((2,)),
            dma((2,)),
            dma((6,)),
            dma,
            dma,
        ]
        + gather_sems()
        + late_gather_sems()
        + small_gather_sems()
        + line_share_sems()
        + scatter_scratch(one),
        compiler_params=pltpu.CompilerParams(
            collective_id=number, has_side_effects=True, vmem_limit_bytes=VMEM_LIMIT
        ),
        name="first_exchange",
    )(*weights, ids, table, lengths, gains, own_ids, got_ids, dy, down, query, kv)


def greet_core(place):
    barrier = pltpu.get_barrier_semaphore()
    pl.semaphore_signal(barrier, inc=1, device_id=place.targets["core"], device_id_type=pl.DeviceIdType.MESH)
    pl.semaphore_wait(barrier, 1)


def started(source, target, sem):
    copy = pltpu.make_async_copy(source, target, sem)
    copy.start()
    return copy


def middle_kernel(
    own_hbm, other_hbm, weight_hbm, inputs_hbm, gains_ref, hidden_hbm, x_own_hbm, x_other_hbm, own, other, weight, inputs, partial, got, hidden,
    x_own, x_got, load_sems, tile_sems, send_sems, recv_sems, row_send_sems, row_recv_sems, out_sems
):
    place = Place()
    tokens, width = inputs.shape
    tiles = [slice(start, start + width // 4) for start in range(0, width, width // 4)]
    blocks = [slice(start, start + tokens // 4) for start in range(0, tokens, tokens // 4)]
    load_other = started(other_hbm, other, load_sems.at[0])
    weights = [started(weight_hbm.at[:, tile], weight.at[:, tile], tile_sems.at[n]) for n, tile in enumerate(tiles)]
    loads = [started(own_hbm, own, load_sems.at[1]), started(inputs_hbm, inputs, load_sems.at[2])]
    greet_core(place)
    target = place.targets["core"]
    load_other.wait()
    for number, tile in enumerate(tiles):
        weights[number].wait()
        partial[:, tile] = dot(other[...], weight[:, tile], (0, 0)).astype(LOW)
        send(partial.at[:, tile], got.at[:, tile], send_sems.at[number], recv_sems.at[number], target)
    for copy in loads:
        copy.wait()
    gain = gains_ref[1:2].astype(WIDE)
    stores = []
    for number, rows in enumerate(blocks):
        here = dot(own[:, rows], weight[...], (0, 0)) + inputs[rows].astype(WIDE)
        if number == 0:
            for turn, tile in enumerate(tiles):
                sent(got.at[:, tile], recv_sems.at[turn])
        here += got[rows].astype(WIDE)
        hidden[rows] = here
        stores.append(started(hidden.at[rows], hidden_hbm.at[rows], out_sems.at[0, number]))
        x_own[rows] = (here * lax.rsqrt(jnp.mean(here * here, -1, keepdims=True) + EPSILON) * gain).astype(LOW)
        send(x_own.at[rows], x_got.at[rows], row_send_sems.at[number], row_recv_sems.at[number], target)
        stores.append(started(x_own.at[rows], x_own_hbm.at[rows], out_sems.at[1, number]))
    for number, rows in enumerate(blocks):
        sent(x_got.at[rows], row_recv_sems.at[number])
        stores.append(started(x_got.at[rows], x_other_hbm.at[rows], out_sems.at[2, number]))
    for copy in stores:
        copy.wait()
    for number in range(4):
        sent(partial.at[:, tiles[number]], send_sems.at[number])
        sent(x_own.at[blocks[number]], row_send_sems.at[number])


def middle(heads_own, heads_other, weight, inputs, gains, number):
    in_vmem, anywhere = pl.BlockSpec(memory_space=pltpu.VMEM), pl.BlockSpec(memory_space=pl.ANY)
    tokens = pltpu.VMEM(inputs.shape, LOW)
    low = jax.ShapeDtypeStruct(inputs.shape, LOW)
    return pl.pallas_call(
        middle_kernel,
        in_specs=[anywhere] * 4 + [in_vmem],
        out_specs=[anywhere] * 3,
        out_shape=[jax.ShapeDtypeStruct(inputs.shape, WIDE), low, low],
        scratch_shapes=[
            pltpu.VMEM(heads_own.shape, LOW),
            pltpu.VMEM(heads_own.shape, LOW),
            pltpu.VMEM(weight.shape, LOW),
            tokens,
            tokens,
            tokens,
            pltpu.VMEM(inputs.shape, WIDE),
            tokens,
            tokens,
            dma_grid(3),
            dma_grid(4),
            dma_grid(4),
            dma_grid(4),
            dma_grid(4),
            dma_grid(4),
            dma_grid(3, 4),
        ],
        compiler_params=pltpu.CompilerParams(
            collective_id=number, has_side_effects=True, vmem_limit_bytes=VMEM_LIMIT
        ),
        name="middle",
    )(heads_own, heads_other, weight, inputs, gains)


def turn_kernel(
    hidden_hbm, dy_hbm, back_own_hbm, back_got_hbm, weight_hbm, gains_ref, grad_hbm, heads_own_hbm, heads_other_hbm, hidden, loaded, grad, got,
    weight, heads, load_sems, weight_sem, send_sems, recv_sems, out_sems
):
    place = Place()
    tokens, width = grad.shape
    count = hidden.shape[0]
    blocks = [slice(n * hidden.shape[1], (n + 1) * hidden.shape[1]) for n in range(count)]
    sources = (dy_hbm, back_own_hbm, back_got_hbm)
    loads = []
    for number, rows in enumerate(blocks):
        loads.append(
            [started(hidden_hbm.at[rows], hidden.at[number], load_sems.at[number, 3])]
            + [started(source.at[rows], loaded.at[number, n], load_sems.at[number, n]) for n, source in enumerate(sources)]
        )
        if number == 1:
            load_weight = started(weight_hbm, weight, weight_sem)
    greet_core(place)
    target = place.targets["core"]
    gain = gains_ref[1:2].astype(WIDE)
    half = tokens // 2
    for number, rows in enumerate(blocks):
        for copy in loads[number]:
            copy.wait()
        here = hidden[number]
        dy, back_own, back_got = (loaded[number, n].astype(WIDE) for n in range(3))
        scale = lax.rsqrt(jnp.mean(here * here, -1, keepdims=True) + EPSILON)
        inner = (back_own + back_got) * gain
        back = scale * inner - here * (scale * scale * scale * jnp.mean(here * inner, -1, keepdims=True))
        grad[rows] = (dy + back).astype(LOW)
        send(grad.at[rows], got.at[rows], send_sems.at[number], recv_sems.at[number], target)
    load_weight.wait()
    stores = [started(grad, grad_hbm, out_sems.at[0])]
    heads[0, :, :half] = dot(weight[...], grad[:half], (1, 1)).astype(LOW)
    heads[0, :, half:] = dot(weight[...], grad[half:], (1, 1)).astype(LOW)
    stores.append(started(heads.at[0], heads_own_hbm, out_sems.at[1]))
    for part in range(2):
        for number in range(part * count // 2, (part + 1) * count // 2):
            sent(got.at[blocks[number]], recv_sems.at[number])
        rows = slice(part * half, (part + 1) * half)
        heads[1, :, rows] = dot(weight[...], got[rows], (1, 1)).astype(LOW)
    stores.append(started(heads.at[1], heads_other_hbm, out_sems.at[2]))
    for copy in stores:
        copy.wait()
    for number, rows in enumerate(blocks):
        sent(grad.at[rows], send_sems.at[number])


def turn_around(hidden, dy, backs, weight, gains, number):
    in_vmem, anywhere = pl.BlockSpec(memory_space=pltpu.VMEM), pl.BlockSpec(memory_space=pl.ANY)
    tokens, width = dy.shape
    count = 4
    block = tokens // count
    heads = (weight.shape[0], tokens)
    return pl.pallas_call(
        turn_kernel,
        in_specs=[anywhere] * 5 + [in_vmem],
        out_specs=[anywhere] * 3,
        out_shape=[
            jax.ShapeDtypeStruct(dy.shape, LOW),
            jax.ShapeDtypeStruct(heads, LOW),
            jax.ShapeDtypeStruct(heads, LOW),
        ],
        scratch_shapes=[
            pltpu.VMEM((count, block, width), WIDE),
            pltpu.VMEM((count, 3, block, width), LOW),
            pltpu.VMEM(dy.shape, LOW),
            pltpu.VMEM(dy.shape, LOW),
            pltpu.VMEM(weight.shape, LOW),
            pltpu.VMEM((2, *heads), LOW),
            dma_grid(count, 4),
            pltpu.SemaphoreType.DMA,
            dma_grid(count),
            dma_grid(count),
            dma_grid(3),
        ],
        compiler_params=pltpu.CompilerParams(
            collective_id=number, has_side_effects=True, vmem_limit_bytes=VMEM_LIMIT
        ),
        name="turn_around",
    )(hidden, dy, *backs, weight, gains)


def outer(left, right):
    return dot(left, right, (0, 0))


def column_sum(values):
    return jnp.sum(values.astype(WIDE), 0, keepdims=True)


def own_part(ref, own, rows=slice(None)):
    if own is None:
        return ref[rows]
    size = ref.shape[1] // PLANES
    return ref[rows, pl.ds(pl.multiple_of(own * size, size), size)]


def back_dense(dense, vectors, rows_low, pooled_ref, residual, pre_ref, normed_ref, act_ref, put, own=None):
    width = pooled_ref.shape[1]
    d_pooled, proj_bias = 0.0, []
    for turn in range(4):
        rows = rows_low[:, turn * width : (turn + 1) * width]
        put(True, PROJ_ROW + 16 * turn, outer(own_part(pooled_ref, own), rows))
        d_pooled += dot(rows, weight(dense, PROJ_ROW + 16 * turn), (1, 1))
        proj_bias.append(column_sum(rows))
    ffn_low = d_pooled.astype(LOW)
    unit, scale = normalize(residual)
    normed_ref[...] = (unit * vectors[1:2] + vectors[3:4]).astype(LOW)
    out_weight = weight(dense, OUT_ROW, 64)
    d_normed, ffn_bias = 0.0, []
    for turn in range(4):
        pre = pre_ref[turn]
        bent = gelu_tanh(pre)
        act_ref[turn] = (0.5 * pre * (1.0 + bent)).astype(LOW)
        slope = 0.5 * (1.0 + bent) + 0.5 * pre * (1.0 - bent * bent) * GELU_A * (1.0 + 3.0 * GELU_B * pre * pre)
        d_act = dot(ffn_low, out_weight[turn * width : (turn + 1) * width], (1, 1))
        pre_low = (d_act * slope).astype(LOW)
        put(True, IN_ROW + 16 * turn, outer(own_part(normed_ref, own), pre_low))
        ffn_bias.append(column_sum(pre_low))
        d_normed += dot(pre_low, weight(dense, IN_ROW + 16 * turn), (1, 1))
    if own is None:
        put(True, OUT_ROW, jnp.concatenate([outer(act_ref[turn], ffn_low).astype(LOW) for turn in range(4)], 0), 64)
    else:
        put(True, OUT_ROW, outer(act_ref[own], ffn_low), 64)
    back, gain, bias = normalize_back(d_normed, vectors[1:2], unit, scale)
    return d_pooled + back, gain, bias, [column_sum(ffn_low)] + ffn_bias + proj_bias


def first_slot_plus(by_slot, by_entry):
    entries = by_entry.shape[0]
    return jnp.concatenate([by_slot[:entries] + by_entry, by_slot[entries:]], 0)


def back_attention(rest, vectors, d_resid, slot_rows, saved, put, own=None):
    normed_ref, query_ref, key_ref, value_ref, probs_ref, heads_ref = saved
    count, width = slot_rows.shape
    entries = query_ref.shape[0]
    slots = count // entries
    scale = (width // HYP_HEADS) ** (-0.5)
    attn_low = d_resid.astype(LOW)
    put(False, 48, outer(own_part(heads_ref, own), attn_low))
    d_heads = dot(attn_low, weight(rest, 48), (1, 1)).astype(LOW)
    heads = head_matrix(width)
    d_heads_all = every_slot(d_heads.astype(WIDE), slots)
    query_all = every_slot(query_ref[...].astype(WIDE), slots)
    probs = probs_ref[...]
    d_probs = dot_wide(d_heads_all * value_ref[...].astype(WIDE), heads.astype(WIDE), (1, 1))
    delta = every_slot(jnp.sum((probs * d_probs).reshape(slots, entries, 128), 0), slots)
    d_scores = dot((probs * (d_probs - delta) * scale).astype(LOW), heads, (1, 0))
    d_value = (dot(probs.astype(LOW), heads, (1, 0)) * d_heads_all).astype(LOW)
    d_key = (d_scores * query_all).astype(LOW)
    d_query = (d_scores * key_ref[...].astype(WIDE)).reshape(slots, entries, width)
    d_query = jnp.sum(d_query, 0).astype(LOW)
    put(False, 0, outer(own_part(normed_ref, own, slice(0, entries)), d_query))
    put(False, 16, outer(own_part(normed_ref, own), d_key))
    put(False, 32, outer(own_part(normed_ref, own), d_value))
    d_normed = dot(d_key, weight(rest, 16), (1, 1)) + dot(d_value, weight(rest, 32), (1, 1))
    d_normed = first_slot_plus(d_normed, dot(d_query, weight(rest, 0), (1, 1)))
    unit, inverse = normalize(slot_rows)
    back, gain, bias = normalize_back(d_normed, vectors[0:1], unit, inverse)
    return first_slot_plus(back, d_resid).astype(LOW), gain, bias


def vector_rows(gain_one, gain_two, bias_one, bias_two, rest):
    rows = [gain_one, gain_two, bias_one, bias_two] + rest
    rows.append(jnp.zeros((16 - len(rows), gain_one.shape[1]), WIDE))
    return jnp.concatenate(rows, 0).astype(LOW)


def hyper_backward_kernel(
    dense, rest, row_grad_ref, rows_ref, pooled_ref, normed_ref, query_ref, key_ref, value_ref, probs_ref, heads_ref, resid_ref, pre_ref,
    dense_grad, rest_grad, slot_ref, normed_two_ref, act_ref
):
    vectors = vectors_of(rest)
    put = putter(dense_grad, rest_grad)
    d_resid, gain_two, bias_two, sums = back_dense(
        dense, vectors, row_grad_ref[...].astype(LOW), pooled_ref, resid_ref[...], pre_ref, normed_two_ref, act_ref, put
    )
    saved = (normed_ref, query_ref, key_ref, value_ref, probs_ref, heads_ref)
    slot_ref[...], gain_one, bias_one = back_attention(rest, vectors, d_resid, rows_ref[...], saved, put)
    put_vectors(rest_grad, vector_rows(gain_one, gain_two, bias_one, bias_two, sums))


def putter(dense_grad, rest_grad):
    def put(in_dense, row, grad, height=16):
        target = dense_grad if in_dense else rest_grad
        target[:, row : row + height, :] = grad.astype(LOW).reshape(target.shape[0], height, target.shape[2])

    return put


def put_vectors(rest_grad, sums):
    rest_grad[:, VECTOR_ROW : VECTOR_ROW + 16, :] = jnp.broadcast_to(sums[None], (rest_grad.shape[0], *sums.shape))


def hyper_backward(dense, rest, row_grad, slot_rows, saved):
    return pl.pallas_call(
        hyper_backward_kernel,
        out_shape=[jax.ShapeDtypeStruct(like.shape, LOW) for like in (dense, rest, slot_rows)],
        scratch_shapes=[pltpu.VMEM(saved[0].shape, LOW), pltpu.VMEM((4, *saved[0].shape), LOW)],
        compiler_params=pltpu.CompilerParams(vmem_limit_bytes=VMEM_LIMIT),
        name="hyper_backward",
    )(dense, rest, row_grad, slot_rows, *saved)


def row_part_steps(place, hbm_refs, refs, ids_refs, gains_ref, weights, row_parts, sems):
    dq_ref, dk_ref, dv_ref, grad_ref, rows_ref, sums_ref = refs
    dq_hbm, dk_hbm, dv_hbm, query_hbm, kv_hbm, grad_hbm, rows_hbm = hbm_refs
    own_ids, got_ids = ids_refs[0][...], ids_refs[1][...]
    entries, d_model = rows_ref.shape
    q_width, kv_width = dq_ref.shape[0], dk_ref.shape[0]
    width = weights.shape[2]
    height = d_model // weights.shape[0]
    kv_columns = pl.ds(pl.multiple_of(place.core * kv_width, kv_width), kv_width)
    copies = [
        started(source, target, sems.at[number])
        for number, (source, target) in enumerate(
            (
                (dq_hbm, dq_ref),
                (dk_hbm, dk_ref),
                (dv_hbm, dv_ref),
                (query_hbm.at[:, :, :width], weights.at[:, 0:height, :]),
                (query_hbm.at[:, :, width:], weights.at[:, height : 2 * height, :]),
                (kv_hbm.at[0, :, :, kv_columns], weights.at[:, 2 * height : 3 * height, 0:kv_width]),
                (kv_hbm.at[1, :, :, kv_columns], weights.at[:, 2 * height : 3 * height, kv_width : 2 * kv_width]),
                (rows_hbm, rows_ref),
                (grad_hbm, grad_ref),
            )
        )
    ]
    yield
    pick = pick_tokens(entries, place.core, own_ids, got_ids)
    for copy in copies[:3]:
        copy.wait()
    sums_ref[:, :q_width] = dot(pick, dq_ref[...], (1, 1)).astype(LOW)
    sums_ref[:, q_width : q_width + kv_width] = dot(pick, dk_ref[...], (1, 1)).astype(LOW)
    sums_ref[:, q_width + kv_width :] = dot(pick, dv_ref[...], (1, 1)).astype(LOW)
    for copy in copies[3:]:
        copy.wait()
    gain = gains_ref[0:1].astype(WIDE)
    block = entries // 2
    group = row_parts.shape[0] // 2
    upper = lax.div(place.z, PLANES // 2)
    for number in (1 - upper, upper):
        here = pl.ds(pl.multiple_of(number * block, block), block)
        first = dot(sums_ref[here, :width], weight(weights, 0, height), (1, 1))
        first += dot(sums_ref[here, width : 2 * width], weight(weights, height, height), (1, 1))
        kv = weights[:, 2 * height : 3 * height, 0 : 2 * kv_width].reshape(d_model, 2 * kv_width)
        first += dot(sums_ref[here, q_width:], kv, (1, 1))
        rows = rows_ref[here].astype(WIDE)
        scale = lax.rsqrt(jnp.mean(rows * rows, -1, keepdims=True) + EPSILON)
        inner = first * gain
        inner = scale * inner - rows * (scale * scale * scale * jnp.mean(rows * inner, -1, keepdims=True))
        entry = lax.broadcasted_iota(jnp.int32, (block, own_ids.shape[1]), 0) + number * block
        own_pick = (entry == own_ids).astype(LOW)
        part = (inner + dot(own_pick, grad_ref[...], (1, 0))).astype(LOW)
        row_parts[pl.ds(number * group, group)] = part.reshape(group, *row_parts.shape[1:])
        yield


def last_kernel(
    dq_hbm, dk_hbm, dv_hbm, query_hbm, kv_hbm, grad_hbm, new_rows_hbm, own_ids_ref, got_ids_ref, gains_ref, ids_ref, dense_hbm, rest_hbm,
    *refs
):
    column_hbm, refs = refs[0], refs[1:]
    row_grad, dense_total, rest_total, table_grad, dense, rest, in_grad, out_grad, proj_grad, rest_grad, *refs = refs
    kept, refs = refs[:10], refs[10:]
    slot_all, rows_low, normed_two, acts, load_sems, dq_ref, dk_ref, dv_ref, grad_ref, new_rows_ref, sums_ref, row_parts, row_sems, column, *refs = refs
    row_scratch, refs = refs[:12], refs[12:]
    plane_scratch = [refs[9 * turn : 9 * turn + 9] for turn in range(4)]
    slot_sems, line_sems = refs[36:40], refs[40:42]
    place = Place()
    row_run = row_part_steps(
        place,
        (dq_hbm, dk_hbm, dv_hbm, query_hbm, kv_hbm, grad_hbm, new_rows_hbm),
        (dq_ref, dk_ref, dv_ref, grad_ref, new_rows_ref, sums_ref),
        (own_ids_ref, got_ids_ref),
        gains_ref,
        dense,
        row_parts,
        row_sems,
    )
    next(row_run)
    place.greet()
    next(row_run)
    loads = []

    def near_half():
        next(row_run)
        for number, pair in enumerate(((column_hbm, column), (rest_hbm, rest), (dense_hbm, dense))):
            loads.append(started(*pair, load_sems.at[number]))

    slot_rows, pooled, normed, query, key, value, probs, heads, resid, pre = kept
    width = dense.shape[2]
    slots = ids_ref.shape[0]
    height = slot_all.shape[1] // slots

    def forward_steps():
        for copy in loads:
            copy.wait()
        lengths = []
        for plane in range(PLANES):
            for slot in range(slots):
                here = (slot * PLANES + plane) * height
                slot_rows[here : here + height] = column[plane, slot * height : (slot + 1) * height].astype(WIDE)
            lengths.append(lengths_column(column[plane, slots * height :, :height]))
        hyper_forward_body(dense, rest, slot_rows, jnp.concatenate(lengths, 0), *kept[1:])
        yield

    def sum_steps():
        yield from scatter_steps(place, row_parts, row_grad, row_scratch, near_half)
        rows_low[place.z] = row_grad[...].astype(LOW)
        yield from line_share_steps(place, rows_low, line_sems)

    run_in_order([sum_steps(), forward_steps()], ROW_ORDER)
    vectors = vectors_of(rest)

    def put(in_dense, row, grad, height=16):
        target = (in_grad, out_grad, proj_grad)[row // 64] if in_dense else rest_grad
        row = row % 64 if in_dense else row
        target[:, row : row + height, :] = grad.astype(LOW).reshape(target.shape[0], height, width)

    d_resid, gain_two, bias_two, sums = back_dense(
        dense, vectors, rows_low[...].reshape(-1, rows_low.shape[2]), pooled, resid[...], pre, normed_two, acts, put, place.z
    )
    own = lax.axis_index("dp") * 2 + place.core

    def attention_steps():
        saved = (normed, query, key, value, probs, heads)
        slot_low, gain_one, bias_one = back_attention(rest, vectors, d_resid, slot_rows[...], saved, put, place.z)
        slot_low = slot_low.reshape(slots, PLANES, height, width)
        for plane in range(PLANES):
            slot_all[place.slot(0, plane, place.core)] = slot_low[:, plane].reshape(slots * height, width)
        put_vectors(rest_grad, vector_rows(gain_one, gain_two, bias_one, bias_two, sums))
        yield

    def table_steps():
        pieces, chunk = table_grad.shape[0], ids_ref.shape[1] // PLANES
        groups = slot_all.shape[0] // PLANES
        piece = lax.broadcasted_iota(jnp.int32, (pieces, slots * chunk), 0) + own * pieces
        for part in plane_gather_steps(place, slot_all, slot_sems):
            yield
            if part is None:
                continue
            lanes, here = slice(part * chunk, (part + 1) * chunk), slice(part * groups, (part + 1) * groups)
            ids = jnp.concatenate([ids_ref[turn : turn + 1, lanes] for turn in range(slots)], 1)
            rows = [slot_all[here, turn * height : (turn + 1) * height, :].reshape(chunk, width) for turn in range(slots)]
            found = dot((piece == ids).astype(LOW), jnp.concatenate(rows, 0), (1, 0))
            if part:
                table_grad[...] += found
            else:
                table_grad[...] = found
            yield

    places = (slice(IN_ROW, IN_ROW + 64), slice(OUT_ROW, OUT_ROW + 64), slice(PROJ_ROW, PROJ_ROW + 64))
    runs = [
        plane_scatter_steps(place, grad, dense_total, rows, scratch)
        for grad, rows, scratch in zip((in_grad, out_grad, proj_grad), places, plane_scratch)
    ]
    runs.append(plane_scatter_steps(place, rest_grad, rest_total, slice(None), plane_scratch[3]))
    runs += [table_steps(), attention_steps()]
    run_in_order(runs, LAST_ORDER)


def last_exchange(attention, ids, gains, slot_ids, dense, rest, column, pieces, number):
    in_vmem, anywhere = pl.BlockSpec(memory_space=pltpu.VMEM), pl.BlockSpec(memory_space=pl.ANY)
    devices = 8 * PLANES
    width = dense.shape[2]
    dq, dk, dv, query, kv, grad, rows = attention
    entries, d_model = rows.shape
    groups = dense.shape[0]
    query = query.reshape(groups, -1, query.shape[1])
    kv = kv.reshape(2, groups, -1, kv.shape[2])
    one = (entries // devices, d_model)
    slots = slot_ids.size // devices
    kept = [jax.ShapeDtypeStruct((PLANES * slots, width), WIDE)]
    kept += forward_shapes(PLANES * entries // devices, PLANES * slots, width)
    pooled = kept[1].shape
    return pl.pallas_call(
        last_kernel,
        in_specs=[anywhere] * 7 + [in_vmem] * 4 + [anywhere] * 3,
        out_specs=[in_vmem] * 4,
        out_shape=[
            jax.ShapeDtypeStruct(one, WIDE),
            jax.ShapeDtypeStruct(dense.shape[1:], WIDE),
            jax.ShapeDtypeStruct(rest.shape[1:], WIDE),
            jax.ShapeDtypeStruct((pieces, width), WIDE),
        ],
        scratch_shapes=[pltpu.VMEM(dense.shape, LOW), pltpu.VMEM(rest.shape, LOW)]
        + [pltpu.VMEM((8, 64, width), LOW)] * 3
        + [pltpu.VMEM((8, *rest.shape[1:]), LOW)]
        + [pltpu.VMEM(array.shape, array.dtype) for array in kept]
        + [
            pltpu.VMEM((devices, slots, width), LOW),
            pltpu.VMEM((PLANES, *one), LOW),
            pltpu.VMEM(pooled, LOW),
            pltpu.VMEM((4, *pooled), LOW),
            dma_grid(3),
        ]
        + [pltpu.VMEM(array.shape, LOW) for array in (dq, dk, dv, grad, rows)]
        + [
            pltpu.VMEM((entries, dq.shape[0] + 2 * dk.shape[0]), LOW),
            pltpu.VMEM((devices, *one), LOW),
            dma_grid(9),
            pltpu.VMEM(column.shape, LOW),
        ]
        + scatter_scratch(one)
        + plane_scatter_scratch((64, width)) * 3
        + plane_scatter_scratch(rest.shape[1:])
        + plane_gather_sems()
        + line_share_sems(),
        compiler_params=pltpu.CompilerParams(
            collective_id=number, has_side_effects=True, vmem_limit_bytes=VMEM_LIMIT
        ),
        name="last_exchange",
    )(dq, dk, dv, query, kv, grad, rows, *ids, gains, slot_ids, dense, rest, column)


def finish_kernel(
    own_ref, dense_ref, rest_ref, row_ref, table_ref, row_out, table_out, gains_out, biases_out, attn_out, in_out, in_bias_out, out_out,
    proj_out, proj_bias_out
):
    own = own_ref[0]
    width = rest_ref.shape[1]
    row_out[...] = row_ref[...]
    table_out[...] = table_ref[...]
    attn_out[...] = rest_ref[0:64].reshape(attn_out.shape)
    for turn in range(4):
        columns = slice(turn * width, (turn + 1) * width)
        in_out[:, columns] = dense_ref[IN_ROW + 16 * turn : IN_ROW + 16 * turn + 16]
        proj_out[:, columns] = dense_ref[PROJ_ROW + 16 * turn : PROJ_ROW + 16 * turn + 16]
    out_out[...] = dense_ref[OUT_ROW : OUT_ROW + 64]
    vectors = rest_ref[VECTOR_ROW : VECTOR_ROW + 16]

    def own_lanes(rows, size, base):
        lane = lax.broadcasted_iota(jnp.int32, (width, size), 0)
        column = lax.broadcasted_iota(jnp.int32, (width, size), 1)
        return dot_wide(rows, (lane + base - own * size == column).astype(WIDE), (1, 0))

    small = own_lanes(vectors, gains_out.shape[1], 0)
    gains_out[...] = small[0:2]
    biases_out[...] = small[2:5]
    size = in_bias_out.shape[1]
    picked = [own_lanes(vectors, size, turn * width) for turn in range(4)]
    in_bias_out[...] = sum(picked[turn][5 + turn : 6 + turn] for turn in range(4))
    proj_bias_out[...] = sum(picked[turn][9 + turn : 10 + turn] for turn in range(4))


def finish(own, dense, rest, row_grad, table_grad, shapes):
    return pl.pallas_call(
        finish_kernel,
        in_specs=[pl.BlockSpec(memory_space=pltpu.SMEM)] + [pl.BlockSpec(memory_space=pltpu.VMEM)] * 4,
        out_shape=[jax.ShapeDtypeStruct(shape, WIDE) for shape in (row_grad.shape, table_grad.shape, *shapes)],
        name="finish",
        compiler_params=pltpu.CompilerParams(vmem_limit_bytes=VMEM_LIMIT),
    )(own, dense, rest, row_grad, table_grad)


def to_slabs(attn, ffn_in, ffn_out, proj, vectors):
    width = attn.shape[-1]
    groups = width // 16

    def columns(matrix):
        return matrix.reshape(groups, 16, 4, width).transpose(0, 2, 1, 3).reshape(groups, 64, width)

    dense = [columns(ffn_in), ffn_out.reshape(groups, 64, width), columns(proj)]
    rest = [
        attn.reshape(4, groups, 16, width).transpose(1, 0, 2, 3).reshape(groups, 64, width),
        jnp.pad(vectors[None], ((0, groups - 1), (0, 0), (0, 0))),
    ]
    return jnp.concatenate(dense, 1), jnp.concatenate(rest, 1)


def from_slabs(dense, rest):
    groups, _, width = dense.shape

    def columns(row):
        part = dense[:, row : row + 64].reshape(groups, 4, 16, width)
        return part.transpose(0, 2, 1, 3).reshape(groups * 16, 4 * width)

    attn = rest[:, 0:64].reshape(groups, 4, 16, width).transpose(1, 0, 2, 3).reshape(4, groups * 16, width)
    return attn, columns(IN_ROW), dense[:, OUT_ROW : OUT_ROW + 64].reshape(groups * 64, width), columns(PROJ_ROW)


def shards(
    piece_ids,
    piece_lengths,
    group_ids,
    piece_table,
    ln_gains,
    hyp_biases,
    attn_weights,
    ffn_in_weight,
    ffn_in_bias,
    ffn_out_weight,
    proj_weight,
    proj_bias,
    lm_gains,
    query_weight,
    kv_weights,
    output_weight,
    gate_up_weight,
    down_weight,
    out_grad,
):
    n_mp = lax.axis_size("mp")
    devices = lax.axis_size(BOTH)
    me = lax.axis_index("mp")
    grid = n_mp == 2 and devices == 32
    entries, slot_count = piece_lengths.shape[0], piece_ids.shape[1]
    hyp_width = piece_table.shape[1]

    def swap(value):
        return lax.ppermute(value, "mp", [(0, 1), (1, 0)])

    def whole_of(value, axis):
        return lax.all_gather(value, BOTH, axis=axis, tiled=True)

    def share_of(value, axis):
        return lax.psum_scatter(value, BOTH, scatter_dimension=axis, tiled=True).astype(WIDE)

    def gather_tokens(value):
        return lax.all_gather(value, "mp", axis=0, tiled=True)

    me_all = lax.axis_index(BOTH)
    my_place = me.astype(jnp.int32).reshape(1)
    table_rows = piece_table.shape[0]
    lengths = piece_lengths[None]
    local_len = group_ids.shape[1]
    own_ids = group_ids.reshape(-1)
    got_ids = swap(own_ids) if grid else None
    seq_len = n_mp * local_len
    q_heads = query_weight.shape[1] // HEAD_DIM
    kv_here = max(KV_HEADS // n_mp, 1)
    cosine, sine = rope_tables(seq_len)
    lm_wide = lm_gains.astype(WIDE)
    dy_low = out_grad.reshape(local_len, -1)

    def norm_first(values):
        return rms_norm(values, lm_wide[0])

    def norm_second(values):
        return rms_norm(values, lm_wide[1])

    if grid:
        weights = (
            ln_gains,
            hyp_biases,
            attn_weights,
            ffn_in_weight,
            ffn_in_bias[None],
            ffn_out_weight,
            proj_weight,
            proj_bias[None],
        )
        slot_ids = piece_ids.T
        dense, rest, column, d_act, new_rows, inputs, qkv = first_exchange(
            weights,
            slot_ids,
            piece_table,
            lengths,
            lm_gains,
            own_ids[None],
            got_ids[None],
            dy_low,
            down_weight,
            query_weight,
            kv_weights,
            0,
        )
    else:
        own_pieces = me_all * table_rows + jnp.arange(table_rows, dtype=jnp.int32)
        slot_ids = piece_ids.reshape(devices, entries, slot_count).transpose(0, 2, 1).reshape(-1)
        slot_pick = (slot_ids[:, None] == own_pieces[None, :]).astype(LOW)
        slot_parts = dot(slot_pick, piece_table, (1, 0)).astype(LOW)
        slot_rows = lax.psum_scatter(slot_parts, BOTH, scatter_dimension=0, tiled=True).astype(WIDE)
        vectors = jnp.concatenate(
            [
                whole_of(ln_gains, 1),
                whole_of(hyp_biases, 1),
                whole_of(ffn_in_bias, 0).reshape(4, hyp_width),
                whole_of(proj_bias, 0).reshape(4, hyp_width),
                jnp.zeros((3, hyp_width), LOW),
            ]
        )
        dense, rest = to_slabs(
            whole_of(attn_weights, 1),
            whole_of(ffn_in_weight, 0),
            whole_of(ffn_out_weight, 0),
            whole_of(proj_weight, 0),
            vectors,
        )
        saved = hyper_forward(dense, rest, slot_rows, lengths, entries)
        new_rows, normed_rows = project(whole_of(saved[0], 0), dense, rest, lm_gains)
        kv_start = me * q_heads // (HEADS // KV_HEADS) * HEAD_DIM
        kv_local = lax.dynamic_slice_in_dim(kv_weights, kv_start, kv_here * HEAD_DIM, 2)
        qkv_weight = jnp.concatenate([query_weight, kv_local[0], kv_local[1]], 1)
        row_ids = lax.all_gather(own_ids, "mp", axis=0, tiled=True)
        row_index = jnp.arange(new_rows.shape[0], dtype=jnp.int32)
        row_pick = (row_index[:, None] == row_ids[None, :]).astype(LOW)
        own_pick = (own_ids[:, None] == row_index[None, :]).astype(LOW)
        qkv = dot(qkv_weight, dot(row_pick, normed_rows, (0, 0)).astype(LOW), (0, 1)).astype(LOW)
        inputs = dot(own_pick, new_rows, (1, 0))
        d_act = dot(gather_tokens(dy_low), down_weight, (1, 1)).astype(LOW)
    *heads, log_total = attend(my_place, qkv, cosine, sine, q_heads, kv_here, 2 if grid else 1)

    if grid:
        hidden, x_own, x_other = middle(*heads, output_weight, inputs, lm_gains, 2)
        out_other, back_other = feed_forward(x_other, d_act, 1, gate_up_weight, down_weight)
        out_got, back_got = swap(out_other), swap(back_other)
        out_own, back_own = feed_forward(x_own, d_act, 0, gate_up_weight, down_weight)
        grad_hidden_low, *grad_heads = turn_around(hidden, dy_low, (back_own, back_got), output_weight, lm_gains, 3)
    else:
        attn_part = dot(heads[0], output_weight, (0, 0)).astype(LOW)
        attn_sum = lax.psum_scatter(attn_part, "mp", scatter_dimension=0, tiled=True).astype(WIDE)
        hidden = inputs + attn_sum
        second_low = norm_second(hidden).astype(LOW)
        out_part, back_part = feed_forward(gather_tokens(second_low), d_act, 0, gate_up_weight, down_weight)
        outs = (lax.psum_scatter(out_part, "mp", scatter_dimension=0, tiled=True),)
        backs = (lax.psum_scatter(back_part, "mp", scatter_dimension=0, tiled=True),)
        lm_out, grad_hidden_low = second_back(hidden, dy_low, lm_gains, outs, backs)
        grad_heads = [dot(output_weight, gather_tokens(grad_hidden_low), (1, 1)).astype(LOW)]
    terms = (hidden, out_own, out_got) if grid else ()
    dq, dk, dv, *sums = attend_back(my_place, qkv, heads, log_total, grad_heads, cosine, sine, q_heads, kv_here, terms)
    if grid:
        lm_out = sums[0]

    if grid:
        attention = (dq, dk, dv, query_weight, kv_weights, grad_hidden_low, new_rows)
        ids = (own_ids[None], got_ids[None])
        row_grad, dense, rest, table_grad = last_exchange(
            attention, ids, lm_gains, slot_ids, dense, rest, column, table_rows, 1
        )
        bias_shape = (1, ffn_in_bias.shape[0])
        shapes = [
            ln_gains.shape,
            hyp_biases.shape,
            attn_weights.shape,
            ffn_in_weight.shape,
            bias_shape,
            ffn_out_weight.shape,
            proj_weight.shape,
            bias_shape,
        ]
        grads = finish(me_all.astype(jnp.int32).reshape(1), dense, rest, row_grad, table_grad, shapes)
        row_grad, table_grad, gains_grad, biases_grad, attn_grad, in_grad, in_bias, out_weight_grad, proj_grad, proj_bias_grad = grads
        in_bias, proj_bias_grad = in_bias[0], proj_bias_grad[0]
    else:
        grad_qkv = dot(jnp.concatenate([dq, dk, dv], 0), row_pick, (1, 1)).astype(LOW)
        first_part = dot(grad_qkv, qkv_weight, (0, 1))
        direct_part = dot(own_pick, grad_hidden_low, (0, 0))
        _, first_back = jax.vjp(norm_first, new_rows.astype(WIDE))
        row_parts = (direct_part + first_back(first_part)[0]).astype(LOW)
        row_grad = lax.psum_scatter(row_parts, BOTH, scatter_dimension=0, tiled=True).astype(WIDE)
        dense_grad, rest_grad, slot_low = hyper_backward(dense, rest, row_grad, slot_rows, saved)
        attn_grad, *dense_grads = from_slabs(dense_grad, rest_grad)
        attn_grad = share_of(attn_grad, 1)
        in_grad, out_weight_grad, proj_grad = [share_of(grad, 0) for grad in dense_grads]
        table_grad = dot(slot_pick, whole_of(slot_low, 0), (0, 0))
        sums = lax.psum(rest_grad[0, VECTOR_ROW:], BOTH).astype(WIDE)

        def own_lanes(values, size):
            return lax.dynamic_slice_in_dim(values, me_all * size, size, 1)

        gains_grad = own_lanes(sums[0:2], ln_gains.shape[1])
        biases_grad = own_lanes(sums[2:5], ln_gains.shape[1])
        in_bias, proj_bias_grad = own_lanes(sums[5:13].reshape(2, -1), ffn_in_bias.shape[0])
    return (
        lm_out.reshape(out_grad.shape),
        row_grad,
        table_grad,
        gains_grad,
        biases_grad,
        attn_grad,
        in_grad,
        in_bias,
        out_weight_grad,
        proj_grad,
        proj_bias_grad,
    )


def solution(mesh):
    return jax.shard_map(
        shards,
        mesh=mesh,
        in_specs=(
            P(),
            P(BOTH),
            P("dp", "mp"),
            P(BOTH, None),
            P(None, BOTH),
            P(None, BOTH),
            P(None, BOTH, None),
            P(BOTH, None),
            P(BOTH),
            P(BOTH, None),
            P(BOTH, None),
            P(BOTH),
            P(),
            P(None, "mp"),
            P(),
            P("mp", None),
            P(None, None, "mp"),
            P("mp", None),
            P("dp", "mp", None),
        ),
        out_specs=(
            P("dp", "mp", None),
            P(BOTH, None),
            P(BOTH, None),
            P(None, BOTH),
            P(None, BOTH),
            P(None, BOTH, None),
            P(BOTH, None),
            P(BOTH),
            P(BOTH, None),
            P(BOTH, None),
            P(BOTH),
        ),
        check_vma=False,
    )
```
